128 devices in a mesh: frame: 16 (over z, y_hi, core), res: 8 (over x, y_lo).
Axes of the slice: x: 4, y: 4 (y_hi: 2, y_lo: 2; y = y_hi * 2 + y_lo), z: 4, core: 2. Of those that a mesh axis runs over, the one named last changes fastest.
Arguments:
- tokens: bfloat16 [128, 128, 384], P('frame', 'res'), may hold values from -6 to 6
- rigid_frames: bfloat16 [12, 128, 128], P(None, 'frame', 'res'), may hold values from -4 to 4, as said below
- neighbors: int32 [128, 32], P('res'), may hold values from 0 to 127, as said below
- w_time_qkv: bfloat16 [384, 1152], replicated, may hold values from -3.6742346 to 3.6742346
- w_time_out: bfloat16 [384, 384], replicated, may hold values from -0.3125 to 0.3125
- w_ipa_qkv: bfloat16 [384, 1152], replicated, may hold values from -3.6742346 to 3.6742346
- w_ipa_points: bfloat16 [384, 288], replicated, may hold values from -0.3125 to 0.3125
- point_weight: float32 [12], replicated, may hold values from -2 to 1.5
- w_ipa_out: bfloat16 [384, 384], replicated, may hold values from -0.3125 to 0.3125
- w_up: bfloat16 [384, 1536], replicated, may hold values from -0.3125 to 0.3125
- w_down: bfloat16 [1536, 384], replicated, may hold values from -0.15625 to 0.15625
- cotangent: bfloat16 [128, 128, 384], P('frame', 'res'), may hold values from -6 to 6
Outputs:
- updated: bfloat16 [128, 128, 384], P('frame', 'res')
- grad_tokens: bfloat16 [128, 128, 384], P('frame', 'res')
- grad_time_qkv: float32 [384, 1152], replicated
- grad_time_out: float32 [384, 384], replicated
- grad_ipa_qkv: float32 [384, 1152], replicated
- grad_ipa_points: float32 [384, 288], replicated
- grad_point_weight: float32 [12], replicated
- grad_ipa_out: float32 [384, 384], replicated
- grad_up: float32 [384, 1536], replicated
- grad_down: float32 [1536, 384], replicated
The draws below stay inside these ranges and needn't reach their ends.
Inputs may be any that keep to these rules, and one draw needn't show every extreme that they name: `rigid_frames`: the first nine rows of each column form a rotation matrix row by row, the last three a translation. `neighbors`: each residue's list contains the residue itself.
All inputs are finite; a program needn't handle non-finite values.
Results may differ from the reference program's by a relative error of at most 0.025.
Values may be sent and summed in bfloat16 or wider, within the bound.
No kernel may reach another device: no remote copies, remote signals or barrier semaphores. Data moves between devices by JAX's collectives and lax.ppermute only.
A program may use at most 192 MiB of HBM per device.

```python
import math
import jax
import jax.numpy as jnp
from jax import lax

C = 384
H = 12
HID = 1536
P_SIZE = 4
NB = 32
FRAMES = 128
RES = 128


def attention_weight(key):
    base = jnp.clip(jax.random.normal(key, (C, 3 * C), jnp.float32), -3.0, 3.0) * C ** (-0.5)
    head_index = jnp.arange(C) // (C // H)
    query_part = base[:, :C]
    blended = base[:, C:2 * C]
    key_part = jnp.where(head_index[None, :] < 4, blended, base[:, C:2 * C])
    return jnp.concatenate([query_part, key_part, base[:, 2 * C:]], axis=1).astype(jnp.bfloat16)


def draw_w_time_qkv(key, part):
    key = jax.random.fold_in(key, 21)
    return attention_weight(key)


def draw_w_ipa_qkv(key, part):
    key = jax.random.fold_in(key, 33)
    return attention_weight(key)


def draw_rigid_frames(key, part):
    key = jax.random.fold_in(key, 7)
    turn_key, move_key = jax.random.split(key)
    quaternion = jax.random.normal(turn_key, (4, FRAMES, RES), jnp.float32)
    shift = jnp.clip(jax.random.normal(move_key, (3, FRAMES, RES), jnp.float32) * 1.5, -4.0, 4.0)
    quaternion = quaternion / jnp.sqrt(jnp.sum(quaternion * quaternion, axis=0, keepdims=True) + 1e-06)
    real_part, first_axis, second_axis, third_axis = (quaternion[0], quaternion[1], quaternion[2], quaternion[3])
    rows = [1.0 - 2.0 * (second_axis * second_axis + third_axis * third_axis), 2.0 * (first_axis * second_axis - real_part * third_axis), 2.0 * (first_axis * third_axis + real_part * second_axis), 2.0 * (first_axis * second_axis + real_part * third_axis), 1.0 - 2.0 * (first_axis * first_axis + third_axis * third_axis), 2.0 * (second_axis * third_axis - real_part * first_axis), 2.0 * (first_axis * third_axis - real_part * second_axis), 2.0 * (second_axis * third_axis + real_part * first_axis), 1.0 - 2.0 * (first_axis * first_axis + second_axis * second_axis)]
    rotation = jnp.stack(rows, axis=0)
    return jnp.concatenate([rotation, shift], axis=0).astype(jnp.bfloat16)


def draw_neighbors(key, part):
    key = jax.random.fold_in(key, 5)
    half_count = NB // 2
    residue_ids = jnp.arange(RES, dtype=jnp.int32)[:, None]
    offsets = jnp.arange(half_count, dtype=jnp.int32) - half_count // 2
    nearby = (residue_ids + offsets[None, :]) % RES
    distant = jax.random.randint(key, (RES, NB - half_count), 0, RES, dtype=jnp.int32)
    return jnp.concatenate([nearby, distant], axis=1).astype(jnp.int32)


def shard_levels(own_key, dims, shards, least, high):
    def one(dim, parts):
        heights = jax.random.uniform(jax.random.fold_in(jax.random.fold_in(own_key, 6), dim), (parts,), jnp.float32, least / len(shards), high / len(shards))
        return jnp.repeat(jnp.exp(heights), dims[dim] // parts).reshape((-1,) + (1,) * (len(dims) - dim - 1))

    factor_of = one(*shards[0])
    for cut in shards[1:]:
        factor_of = factor_of * one(*cut)
    return factor_of


def centred(rng, extent, scale, most, cuts=(), kind=jnp.bfloat16):
    result = jax.random.normal(rng, extent, jnp.float32) * scale
    if len(cuts) > 0:
        result = shard_levels(rng, extent, cuts, -0.22, 0.18) * result
    return jnp.clip(result, min=-most, max=most).astype(kind)


def setup_inputs(seed: int = 0) -> dict:
    splits = jax.random.split(jax.random.key(seed), 13)
    return {
        "tokens": centred(splits[0], (FRAMES, RES, C), 1.0, 6.0, ((0, 16), (1, 8))),
        "rigid_frames": draw_rigid_frames(jax.random.fold_in(splits[12], 71), 0),
        "neighbors": draw_neighbors(jax.random.fold_in(splits[12], 71), 0),
        "w_time_qkv": draw_w_time_qkv(jax.random.fold_in(splits[12], 71), 0),
        "w_time_out": centred(splits[4], (C, C), C ** -0.5, 0.3125),
        "w_ipa_qkv": draw_w_ipa_qkv(jax.random.fold_in(splits[12], 71), 0),
        "w_ipa_points": centred(splits[6], (C, 6 * H * P_SIZE), C ** -0.5, 0.3125),
        "point_weight": jnp.clip(jax.random.uniform(splits[7], (H,), jnp.float32, -2.0, 1.5), -2.0, 1.5),
        "w_ipa_out": centred(splits[8], (C, C), C ** -0.5, 0.3125),
        "w_up": centred(splits[9], (C, HID), C ** -0.5, 0.3125),
        "w_down": centred(splits[10], (HID, C), HID ** -0.5, 0.15625),
        "cotangent": centred(splits[11], (FRAMES, RES, C), 1.0, 6.0, ((0, 16), (1, 8))),
    }


EPSILON = 1e-05
PRECISE = lax.Precision.HIGHEST

def stored(values):
    return lax.optimization_barrier(values.astype(jnp.bfloat16))

def normalize(values):
    widened = values.astype(jnp.float32)
    centered = widened - lax.optimization_barrier(jnp.mean(widened, axis=-1, keepdims=True))
    variance = lax.optimization_barrier(jnp.mean(centered * centered, axis=-1, keepdims=True))
    return stored(centered * lax.rsqrt(variance + EPSILON))

def project(activations, weight):
    return jnp.dot(activations, weight, preferred_element_type=jnp.float32)

def split_three(activations, weight):
    product = project(activations, weight)
    portion = weight.shape[1] // 3
    return (stored(product[..., :portion]), stored(product[..., portion:2 * portion]), stored(product[..., 2 * portion:]))

def softmax_rounded(logits):
    highest = lax.optimization_barrier(jnp.max(logits, axis=-1, keepdims=True))
    raised = jnp.exp(logits - highest)
    shares = raised / lax.optimization_barrier(jnp.sum(raised, axis=-1, keepdims=True))
    return stored(shares).astype(jnp.float32)

def time_mix(query_rows, key_rows, value_rows):
    frames, residues, channels = query_rows.shape

    def shaped(tensor):
        return tensor.astype(jnp.float32).reshape(frames, residues, H, channels // H)
    scores = jnp.einsum('fshd,gshd->shfg', shaped(query_rows), shaped(key_rows), precision=PRECISE) * (1.0 / math.sqrt(channels // H))
    shares = softmax_rounded(scores)
    mixture = jnp.einsum('shfg,gshd->fshd', shares, shaped(value_rows), precision=PRECISE)
    return stored(mixture.reshape(frames, residues, channels))

def ipa_inputs(hidden, rigid_frames, weight_qkv, weight_points):
    normed = normalize(hidden)
    query_rows, key_rows, value_rows = split_three(normed, weight_qkv)
    frames, residues = (hidden.shape[0], hidden.shape[1])
    points = project(normed, weight_points).reshape(frames, residues, 2, 3, H * P_SIZE)
    frame_data = rigid_frames.astype(jnp.float32)
    rotation = frame_data[:9].reshape(3, 3, frames, residues)
    offset = jnp.transpose(frame_data[9:], (1, 2, 0))
    placed = jnp.einsum('abfr,frcbp->frcap', rotation, points, precision=PRECISE) + offset[:, :, None, :, None]
    query_points = placed[:, :, 0].reshape(frames, residues, 3 * H * P_SIZE)
    key_points = stored(placed[:, :, 1].reshape(frames, residues, 3 * H * P_SIZE))
    return (query_rows, key_rows, value_rows, query_points, key_points)

def ipa_mix(query_rows, query_points, key_table, value_table, point_table, neighbor_rows, point_weight):
    frames, members, channels = query_rows.shape
    near_keys = key_table[:, neighbor_rows].reshape(frames, members, NB, H, channels // H)
    near_values = value_table[:, neighbor_rows].reshape(frames, members, NB, H, channels // H)
    near_points = point_table[:, neighbor_rows].reshape(frames, members, NB, 3, H, P_SIZE)
    queries = query_rows.astype(jnp.float32).reshape(frames, members, H, channels // H)
    direct = jnp.einsum('frhd,frnhd->frhn', queries, near_keys, precision=PRECISE) * (1.0 / math.sqrt(channels // H))
    spread = query_points.reshape(frames, members, 1, 3, H, P_SIZE) - near_points
    distance = jnp.transpose(lax.optimization_barrier(jnp.sum(spread * spread, axis=(3, 5))), (0, 1, 3, 2))
    strength = jax.nn.softplus(point_weight) * math.sqrt(2.0 / (9.0 * P_SIZE))
    logits = math.sqrt(0.5) * (direct - 0.5 * strength[:, None] * distance)
    shares = softmax_rounded(logits)
    mixture = jnp.einsum('frhn,frnhd->frhd', shares, near_values, precision=PRECISE)
    return stored(mixture.reshape(frames, members, channels))

def closing(hidden, mixture, weight_out, weight_up, weight_down):
    second = stored(hidden.astype(jnp.float32) + project(mixture, weight_out))
    hidden_units = stored(jax.nn.gelu(project(normalize(second), weight_up), approximate=True))
    return stored(second.astype(jnp.float32) + project(hidden_units, weight_down))

def forward(tokens, rigid_frames, neighbors, params):
    time_qkv, time_out, ipa_qkv, ipa_points, point_weight, ipa_out, up_weight, down_weight = params
    frames, residues, channels = tokens.shape
    query_rows, key_rows, value_rows = split_three(normalize(tokens), time_qkv)

    def stacked(tensor):
        return jnp.transpose(tensor.reshape(frames, residues // 16, 16, channels), (1, 0, 2, 3))

    def time_block(tensors):
        return time_mix(tensors[0], tensors[1], tensors[2])
    mixture = lax.map(jax.checkpoint(time_block), (stacked(query_rows), stacked(key_rows), stacked(value_rows)))
    mixture = jnp.transpose(mixture, (1, 0, 2, 3)).reshape(frames, residues, channels)
    after_time = stored(tokens.astype(jnp.float32) + project(mixture, time_out))
    ipa_query, ipa_key, ipa_value, query_points, key_points = ipa_inputs(after_time, rigid_frames, ipa_qkv, ipa_points)

    def per_frame(tensors):
        return ipa_mix(tensors[0][None], tensors[1][None], tensors[2][None].astype(jnp.float32), tensors[3][None].astype(jnp.float32), tensors[4][None].astype(jnp.float32), neighbors, point_weight)[0]
    attended = lax.map(jax.checkpoint(per_frame), (ipa_query, query_points, ipa_key, ipa_value, key_points))
    return closing(after_time, attended, ipa_out, up_weight, down_weight)

def reference(tokens, rigid_frames, neighbors, w_time_qkv, w_time_out, w_ipa_qkv, w_ipa_points, point_weight, w_ipa_out, w_up, w_down, cotangent):
    params = (w_time_qkv.astype(jnp.float32), w_time_out.astype(jnp.float32), w_ipa_qkv.astype(jnp.float32), w_ipa_points.astype(jnp.float32), point_weight, w_ipa_out.astype(jnp.float32), w_up.astype(jnp.float32), w_down.astype(jnp.float32))

    def apply_layer(source, weights):
        return forward(source, rigid_frames, neighbors, weights)
    output, pullback = jax.vjp(apply_layer, tokens, params)
    token_grad, gradients = pullback(cotangent)
    return (output, token_grad, gradients[0], gradients[1], gradients[2], gradients[3], gradients[4], gradients[5], gradients[6], gradients[7])
```

```python
import math

import jax
import jax.numpy as jnp
import numpy as np
from jax import lax
from jax.experimental import pallas as pl
from jax.experimental.pallas import tpu as pltpu
from jax.sharding import PartitionSpec as P

H = 12
P_SIZE = 4
NB = 32
C = 384
HID = 1536
N = 128
POINTS = H * P_SIZE
EPSILON = 1e-05
SCALE = 1.0 / math.sqrt(C // H)
STRENGTH = math.sqrt(2.0 / (9.0 * P_SIZE)) * math.sqrt(0.5)
F32 = jnp.float32
BF16 = jnp.bfloat16
PARAMS = pltpu.CompilerParams(vmem_limit_bytes=48 * 1024 * 1024)


def mm(left, right):
    return lax.dot_general(left, right, (((1,), (0,)), ((), ())), preferred_element_type=F32)


def mt(left, right):
    return lax.dot_general(left, right, (((1,), (1,)), ((), ())), preferred_element_type=F32)


def tm(left, right):
    return lax.dot_general(left, right, (((0,), (0,)), ((), ())), preferred_element_type=F32)


def norm(values):
    centered = values - jnp.mean(values, axis=-1, keepdims=True)
    inverse = lax.rsqrt(jnp.mean(centered * centered, axis=-1, keepdims=True) + EPSILON)
    return centered * inverse, inverse


def norm_pull(cotangent, normed, inverse):
    return inverse * (
        cotangent
        - jnp.mean(cotangent, axis=-1, keepdims=True)
        - normed * jnp.mean(cotangent * normed, axis=-1, keepdims=True)
    )


def split_two(values):
    high = values.astype(BF16)
    return high, (values - high.astype(F32)).astype(BF16)


def split_three(values):
    high, rest = values.astype(BF16), None
    rest = values - high.astype(F32)
    middle = rest.astype(BF16)
    return high, middle, (rest - middle.astype(F32)).astype(BF16)


def tile_masks():
    lane = lax.broadcasted_iota(jnp.int32, (1, 128), 1)
    return [jnp.where(lane // 32 == m, 1.0, 0.0).astype(BF16) for m in range(4)]


def masked_stack(tile, masks):
    return jnp.concatenate([tile * mask for mask in masks], axis=0)


def time_forward(x_ref, wqkv_ref, wout_ref, x1_ref, qkv_ref, shares_ref, mix_ref):
    x = x_ref[...].astype(F32)
    normed, _ = norm(x)
    qkv_ref[...] = mm(normed.astype(BF16), wqkv_ref[...]).astype(BF16)
    masks = tile_masks()
    for g in range(3):
        q = qkv_ref[:, g * 128 : (g + 1) * 128]
        k = qkv_ref[:, C + g * 128 : C + (g + 1) * 128]
        v = qkv_ref[:, 2 * C + g * 128 : 2 * C + (g + 1) * 128]
        for m in range(4):
            h = 4 * g + m
            scores = mt(q * masks[m], k) * SCALE
            raised = jnp.exp(scores - jnp.max(scores, axis=-1, keepdims=True))
            shares = raised / jnp.sum(raised, axis=-1, keepdims=True)
            shares_ref[:, h * 128 : (h + 1) * 128] = shares.astype(BF16)
        mixed = mm(shares_ref[:, g * 512 : (g + 1) * 512], masked_stack(v, masks))
        mix_ref[:, g * 128 : (g + 1) * 128] = mixed.astype(BF16)
    x1_ref[...] = (x + mm(mix_ref[...], wout_ref[...])).astype(BF16)


def time_backward(
    dx1_ref, x_ref, qkv_ref, shares_ref, mix_ref, wqkv_ref, wout_ref,
    dx_ref, gqkv_ref, gout_ref, dqkv_ref, dcol_ref, pcol_ref,
):
    dx1 = dx1_ref[...]
    normed, inverse = norm(x_ref[...].astype(F32))
    dmix = mt(dx1, wout_ref[...]).astype(BF16)
    gout_ref[...] = tm(mix_ref[...], dx1).astype(gout_ref.dtype)
    masks = tile_masks()
    for g in range(3):
        q = qkv_ref[:, g * 128 : (g + 1) * 128]
        k = qkv_ref[:, C + g * 128 : C + (g + 1) * 128]
        v = qkv_ref[:, 2 * C + g * 128 : 2 * C + (g + 1) * 128]
        dm = dmix[:, g * 128 : (g + 1) * 128]
        rows = []
        for m in range(4):
            h = 4 * g + m
            kept = shares_ref[:, h * 128 : (h + 1) * 128]
            pcol_ref[m * 128 : (m + 1) * 128, :] = kept
            shares = kept.astype(F32)
            dshares = mt(dm * masks[m], v)
            inner = jnp.sum(shares * dshares, axis=-1, keepdims=True)
            dlogit = (shares * (dshares - inner) * SCALE).astype(BF16)
            dcol_ref[m * 128 : (m + 1) * 128, :] = dlogit
            rows.append(dlogit)
        dq = mm(jnp.concatenate(rows, axis=1), masked_stack(k, masks))
        dk = tm(dcol_ref[...], masked_stack(q, masks))
        dv = tm(pcol_ref[...], masked_stack(dm, masks))
        dqkv_ref[:, g * 128 : (g + 1) * 128] = dq.astype(BF16)
        dqkv_ref[:, C + g * 128 : C + (g + 1) * 128] = dk.astype(BF16)
        dqkv_ref[:, 2 * C + g * 128 : 2 * C + (g + 1) * 128] = dv.astype(BF16)
    gqkv_ref[...] = tm(normed.astype(BF16), dqkv_ref[...]).astype(gqkv_ref.dtype)
    dnormed = mt(dqkv_ref[...], wqkv_ref[...]).astype(BF16).astype(F32)
    pulled = norm_pull(dnormed, normed, inverse).astype(BF16).astype(F32)
    dx_ref[...] = (dx1.astype(F32) + pulled).astype(BF16)


def selectors():
    lane = np.arange(256)
    inside = lane < 3 * POINTS
    head = np.where(inside, (lane % POINTS) // P_SIZE, -1)
    heads = (head[None, :] == np.arange(16)[:, None]).astype(np.float32)
    turn = np.zeros((128, 4 * 256), np.float32)
    for a in range(3):
        at = a * POINTS + np.arange(POINTS)
        for b in range(3):
            turn[3 * a + b, b * 256 + at] = 1.0
        turn[9 + a, 3 * 256 + at] = 1.0
    spread = np.zeros((128, 256), np.float32)
    spread[16:32] = heads
    gather = np.zeros((6 * 256, 6 * POINTS), np.float32)
    for c in range(2):
        for b in range(3):
            for a in range(3):
                for p in range(POINTS):
                    gather[(3 * c + b) * 256 + a * POINTS + p, (3 * c + b) * POINTS + p] = 1.0
    return [jnp.asarray(item, BF16) for item in (heads, turn, spread, gather)]


def point_attention(
    weight_ref, x1_ref, side_ref, wqkv_ref, wpts_ref, wrep_ref, wout_ref, wup_ref, wdown_ref,
    heads_ref, turn_ref, spread_ref, gather_ref,
    updated_ref, dx1_ref, gqkv_ref, gpts_ref, gout_ref, gup_ref, gdown_ref, gweight_ref,
    qkv_ref, mix_ref, shares_ref, point_ref, prow_ref, pcol_ref, drow_ref, dcol_ref,
    dqkv_ref, dlocal_ref, keys_ref, queries_ref,
):
    masks = tile_masks()
    row = lax.broadcasted_iota(jnp.int32, (N, N), 0)
    col = lax.broadcasted_iota(jnp.int32, (N, N), 1)
    order = jnp.where((col // 8 == row % 16) & (col % 8 == row // 16), 1.0, 0.0).astype(BF16)
    x1 = mm(order, x1_ref[...])
    normed, inverse = norm(x1)
    n2 = normed.astype(BF16)
    qkv_ref[...] = mm(n2, wqkv_ref[...]).astype(BF16)

    lane = lax.broadcasted_iota(jnp.int32, (1, 256), 1)
    lane_head = jnp.where(lane < 3 * POINTS, (lane % POINTS) // P_SIZE, lane - 3 * POINTS)
    raw = jnp.zeros((1, 256), F32)
    for h in range(H):
        raw = jnp.where((lane < 3 * POINTS) & (lane_head == h), weight_ref[h], raw)
    soft = jnp.maximum(raw, 0.0) + jnp.log(1.0 + jnp.exp(-jnp.abs(raw)))
    strength = jnp.where(lane < 3 * POINTS, soft * STRENGTH, 0.0)
    head_masks = [jnp.where(lane_head == h, 1.0, 0.0).astype(BF16) for h in range(H)]

    turned = mm(side_ref[:, 512:640], turn_ref[...])
    turns = [turned[:, b * 256 : (b + 1) * 256] for b in range(3)]
    local = mm(n2, wrep_ref[...])
    placed = []
    for c in range(2):
        total = turned[:, 768:1024]
        for b in range(3):
            total = total + turns[b] * local[:, (3 * c + b) * 256 : (3 * c + b + 1) * 256]
        placed.append(total)
    gq = placed[0]
    gk_bf = placed[1].astype(BF16)
    gk = gk_bf.astype(F32)
    heads = heads_ref[...]
    own = sum(mt(part, heads) for part in split_three(gq * gq * (0.5 * strength)))
    other = sum(mt(heads, part) for part in split_three(gk * gk * (0.5 * strength)))
    q_high, q_low = split_two(gq * strength)
    ones = (lane >= 3 * POINTS) & (lane < 3 * POINTS + 16)
    keys_one = jnp.where(ones, 1.0, gk).astype(BF16)
    queries_one = jnp.where(ones, 1.0, gq).astype(BF16)
    two_keys = jnp.concatenate([gk_bf, gk_bf], axis=1)
    count = side_ref[:, 384:512].astype(F32)
    near = count > 0.0

    for g in range(3):
        q = qkv_ref[:, g * 128 : (g + 1) * 128]
        k = qkv_ref[:, C + g * 128 : C + (g + 1) * 128]
        v = qkv_ref[:, 2 * C + g * 128 : 2 * C + (g + 1) * 128]
        for m in range(4):
            h = 4 * g + m
            at = slice(h * 128, (h + 1) * 128)
            direct = mt(q * masks[m], k) * (SCALE * math.sqrt(0.5))
            cross = mt(
                jnp.concatenate([q_high * head_masks[h], q_low * head_masks[h]], axis=1), two_keys
            )
            spot = cross - own[:, h : h + 1] - other[h : h + 1, :]
            point_ref[:, at] = spot
            logits = jnp.where(near, direct + spot, -1e30)
            raised = jnp.exp(logits - jnp.max(logits, axis=-1, keepdims=True)) * count
            shares = raised / jnp.sum(raised, axis=-1, keepdims=True)
            shares_ref[:, at] = shares
            prow_ref[:, at] = shares.astype(BF16)
            pcol_ref[at, :] = shares.astype(BF16)
            keys_ref[at, :] = keys_one * head_masks[h]
            queries_ref[at, :] = queries_one * head_masks[h]
        mixed = mm(prow_ref[:, g * 512 : (g + 1) * 512], masked_stack(v, masks))
        mix_ref[:, g * 128 : (g + 1) * 128] = mixed.astype(BF16)

    cot = side_ref[:, 0:384]
    x2 = (x1 + mm(mix_ref[...], wout_ref[...])).astype(BF16).astype(F32)
    normed2, inverse2 = norm(x2)
    n3 = normed2.astype(BF16)
    u = mm(n3, wup_ref[...])
    root = math.sqrt(2.0 / math.pi)
    bent = jnp.tanh(root * (u + 0.044715 * u * u * u))
    hidden = (0.5 * u * (1.0 + bent)).astype(BF16)
    slope = 0.5 * (1.0 + bent) + 0.5 * u * (1.0 - bent * bent) * root * (
        1.0 + 3.0 * 0.044715 * u * u
    )
    updated_ref[...] = (x2 + mm(hidden, wdown_ref[...])).astype(BF16)
    gdown_ref[...] = tm(hidden, cot).astype(gdown_ref.dtype)
    dhidden = mt(cot, wdown_ref[...]).astype(BF16).astype(F32)
    du = (dhidden * slope).astype(BF16)
    gup_ref[...] = tm(n3, du).astype(gup_ref.dtype)
    dn3 = mt(du, wup_ref[...]).astype(BF16).astype(F32)
    dx2 = (cot.astype(F32) + norm_pull(dn3, normed2, inverse2).astype(BF16).astype(F32)).astype(
        BF16
    )
    dmix = mt(dx2, wout_ref[...]).astype(BF16)
    gout_ref[...] = tm(mix_ref[...], dx2).astype(gout_ref.dtype)

    gains = []
    for g in range(3):
        q = qkv_ref[:, g * 128 : (g + 1) * 128]
        k = qkv_ref[:, C + g * 128 : C + (g + 1) * 128]
        v = qkv_ref[:, 2 * C + g * 128 : 2 * C + (g + 1) * 128]
        dm = dmix[:, g * 128 : (g + 1) * 128]
        for m in range(4):
            h = 4 * g + m
            at = slice(h * 128, (h + 1) * 128)
            shares = shares_ref[:, at]
            dshares = mt(dm * masks[m], v)
            dlogit = shares * (dshares - jnp.sum(shares * dshares, axis=-1, keepdims=True))
            gains.append(jnp.sum(dlogit * point_ref[:, at], axis=0, keepdims=True))
            drow_ref[:, at] = dlogit.astype(BF16)
            dcol_ref[at, :] = dlogit.astype(BF16)
        group = slice(g * 512, (g + 1) * 512)
        dq = mm(drow_ref[:, group], masked_stack(k, masks)) * (SCALE * math.sqrt(0.5))
        dk = tm(dcol_ref[group, :], masked_stack(q, masks)) * (SCALE * math.sqrt(0.5))
        dv = tm(pcol_ref[group, :], masked_stack(dm, masks))
        dqkv_ref[:, g * 128 : (g + 1) * 128] = dq.astype(BF16)
        dqkv_ref[:, C + g * 128 : C + (g + 1) * 128] = dk.astype(BF16)
        dqkv_ref[:, 2 * C + g * 128 : 2 * C + (g + 1) * 128] = dv.astype(BF16)

    gain = jnp.sum(jnp.concatenate(gains + gains[:4], axis=0), axis=1, keepdims=True)
    row16 = lax.broadcasted_iota(jnp.int32, (16, 128), 0)
    raw16 = jnp.zeros((16, 128), F32)
    for h in range(H):
        raw16 = jnp.where(row16 == h, weight_ref[h], raw16)
    soft16 = jnp.maximum(raw16, 0.0) + jnp.log(1.0 + jnp.exp(-jnp.abs(raw16)))
    gweight_ref[...] = (gain / ((1.0 + jnp.exp(-raw16)) * soft16)).astype(gweight_ref.dtype)

    from_keys = mm(drow_ref[...], keys_ref[...])
    from_queries = tm(dcol_ref[...], queries_ref[...])
    spread = spread_ref[...]
    own_sum = sum(mm(part, spread) for part in split_two(from_keys[:, 128:256]))
    other_sum = sum(mm(part, spread) for part in split_two(from_queries[:, 128:256]))
    dgq = strength * (from_keys - gq * own_sum)
    dgk = (strength * (from_queries - gk * other_sum)).astype(BF16).astype(F32)
    for b in range(3):
        dlocal_ref[:, b * 256 : (b + 1) * 256] = (turns[b] * dgq).astype(BF16)
        dlocal_ref[:, (3 + b) * 256 : (4 + b) * 256] = (turns[b] * dgk).astype(BF16)
    dpoints = mm(dlocal_ref[...], gather_ref[...]).astype(BF16)
    dqkv = dqkv_ref[...]
    gqkv_ref[...] = tm(n2, dqkv).astype(gqkv_ref.dtype)
    gpts_ref[...] = tm(n2, dpoints).astype(gpts_ref.dtype)
    dn2 = (mt(dqkv, wqkv_ref[...]) + mt(dpoints, wpts_ref[...])).astype(BF16).astype(F32)
    dx1 = (dx2.astype(F32) + norm_pull(dn2, normed, inverse).astype(BF16).astype(F32)).astype(BF16)
    dx1_ref[...] = tm(order, dx1).astype(BF16)


def like(shape, dtype):
    return jax.ShapeDtypeStruct(shape, dtype)


GRAD = F32


def call_time_forward(x, w_qkv, w_out):
    return pl.pallas_call(
        time_forward,
        out_shape=(
            like((N, C), BF16), like((N, 3 * C), BF16), like((N, H * N), BF16), like((N, C), BF16),
        ),
        compiler_params=PARAMS,
        name="time_forward",
    )(x, w_qkv, w_out)


def call_time_backward(dx1, x, qkv, shares, mix, w_qkv, w_out):
    return pl.pallas_call(
        time_backward,
        out_shape=(like((N, C), BF16), like((C, 3 * C), GRAD), like((C, C), GRAD)),
        scratch_shapes=[
            pltpu.VMEM((N, 3 * C), BF16), pltpu.VMEM((4 * N, N), BF16), pltpu.VMEM((4 * N, N), BF16),
        ],
        compiler_params=PARAMS,
        name="time_backward",
    )(dx1, x, qkv, shares, mix, w_qkv, w_out)


def call_point_attention(weight, x1, side, w_qkv, w_pts, w_rep, w_out, w_up, w_down):
    whole = pl.BlockSpec(memory_space=pltpu.VMEM)
    return pl.pallas_call(
        point_attention,
        in_specs=[pl.BlockSpec(memory_space=pltpu.SMEM)] + [whole] * 12,
        out_shape=(
            like((N, C), BF16), like((N, C), BF16), like((C, 3 * C), GRAD),
            like((C, 6 * POINTS), GRAD), like((C, C), GRAD), like((C, HID), GRAD),
            like((HID, C), GRAD), like((16, 128), GRAD),
        ),
        scratch_shapes=[
            pltpu.VMEM((N, 3 * C), BF16), pltpu.VMEM((N, C), BF16),
            pltpu.VMEM((N, H * N), F32), pltpu.VMEM((N, H * N), F32),
            pltpu.VMEM((N, H * N), BF16), pltpu.VMEM((H * N, N), BF16),
            pltpu.VMEM((N, H * N), BF16), pltpu.VMEM((H * N, N), BF16),
            pltpu.VMEM((N, 3 * C), BF16), pltpu.VMEM((N, 6 * 256), BF16),
            pltpu.VMEM((H * N, 256), BF16), pltpu.VMEM((H * N, 256), BF16),
        ],
        compiler_params=PARAMS,
        name="point_attention",
    )(weight, x1, side, w_qkv, w_pts, w_rep, w_out, w_up, w_down, *selectors())


def repeat_points(weight):
    parts = weight.reshape(C, 6, POINTS)
    tripled = jnp.concatenate([parts, parts, parts], axis=2)
    return jnp.pad(tripled, ((0, 0), (0, 0), (0, 256 - 3 * POINTS))).reshape(C, 6 * 256)


def side_rows(cotangent, neighbors, rigid_frames):
    frames, residues, _ = cotangent.shape
    hits = neighbors[:, :, None] == lax.broadcasted_iota(jnp.int32, (1, 1, N), 2)
    count = jnp.sum(hits.astype(F32), axis=1).astype(BF16)
    return jnp.concatenate(
        [
            cotangent,
            jnp.broadcast_to(count[None], (frames, residues, N)),
            jnp.pad(jnp.transpose(rigid_frames, (1, 2, 0)), ((0, 0), (0, 0), (0, 116))),
        ],
        axis=2,
    )


def body(
    tokens, rigid_frames, neighbors, w_time_qkv, w_time_out, w_ipa_qkv, w_ipa_points,
    point_weight, w_ipa_out, w_up, w_down, cotangent,
):
    everyone = ("frame", "res")
    x = lax.all_to_all(tokens, "frame", split_axis=1, concat_axis=0, tiled=True).reshape(N, C)
    side = lax.all_to_all(
        side_rows(cotangent, neighbors, rigid_frames), "res", split_axis=0, concat_axis=0, tiled=True
    ).reshape(N, 640)
    x1, qkv, shares, mix = call_time_forward(x, w_time_qkv, w_time_out)
    x1 = lax.all_to_all(x1, everyone, split_axis=0, concat_axis=0, tiled=True)
    updated, dx1, g_ipa_qkv, g_pts, g_ipa_out, g_up, g_down, g_weight = call_point_attention(
        point_weight, x1, side, w_ipa_qkv, w_ipa_points, repeat_points(w_ipa_points), w_ipa_out,
        w_up, w_down,
    )
    dx1 = lax.all_to_all(dx1, everyone, split_axis=0, concat_axis=0, tiled=True)
    dx, g_time_qkv, g_time_out = call_time_backward(
        dx1, x, qkv, shares, mix, w_time_qkv, w_time_out
    )
    frames, residues = tokens.shape[:2]
    output = lax.all_to_all(
        updated.reshape(frames, residues, C), "res", split_axis=0, concat_axis=0, tiled=True
    )
    token_grad = lax.all_to_all(
        dx.reshape(N, 1, C), "frame", split_axis=0, concat_axis=1, tiled=True
    )
    early = lax.psum((g_ipa_qkv, g_pts, g_ipa_out, g_up, g_down, g_weight), everyone)
    late = lax.psum((g_time_qkv, g_time_out), everyone)
    return (
        output, token_grad, late[0], late[1], early[0], early[1], early[5][:H, 0], early[2],
        early[3], early[4],
    )


def solution(mesh):
    rows = P("frame", "res", None)
    placed = (rows, P(None, "frame", "res"), P("res", None)) + (P(),) * 8 + (rows,)
    return jax.shard_map(
        body,
        mesh=mesh,
        in_specs=placed,
        out_specs=(rows, rows) + (P(),) * 8,
        check_vma=False,
    )
```

```python
import math

import jax
import jax.numpy as jnp
import numpy as np
from jax import lax
from jax.experimental import pallas as pl
from jax.experimental.pallas import tpu as pltpu
from jax.sharding import Mesh, PartitionSpec as P

H = 12
P_SIZE = 4
NB = 32
C = 384
HID = 1536
N = 128
POINTS = H * P_SIZE
EPSILON = 1e-05
SCALE = 1.0 / math.sqrt(C // H)
STRENGTH = math.sqrt(2.0 / (9.0 * P_SIZE)) * math.sqrt(0.5)
F32 = jnp.float32
BF16 = jnp.bfloat16
EVERYONE = ("line", "core", "res")
SHARERS = 64
GAIN_LANE = 6 * POINTS - 256

PIECES = {
    "up": (C, HID),
    "ipa_out": (C, C),
    "ipa_points": (C, C),
    "ipa_qkv": (C, 3 * C),
    "down": (HID, C),
    "time_qkv": (C, 3 * C),
    "time_out": (C, C),
}
EARLY_UNITS = [20, 19]
LATE_UNITS = [6, 6]
EARLY = max(EARLY_UNITS) * C
LATE = max(LATE_UNITS) * C
HALF = -(-(EARLY + LATE) // (SHARERS * 16)) * SHARERS * 16


def place_units():
    units, taken = {}, {True: [0, 0], False: [0, 0]}
    for name, (rows, columns) in PIECES.items():
        late = name.startswith("time")
        room = LATE_UNITS if late else EARLY_UNITS
        units[name] = []
        for _ in range(rows * columns // (C * 128)):
            half = 0 if taken[late][0] < room[0] else 1
            units[name].append((half, (EARLY if late else 0) + taken[late][half] * C))
            taken[late][half] += 1
    return units


UNITS = place_units()


def halves(core, keep_ref, give_ref):
    def put(name, value):
        tiles = value.shape[1] // 128
        base = EARLY if name.startswith("time") else 0
        pieces = [[], []]
        for unit, (half, at) in enumerate(UNITS[name]):
            down, across = (unit // tiles) * C, (unit % tiles) * 128
            part = value[down : down + C, across : across + 128].astype(BF16)
            pieces[half].append((at - base, part))

        for half in range(2):
            for ref, mine in ((keep_ref, True), (give_ref, False)):
                @pl.when((core == half) == mine)
                def store(ref=ref, parts=pieces[half]):
                    for at, part in parts:
                        ref[at : at + C, :] = part

    return put


PARAMS = pltpu.CompilerParams(vmem_limit_bytes=48 * 1024 * 1024)


def mm(left, right):
    return lax.dot_general(left, right, (((1,), (0,)), ((), ())), preferred_element_type=F32)


def mt(left, right):
    return lax.dot_general(left, right, (((1,), (1,)), ((), ())), preferred_element_type=F32)


def tm(left, right):
    return lax.dot_general(left, right, (((0,), (0,)), ((), ())), preferred_element_type=F32)


def norm(values):
    centered = values - jnp.mean(values, axis=-1, keepdims=True)
    inverse = lax.rsqrt(jnp.mean(centered * centered, axis=-1, keepdims=True) + EPSILON)
    return centered * inverse, inverse


def norm_pull(cotangent, normed, inverse):
    return inverse * (
        cotangent
        - jnp.mean(cotangent, axis=-1, keepdims=True)
        - normed * jnp.mean(cotangent * normed, axis=-1, keepdims=True)
    )


def split_two(values):
    high = values.astype(BF16)
    return high, (values - high.astype(F32)).astype(BF16)


def split_three(values):
    high, rest = values.astype(BF16), None
    rest = values - high.astype(F32)
    middle = rest.astype(BF16)
    return high, middle, (rest - middle.astype(F32)).astype(BF16)


def tile_masks():
    lane = lax.broadcasted_iota(jnp.int32, (1, 128), 1)
    return [jnp.where(lane // 32 == m, 1.0, 0.0).astype(BF16) for m in range(4)]


def masked_stack(tile, masks):
    return jnp.concatenate([tile * mask for mask in masks], axis=0)


def time_forward(
    place_ref, neighbors_ref, rows_ref, wqkv_ref, wout_ref, sent_ref, qkv_ref, shares_ref, mix_ref
):
    x = rows_ref[:, 0:C].astype(F32)
    normed, _ = norm(x)
    qkv_ref[...] = mm(normed.astype(BF16), wqkv_ref[...]).astype(BF16)
    masks = tile_masks()
    for g in range(3):
        q = qkv_ref[:, g * 128 : (g + 1) * 128]
        k = qkv_ref[:, C + g * 128 : C + (g + 1) * 128]
        v = qkv_ref[:, 2 * C + g * 128 : 2 * C + (g + 1) * 128]
        for m in range(4):
            h = 4 * g + m
            scores = mt(q * masks[m], k) * SCALE
            raised = jnp.exp(scores - jnp.max(scores, axis=-1, keepdims=True))
            shares = raised / jnp.sum(raised, axis=-1, keepdims=True)
            shares_ref[:, h * 128 : (h + 1) * 128] = shares.astype(BF16)
        mixed = mm(shares_ref[:, g * 512 : (g + 1) * 512], masked_stack(v, masks))
        mix_ref[:, g * 128 : (g + 1) * 128] = mixed.astype(BF16)
    sent_ref[:, 0:C] = (x + mm(mix_ref[...], wout_ref[...])).astype(BF16)
    sent_ref[:, C : C + 512] = rows_ref[:, C : C + 512]
    lane = lax.broadcasted_iota(jnp.int32, (N, 128), 1)
    count = jnp.zeros((N, 128), F32)
    for n in range(NB):
        count = count + jnp.where(lane == neighbors_ref[place_ref[0], n], 1.0, 0.0)
    sent_ref[:, C + 512 : C + 640] = count.astype(BF16)


def time_backward(
    core_ref, back_ref, rows_ref, qkv_ref, shares_ref, mix_ref, wqkv_ref, wout_ref,
    sent_ref, keep_ref, give_ref, dqkv_ref, dcol_ref, pcol_ref,
):
    put = halves(core_ref[0], keep_ref, give_ref)
    dx1 = back_ref[:, 0:C]
    normed, inverse = norm(rows_ref[:, 0:C].astype(F32))
    dmix = mt(dx1, wout_ref[...]).astype(BF16)
    put("time_out", tm(mix_ref[...], dx1))
    masks = tile_masks()
    for g in range(3):
        q = qkv_ref[:, g * 128 : (g + 1) * 128]
        k = qkv_ref[:, C + g * 128 : C + (g + 1) * 128]
        v = qkv_ref[:, 2 * C + g * 128 : 2 * C + (g + 1) * 128]
        dm = dmix[:, g * 128 : (g + 1) * 128]
        rows = []
        for m in range(4):
            h = 4 * g + m
            kept = shares_ref[:, h * 128 : (h + 1) * 128]
            pcol_ref[m * 128 : (m + 1) * 128, :] = kept
            shares = kept.astype(F32)
            dshares = mt(dm * masks[m], v)
            inner = jnp.sum(shares * dshares, axis=-1, keepdims=True)
            dlogit = (shares * (dshares - inner) * SCALE).astype(BF16)
            dcol_ref[m * 128 : (m + 1) * 128, :] = dlogit
            rows.append(dlogit)
        dq = mm(jnp.concatenate(rows, axis=1), masked_stack(k, masks))
        dk = tm(dcol_ref[...], masked_stack(q, masks))
        dv = tm(pcol_ref[...], masked_stack(dm, masks))
        dqkv_ref[:, g * 128 : (g + 1) * 128] = dq.astype(BF16)
        dqkv_ref[:, C + g * 128 : C + (g + 1) * 128] = dk.astype(BF16)
        dqkv_ref[:, 2 * C + g * 128 : 2 * C + (g + 1) * 128] = dv.astype(BF16)
    put("time_qkv", tm(normed.astype(BF16), dqkv_ref[...]))
    dnormed = mt(dqkv_ref[...], wqkv_ref[...]).astype(BF16).astype(F32)
    pulled = norm_pull(dnormed, normed, inverse).astype(BF16).astype(F32)
    sent_ref[:, 0:C] = (dx1.astype(F32) + pulled).astype(BF16)
    sent_ref[:, C : 2 * C] = back_ref[:, C : 2 * C]


def selectors():
    lane = np.arange(256)
    inside = lane < 3 * POINTS
    head = np.where(inside, (lane % POINTS) // P_SIZE, -1)
    heads = (head[None, :] == np.arange(16)[:, None]).astype(np.float32)
    turn = np.zeros((128, 4 * 256), np.float32)
    for a in range(3):
        at = a * POINTS + np.arange(POINTS)
        for b in range(3):
            turn[3 * a + b, b * 256 + at] = 1.0
        turn[9 + a, 3 * 256 + at] = 1.0
    spread = np.zeros((128, 256), np.float32)
    spread[16:32] = heads
    gather = np.zeros((6 * 256, C), np.float32)
    for c in range(2):
        for b in range(3):
            for a in range(3):
                for p in range(POINTS):
                    gather[(3 * c + b) * 256 + a * POINTS + p, (3 * c + b) * POINTS + p] = 1.0
    return [jnp.asarray(item, BF16) for item in (heads, turn, spread, gather)]


def point_attention(
    core_ref, weight_ref, rows_ref, wqkv_ref, wpts_ref, wrep_ref, wout_ref, wup_ref, wdown_ref,
    heads_ref, turn_ref, spread_ref, gather_ref,
    back_ref, keep_ref, give_ref,
    qkv_ref, mix_ref, shares_ref, point_ref, prow_ref, pcol_ref, drow_ref, dcol_ref,
    dqkv_ref, dlocal_ref, keys_ref, queries_ref, side_ref,
):
    put = halves(core_ref[0], keep_ref, give_ref)
    for ref in (keep_ref, give_ref):
        ref[EARLY - C : EARLY, :] = jnp.zeros((C, 128), BF16)
    masks = tile_masks()
    row = lax.broadcasted_iota(jnp.int32, (N, N), 0)
    col = lax.broadcasted_iota(jnp.int32, (N, N), 1)
    order = jnp.where((col // 8 == row % 16) & (col % 8 == row // 16), 1.0, 0.0).astype(BF16)
    x1 = mm(order, rows_ref[:, 0:C])
    side_ref[...] = mm(order, rows_ref[:, C : C + 640]).astype(BF16)
    normed, inverse = norm(x1)
    n2 = normed.astype(BF16)
    qkv_ref[...] = mm(n2, wqkv_ref[...]).astype(BF16)

    lane = lax.broadcasted_iota(jnp.int32, (1, 256), 1)
    lane_head = jnp.where(lane < 3 * POINTS, (lane % POINTS) // P_SIZE, lane - 3 * POINTS)
    raw = jnp.zeros((1, 256), F32)
    for h in range(H):
        raw = jnp.where((lane < 3 * POINTS) & (lane_head == h), weight_ref[h], raw)
    soft = jnp.maximum(raw, 0.0) + jnp.log(1.0 + jnp.exp(-jnp.abs(raw)))
    strength = jnp.where(lane < 3 * POINTS, soft * STRENGTH, 0.0)
    head_masks = [jnp.where(lane_head == h, 1.0, 0.0).astype(BF16) for h in range(H)]

    turned = mm(side_ref[:, C : C + 128], turn_ref[...])
    turns = [turned[:, b * 256 : (b + 1) * 256] for b in range(3)]
    local = mm(n2, wrep_ref[...])
    placed = []
    for c in range(2):
        total = turned[:, 768:1024]
        for b in range(3):
            total = total + turns[b] * local[:, (3 * c + b) * 256 : (3 * c + b + 1) * 256]
        placed.append(total)
    gq = placed[0]
    gk_bf = placed[1].astype(BF16)
    gk = gk_bf.astype(F32)
    heads = heads_ref[...]
    own = sum(mt(part, heads) for part in split_three(gq * gq * (0.5 * strength)))
    other = sum(mt(heads, part) for part in split_three(gk * gk * (0.5 * strength)))
    q_high, q_low = split_two(gq * strength)
    ones = (lane >= 3 * POINTS) & (lane < 3 * POINTS + 16)
    keys_one = jnp.where(ones, 1.0, gk).astype(BF16)
    queries_one = jnp.where(ones, 1.0, gq).astype(BF16)
    two_keys = jnp.concatenate([gk_bf, gk_bf], axis=1)
    count = side_ref[:, C + 128 : C + 256].astype(F32)
    near = count > 0.0

    for g in range(3):
        q = qkv_ref[:, g * 128 : (g + 1) * 128]
        k = qkv_ref[:, C + g * 128 : C + (g + 1) * 128]
        v = qkv_ref[:, 2 * C + g * 128 : 2 * C + (g + 1) * 128]
        for m in range(4):
            h = 4 * g + m
            at = slice(h * 128, (h + 1) * 128)
            direct = mt(q * masks[m], k) * (SCALE * math.sqrt(0.5))
            cross = mt(
                jnp.concatenate([q_high * head_masks[h], q_low * head_masks[h]], axis=1), two_keys
            )
            spot = cross - own[:, h : h + 1] - other[h : h + 1, :]
            point_ref[:, at] = spot
            logits = jnp.where(near, direct + spot, -1e30)
            raised = jnp.exp(logits - jnp.max(logits, axis=-1, keepdims=True)) * count
            shares = raised / jnp.sum(raised, axis=-1, keepdims=True)
            shares_ref[:, at] = shares
            prow_ref[:, at] = shares.astype(BF16)
            pcol_ref[at, :] = shares.astype(BF16)
            keys_ref[at, :] = keys_one * head_masks[h]
            queries_ref[at, :] = queries_one * head_masks[h]
        mixed = mm(prow_ref[:, g * 512 : (g + 1) * 512], masked_stack(v, masks))
        mix_ref[:, g * 128 : (g + 1) * 128] = mixed.astype(BF16)

    cot = side_ref[:, 0:C]
    x2 = (x1 + mm(mix_ref[...], wout_ref[...])).astype(BF16).astype(F32)
    normed2, inverse2 = norm(x2)
    n3 = normed2.astype(BF16)
    u = mm(n3, wup_ref[...])
    root = math.sqrt(2.0 / math.pi)
    bent = jnp.tanh(root * (u + 0.044715 * u * u * u))
    hidden = (0.5 * u * (1.0 + bent)).astype(BF16)
    slope = 0.5 * (1.0 + bent) + 0.5 * u * (1.0 - bent * bent) * root * (
        1.0 + 3.0 * 0.044715 * u * u
    )
    updated = (x2 + mm(hidden, wdown_ref[...])).astype(BF16)
    back_ref[:, C : 2 * C] = tm(order, updated).astype(BF16)
    put("down", tm(hidden, cot))
    dhidden = mt(cot, wdown_ref[...]).astype(BF16).astype(F32)
    du = (dhidden * slope).astype(BF16)
    put("up", tm(n3, du))
    dn3 = mt(du, wup_ref[...]).astype(BF16).astype(F32)
    dx2 = (cot.astype(F32) + norm_pull(dn3, normed2, inverse2).astype(BF16).astype(F32)).astype(
        BF16
    )
    dmix = mt(dx2, wout_ref[...]).astype(BF16)
    put("ipa_out", tm(mix_ref[...], dx2))

    gains = []
    for g in range(3):
        q = qkv_ref[:, g * 128 : (g + 1) * 128]
        k = qkv_ref[:, C + g * 128 : C + (g + 1) * 128]
        v = qkv_ref[:, 2 * C + g * 128 : 2 * C + (g + 1) * 128]
        dm = dmix[:, g * 128 : (g + 1) * 128]
        for m in range(4):
            h = 4 * g + m
            at = slice(h * 128, (h + 1) * 128)
            shares = shares_ref[:, at]
            dshares = mt(dm * masks[m], v)
            dlogit = shares * (dshares - jnp.sum(shares * dshares, axis=-1, keepdims=True))
            gains.append(jnp.sum(dlogit * point_ref[:, at], axis=0, keepdims=True))
            drow_ref[:, at] = dlogit.astype(BF16)
            dcol_ref[at, :] = dlogit.astype(BF16)
        group = slice(g * 512, (g + 1) * 512)
        dq = mm(drow_ref[:, group], masked_stack(k, masks)) * (SCALE * math.sqrt(0.5))
        dk = tm(dcol_ref[group, :], masked_stack(q, masks)) * (SCALE * math.sqrt(0.5))
        dv = tm(pcol_ref[group, :], masked_stack(dm, masks))
        dqkv_ref[:, g * 128 : (g + 1) * 128] = dq.astype(BF16)
        dqkv_ref[:, C + g * 128 : C + (g + 1) * 128] = dk.astype(BF16)
        dqkv_ref[:, 2 * C + g * 128 : 2 * C + (g + 1) * 128] = dv.astype(BF16)

    lane128 = lax.broadcasted_iota(jnp.int32, (1, 128), 1)
    gain = jnp.zeros((1, 128), F32)
    raw_row = jnp.zeros((1, 128), F32)
    for h in range(H):
        here = lane128 == GAIN_LANE + h
        gain = jnp.where(here, jnp.sum(gains[h], axis=1, keepdims=True), gain)
        raw_row = jnp.where(here, weight_ref[h], raw_row)
    soft_row = jnp.maximum(raw_row, 0.0) + jnp.log(1.0 + jnp.exp(-jnp.abs(raw_row)))
    gain = gain / ((1.0 + jnp.exp(-raw_row)) * soft_row)

    from_keys = mm(drow_ref[...], keys_ref[...])
    from_queries = tm(dcol_ref[...], queries_ref[...])
    spread = spread_ref[...]
    own_sum = sum(mm(part, spread) for part in split_two(from_keys[:, 128:256]))
    other_sum = sum(mm(part, spread) for part in split_two(from_queries[:, 128:256]))
    dgq = strength * (from_keys - gq * own_sum)
    dgk = (strength * (from_queries - gk * other_sum)).astype(BF16).astype(F32)
    for b in range(3):
        dlocal_ref[:, b * 256 : (b + 1) * 256] = (turns[b] * dgq).astype(BF16)
        dlocal_ref[:, (3 + b) * 256 : (4 + b) * 256] = (turns[b] * dgk).astype(BF16)
    dpoints = mm(dlocal_ref[...], gather_ref[...]).astype(BF16)
    dqkv = dqkv_ref[...]
    put("ipa_qkv", tm(n2, dqkv))
    gpts = tm(n2, dpoints)
    first = lax.broadcasted_iota(jnp.int32, (C, 128), 0) == 0
    last = gpts[:, 256:384] + jnp.where(first, gain, 0.0)
    put("ipa_points", jnp.concatenate([gpts[:, 0:256], last], axis=1))
    dn2 = (mt(dqkv, wqkv_ref[...]) + mt(dpoints[:, 0 : 6 * POINTS], wpts_ref[...])).astype(BF16).astype(F32)
    dx1 = (dx2.astype(F32) + norm_pull(dn2, normed, inverse).astype(BF16).astype(F32)).astype(BF16)
    back_ref[:, 0:C] = tm(order, dx1).astype(BF16)


def like(shape, dtype):
    return jax.ShapeDtypeStruct(shape, dtype)


def call_time_forward(place, neighbors, rows, w_qkv, w_out):
    smem, vmem = pl.BlockSpec(memory_space=pltpu.SMEM), pl.BlockSpec(memory_space=pltpu.VMEM)
    return pl.pallas_call(
        time_forward,
        in_specs=[smem, smem, vmem, vmem, vmem],
        out_shape=(
            like((N, 1024), BF16), like((N, 3 * C), BF16), like((N, H * N), BF16),
            like((N, C), BF16),
        ),
        compiler_params=PARAMS,
        name="time_forward",
    )(place, neighbors, rows, w_qkv, w_out)


def call_time_backward(core, back, rows, qkv, shares, mix, w_qkv, w_out):
    smem, vmem = pl.BlockSpec(memory_space=pltpu.SMEM), pl.BlockSpec(memory_space=pltpu.VMEM)
    return pl.pallas_call(
        time_backward,
        in_specs=[smem] + [vmem] * 7,
        out_shape=(like((N, 2 * C), BF16), like((LATE, 128), BF16), like((LATE, 128), BF16)),
        scratch_shapes=[
            pltpu.VMEM((N, 3 * C), BF16), pltpu.VMEM((4 * N, N), BF16), pltpu.VMEM((4 * N, N), BF16),
        ],
        compiler_params=PARAMS,
        name="time_backward",
    )(core, back, rows, qkv, shares, mix, w_qkv, w_out)


def call_point_attention(core, weight, rows, w_qkv, w_pts, w_rep, w_out, w_up, w_down):
    smem, vmem = pl.BlockSpec(memory_space=pltpu.SMEM), pl.BlockSpec(memory_space=pltpu.VMEM)
    return pl.pallas_call(
        point_attention,
        in_specs=[smem, smem] + [vmem] * 11,
        out_shape=(like((N, 2 * C), BF16), like((EARLY, 128), BF16), like((EARLY, 128), BF16)),
        scratch_shapes=[
            pltpu.VMEM((N, 3 * C), BF16), pltpu.VMEM((N, C), BF16),
            pltpu.VMEM((N, H * N), F32), pltpu.VMEM((N, H * N), F32),
            pltpu.VMEM((N, H * N), BF16), pltpu.VMEM((H * N, N), BF16),
            pltpu.VMEM((N, H * N), BF16), pltpu.VMEM((H * N, N), BF16),
            pltpu.VMEM((N, 3 * C), BF16), pltpu.VMEM((N, 6 * 256), BF16),
            pltpu.VMEM((H * N, 256), BF16), pltpu.VMEM((H * N, 256), BF16),
            pltpu.VMEM((N, 640), BF16),
        ],
        compiler_params=PARAMS,
        name="point_attention",
    )(core, weight, rows, w_qkv, w_pts, w_rep, w_out, w_up, w_down, *selectors())


def add_halves(keep_early_ref, got_early_ref, keep_late_ref, got_late_ref, total_ref):
    early = keep_early_ref[...].astype(F32) + got_early_ref[...].astype(F32)
    total_ref[0:EARLY, :] = early.astype(BF16)
    late = keep_late_ref[...].astype(F32) + got_late_ref[...].astype(F32)
    total_ref[EARLY : EARLY + LATE, :] = late.astype(BF16)
    total_ref[EARLY + LATE :, :] = jnp.zeros((HALF - EARLY - LATE, 128), BF16)


def call_add_halves(*parts):
    return pl.pallas_call(
        add_halves, out_shape=like((HALF, 128), BF16), compiler_params=PARAMS, name="add_halves"
    )(*parts)


def add_parts(parts_ref, copies_ref):
    count = parts_ref.shape[0]
    total = parts_ref[0].astype(F32)
    for k in range(1, count):
        total = total + parts_ref[k].astype(F32)
    total = total.astype(BF16)
    for k in range(count):
        copies_ref[k] = total


def call_add_parts(parts):
    return pl.pallas_call(
        add_parts, out_shape=like(parts.shape, BF16), compiler_params=PARAMS, name="add_parts"
    )(parts)


def unpack(core_ref, mine_ref, other_ref, *out_refs):
    outs = dict(zip(PIECES, out_refs))
    gain_ref = out_refs[-1]

    def read(halves_refs):
        for name, (rows, columns) in PIECES.items():
            for unit, (half, at) in enumerate(UNITS[name]):
                value = halves_refs[half][at : at + C, :].astype(F32)
                tiles = columns // 128
                down, across = (unit // tiles) * C, (unit % tiles) * 128
                if name == "ipa_points" and across == 256:
                    outs[name][down : down + C, across:] = value[:, : 6 * POINTS - 256]
                    gain_ref[...] = value[0:1, :]
                else:
                    outs[name][down : down + C, across : across + 128] = value

    @pl.when(core_ref[0] == 0)
    def first():
        read((mine_ref, other_ref))

    @pl.when(core_ref[0] != 0)
    def second():
        read((other_ref, mine_ref))


def call_unpack(core, mine, other):
    smem, vmem = pl.BlockSpec(memory_space=pltpu.SMEM), pl.BlockSpec(memory_space=pltpu.VMEM)
    shapes = [
        like((rows, 6 * POINTS if name == "ipa_points" else columns), F32)
        for name, (rows, columns) in PIECES.items()
    ]
    return pl.pallas_call(
        unpack,
        in_specs=[smem, vmem, vmem],
        out_shape=(*shapes, like((1, 128), F32)),
        compiler_params=PARAMS,
        name="unpack",
    )(core, mine, other)


def repeat_points(weight):
    parts = weight.reshape(C, 6, POINTS)
    tripled = jnp.concatenate([parts, parts, parts], axis=2)
    return jnp.pad(tripled, ((0, 0), (0, 0), (0, 256 - 3 * POINTS))).reshape(C, 6 * 256)


def body(
    tokens, rigid_frames, neighbors, w_time_qkv, w_time_out, w_ipa_qkv, w_ipa_points,
    point_weight, w_ipa_out, w_up, w_down, cotangent,
):
    frames, residues = tokens.shape[:2]
    place = lax.axis_index(("line", "core")).astype(jnp.int32).reshape(1)
    core = lax.axis_index("core").astype(jnp.int32).reshape(1)
    rigid = jnp.pad(jnp.transpose(rigid_frames, (1, 2, 0)), ((0, 0), (0, 0), (0, 116)))
    rows = lax.all_to_all(
        jnp.concatenate([tokens, cotangent, rigid], axis=2),
        ("line", "core"), split_axis=1, concat_axis=0, tiled=True,
    ).reshape(N, 2 * C + 128)
    sent, qkv, shares, mix = call_time_forward(place, neighbors, rows, w_time_qkv, w_time_out)
    moved = lax.all_to_all(sent, EVERYONE, split_axis=0, concat_axis=0, tiled=True)
    back, keep_early, give_early = call_point_attention(
        core, point_weight, moved, w_ipa_qkv, w_ipa_points, repeat_points(w_ipa_points), w_ipa_out,
        w_up, w_down,
    )
    swap = [(0, 1), (1, 0)]
    got_early = lax.ppermute(give_early, "core", swap)
    back = lax.all_to_all(back, EVERYONE, split_axis=0, concat_axis=0, tiled=True)
    ended, keep_late, give_late = call_time_backward(
        core, back, rows, qkv, shares, mix, w_time_qkv, w_time_out
    )
    got_late = lax.ppermute(give_late, "core", swap)
    ended = lax.all_to_all(
        ended.reshape(N, 1, 2 * C), ("line", "core"), split_axis=0, concat_axis=1, tiled=True
    )
    packed = call_add_halves(keep_early, got_early, keep_late, got_late)
    parts = lax.all_to_all(
        packed.reshape(SHARERS, HALF // SHARERS, 128), ("line", "res"), split_axis=0, concat_axis=0,
        tiled=True,
    )
    mine = lax.all_to_all(
        call_add_parts(parts), ("line", "res"), split_axis=0, concat_axis=0, tiled=True
    ).reshape(HALF, 128)
    other = lax.ppermute(mine, "core", swap)
    *grads, gain = call_unpack(core, mine, other)
    grads = dict(zip(PIECES, grads))
    return (
        ended[:, :, C:], ended[:, :, :C], grads["time_qkv"], grads["time_out"], grads["ipa_qkv"],
        grads["ipa_points"], gain[0, GAIN_LANE : GAIN_LANE + H], grads["ipa_out"], grads["up"],
        grads["down"],
    )


def solution(mesh):
    devices = mesh.devices
    split = Mesh(
        devices.reshape(devices.shape[0] // 2, 2, devices.shape[1]), ("line", "core", "res")
    )
    frame = ("line", "core")
    rows = P(frame, "res", None)
    placed = (rows, P(None, frame, "res"), P("res", None)) + (P(),) * 8 + (rows,)
    return jax.shard_map(
        body,
        mesh=split,
        in_specs=placed,
        out_specs=(rows, rows) + (P(),) * 8,
        check_vma=False,
    )
```

```python
import math

import jax
import jax.numpy as jnp
import numpy as np
from jax import lax
from jax.experimental import pallas as pl
from jax.experimental.pallas import tpu as pltpu
from jax.sharding import Mesh, PartitionSpec as P

H = 12
P_SIZE = 4
NB = 32
C = 384
HID = 1536
N = 128
POINTS = H * P_SIZE
EPSILON = 1e-05
SCALE = 1.0 / math.sqrt(C // H)
STRENGTH = math.sqrt(2.0 / (9.0 * P_SIZE)) * math.sqrt(0.5)
F32 = jnp.float32
BF16 = jnp.bfloat16
EVERYONE = ("line", "core", "res")
SHARERS = 64
GAIN_ROW = 6 * POINTS

PIECES = {
    "up": (C, HID),
    "ipa_out": (C, C),
    "ipa_points": (C, C),
    "ipa_qkv": (C, 3 * C),
    "down": (HID, C),
    "time_qkv": (C, 3 * C),
    "time_out": (C, C),
}
EARLY_UNITS = [20, 19]
LATE_UNITS = [6, 6]
EARLY = max(EARLY_UNITS) * C
LATE = max(LATE_UNITS) * C
HALF = -(-(EARLY + LATE) // (SHARERS * 16)) * SHARERS * 16


def place_units():
    units, taken = {}, {True: [0, 0], False: [0, 0]}
    for name, (rows, columns) in PIECES.items():
        late = name.startswith("time")
        room = LATE_UNITS if late else EARLY_UNITS
        units[name] = []
        for _ in range(rows * columns // (C * 128)):
            half = 0 if taken[late][0] < room[0] else 1
            units[name].append((half, (EARLY if late else 0) + taken[late][half] * C))
            taken[late][half] += 1
    return units


UNITS = place_units()


def halves(core, keep_ref, give_ref):
    def put(name, value):
        tiles = value.shape[1] // 128
        base = EARLY if name.startswith("time") else 0
        pieces = [[], []]
        for unit, (half, at) in enumerate(UNITS[name]):
            down, across = (unit // tiles) * C, (unit % tiles) * 128
            part = value[down : down + C, across : across + 128].astype(BF16)
            pieces[half].append((at - base, part))

        for half in range(2):
            for ref, mine in ((keep_ref, True), (give_ref, False)):
                @pl.when((core == half) == mine)
                def store(ref=ref, parts=pieces[half]):
                    for at, part in parts:
                        ref[at : at + C, :] = part

    return put


def staged(core, stage_ref, keep_ref, give_ref, sems):
    waits = []

    def put(name, value):
        tiles = value.shape[1] // 128
        spans = {}
        for unit, (half, at) in enumerate(UNITS[name]):
            down, across = (unit // tiles) * C, (unit % tiles) * 128
            stage_ref[half, at : at + C, :] = value[down : down + C, across : across + 128].astype(
                BF16
            )
            low, _ = spans.get(half, (at, at))
            spans[half] = (low, at + C)
        for half, (low, high) in spans.items():
            sem = sems.at[len(waits)]
            source = stage_ref.at[half, low:high]

            @pl.when(core == half)
            def keep(source=source, low=low, high=high, sem=sem):
                pltpu.make_async_copy(source, keep_ref.at[low:high], sem).start()

            @pl.when(core != half)
            def give(source=source, low=low, high=high, sem=sem):
                pltpu.make_async_copy(source, give_ref.at[low:high], sem).start()

            waits.append(pltpu.make_async_copy(source, keep_ref.at[low:high], sem))

    return put, waits


MEGA = 1024 * 1024


def limit(megabytes):
    return pltpu.CompilerParams(vmem_limit_bytes=megabytes * MEGA)


SMEM = pl.BlockSpec(memory_space=pltpu.SMEM)
VMEM = pl.BlockSpec(memory_space=pltpu.VMEM)
HBM = pl.BlockSpec(memory_space=pltpu.HBM)


def mm(left, right):
    return lax.dot_general(left, right, (((1,), (0,)), ((), ())), preferred_element_type=F32)


def mt(left, right):
    return lax.dot_general(left, right, (((1,), (1,)), ((), ())), preferred_element_type=F32)


def tm(left, right):
    return lax.dot_general(left, right, (((0,), (0,)), ((), ())), preferred_element_type=F32)


def norm(values):
    centered = values - jnp.mean(values, axis=-1, keepdims=True)
    inverse = lax.rsqrt(jnp.mean(centered * centered, axis=-1, keepdims=True) + EPSILON)
    return centered * inverse, inverse


def norm_pull(cotangent, normed, inverse):
    return inverse * (
        cotangent
        - jnp.mean(cotangent, axis=-1, keepdims=True)
        - normed * jnp.mean(cotangent * normed, axis=-1, keepdims=True)
    )


def split_two(values):
    high = values.astype(BF16)
    return high, (values - high.astype(F32)).astype(BF16)


def split_three(values):
    high, rest = values.astype(BF16), None
    rest = values - high.astype(F32)
    middle = rest.astype(BF16)
    return high, middle, (rest - middle.astype(F32)).astype(BF16)


def order_matrix():
    row = lax.broadcasted_iota(jnp.int32, (N, N), 0)
    col = lax.broadcasted_iota(jnp.int32, (N, N), 1)
    return jnp.where((col // 8 == row % 16) & (col % 8 == row // 16), 1.0, 0.0).astype(BF16)


def tile_masks():
    lane = lax.broadcasted_iota(jnp.int32, (1, 128), 1)
    return [jnp.where(lane // 32 == m, 1.0, 0.0).astype(BF16) for m in range(4)]


def masked_stack(tile, masks):
    return jnp.concatenate([tile * mask for mask in masks], axis=0)


def pack_rows(tokens_ref, cotangent_ref, rigid_ref, packed_ref):
    frames, residues, _ = tokens_ref.shape
    order = order_matrix()
    for at, ref in ((0, tokens_ref), (C, cotangent_ref)):
        turned = tm(order, ref[...].reshape(N, C))
        packed_ref[:, :, at : at + C] = turned.reshape(residues, frames, C).astype(BF16)
    row = lax.broadcasted_iota(jnp.int32, (N, residues), 0)
    col = lax.broadcasted_iota(jnp.int32, (N, residues), 1)
    rigid = jnp.zeros((N, 12), F32)
    for f in range(frames):
        pick = jnp.where(row == col * frames + f, 1.0, 0.0).astype(BF16)
        rigid = rigid + mt(pick, rigid_ref[:, f, :])
    packed_ref[:, :, 2 * C :] = jnp.zeros((residues, frames, 128), BF16)
    packed_ref[:, :, 2 * C : 2 * C + 12] = rigid.reshape(residues, frames, 12).astype(BF16)


def time_forward(
    place_ref, neighbors_ref, rows_ref, wqkv_ref, wout_ref, sent_ref, qkv_ref, shares_ref, mix_ref
):
    x = rows_ref[:, 0:C].astype(F32)
    normed, _ = norm(x)
    qkv_ref[...] = mm(normed.astype(BF16), wqkv_ref[...]).astype(BF16)
    masks = tile_masks()
    for g in range(3):
        q = qkv_ref[:, g * 128 : (g + 1) * 128]
        k = qkv_ref[:, C + g * 128 : C + (g + 1) * 128]
        v = qkv_ref[:, 2 * C + g * 128 : 2 * C + (g + 1) * 128]
        for m in range(4):
            h = 4 * g + m
            scores = mt(q * masks[m], k) * SCALE
            raised = jnp.exp(scores - jnp.max(scores, axis=-1, keepdims=True))
            shares = raised / jnp.sum(raised, axis=-1, keepdims=True)
            shares_ref[:, h * 128 : (h + 1) * 128] = shares.astype(BF16)
        mixed = mm(shares_ref[:, g * 512 : (g + 1) * 512], masked_stack(v, masks))
        mix_ref[:, g * 128 : (g + 1) * 128] = mixed.astype(BF16)
    x1 = (x + mm(mix_ref[...], wout_ref[...])).astype(BF16)
    lane = lax.broadcasted_iota(jnp.int32, (N, 128), 1)
    count = jnp.zeros((N, 128), F32)
    for n in range(NB):
        count = count + jnp.where(lane == neighbors_ref[place_ref[0], n], 1.0, 0.0)
    sent = jnp.concatenate([x1, rows_ref[:, C:], count.astype(BF16)], axis=1)
    sent_ref[...] = sent.reshape(N, 8, 128)


def time_backward(
    core_ref, back_ref, rows_ref, qkv_ref, shares_ref, mix_ref, wqkv_ref, wout_ref,
    keep_early_ref, got_early_ref,
    sent_ref, keep_ref, give_ref, total_ref,
    dqkv_ref, dcol_ref, pcol_ref, early_ref, got_ref, sems,
):
    part = EARLY // 3
    spans = [slice(g * part, (g + 1) * part) for g in range(3)]
    arriving = []
    for g, span in enumerate(spans):
        arriving.append(
            (
                pltpu.make_async_copy(keep_early_ref.at[span], early_ref.at[span], sems.at[3 * g]),
                pltpu.make_async_copy(got_early_ref.at[span], got_ref.at[span], sems.at[3 * g + 1]),
            )
        )
    for pair in arriving:
        for copy in pair:
            copy.start()
    leaving = [
        pltpu.make_async_copy(early_ref.at[span], total_ref.at[span], sems.at[3 * g + 2])
        for g, span in enumerate(spans)
    ]
    put = halves(core_ref[0], keep_ref, give_ref)
    back = back_ref[...].reshape(N, 1024)
    dx1 = back[:, 0:C]
    normed, inverse = norm(rows_ref[:, 0:C].astype(F32))
    dmix = mt(dx1, wout_ref[...]).astype(BF16)
    put("time_out", tm(mix_ref[...], dx1))
    masks = tile_masks()
    for g in range(3):
        q = qkv_ref[:, g * 128 : (g + 1) * 128]
        k = qkv_ref[:, C + g * 128 : C + (g + 1) * 128]
        v = qkv_ref[:, 2 * C + g * 128 : 2 * C + (g + 1) * 128]
        dm = dmix[:, g * 128 : (g + 1) * 128]
        rows = []
        for m in range(4):
            h = 4 * g + m
            kept = shares_ref[:, h * 128 : (h + 1) * 128]
            pcol_ref[m * 128 : (m + 1) * 128, :] = kept
            shares = kept.astype(F32)
            dshares = mt(dm * masks[m], v)
            inner = jnp.sum(shares * dshares, axis=-1, keepdims=True)
            dlogit = (shares * (dshares - inner) * SCALE).astype(BF16)
            dcol_ref[m * 128 : (m + 1) * 128, :] = dlogit
            rows.append(dlogit)
        dq = mm(jnp.concatenate(rows, axis=1), masked_stack(k, masks))
        dk = tm(dcol_ref[...], masked_stack(q, masks))
        dv = tm(pcol_ref[...], masked_stack(dm, masks))
        dqkv_ref[:, g * 128 : (g + 1) * 128] = dq.astype(BF16)
        dqkv_ref[:, C + g * 128 : C + (g + 1) * 128] = dk.astype(BF16)
        dqkv_ref[:, 2 * C + g * 128 : 2 * C + (g + 1) * 128] = dv.astype(BF16)
        for copy in arriving[g]:
            copy.wait()
        summed = early_ref[spans[g], :].astype(F32) + got_ref[spans[g], :].astype(F32)
        early_ref[spans[g], :] = summed.astype(BF16)
        leaving[g].start()
    put("time_qkv", tm(normed.astype(BF16), dqkv_ref[...]))
    dnormed = mt(dqkv_ref[...], wqkv_ref[...]).astype(BF16).astype(F32)
    pulled = norm_pull(dnormed, normed, inverse).astype(BF16).astype(F32)
    sent_ref[:, 0:C] = (dx1.astype(F32) + pulled).astype(BF16)
    sent_ref[:, C : 2 * C] = back[:, C : 2 * C]
    for copy in leaving:
        copy.wait()


def selectors():
    lane = np.arange(256)
    inside = lane < 3 * POINTS
    head = np.where(inside, (lane % POINTS) // P_SIZE, -1)
    heads = (head[None, :] == np.arange(16)[:, None]).astype(np.float32)
    turn = np.zeros((128, 4 * 256), np.float32)
    for a in range(3):
        at = a * POINTS + np.arange(POINTS)
        for b in range(3):
            turn[3 * a + b, b * 256 + at] = 1.0
        turn[9 + a, 3 * 256 + at] = 1.0
    spread = np.zeros((128, 256), np.float32)
    spread[16:32] = heads
    gather = np.zeros((6 * 256, C), np.float32)
    for c in range(2):
        for b in range(3):
            for a in range(3):
                for p in range(POINTS):
                    gather[(3 * c + b) * 256 + a * POINTS + p, (3 * c + b) * POINTS + p] = 1.0
    return [jnp.asarray(item, BF16) for item in (heads, turn, spread, gather)]


def point_attention(
    core_ref, weight_ref, rows_ref, *refs
):
    sources, refs = refs[:10], refs[10:]
    back_ref, keep_ref, give_ref = refs[:3]
    (
        qkv_ref, mix_ref, shares_ref, point_ref, prow_ref, pcol_ref, drow_ref, dcol_ref,
        dqkv_ref, dlocal_ref, keys_ref, queries_ref, side_ref, stage_ref,
    ) = refs[3:17]
    held, sems, out_sems = refs[17:27], refs[27], refs[28]
    fetched = [
        pltpu.make_async_copy(source, target, sems.at[k])
        for k, (source, target) in enumerate(zip(sources, held))
    ]
    for copy in fetched:
        copy.start()
    (
        wqkv_ref, turn_ref, wrep_ref, heads_ref, wout_ref, wup_ref, wdown_ref, spread_ref,
        gather_ref, wpts_ref,
    ) = held
    put, leaving = staged(core_ref[0], stage_ref, keep_ref, give_ref, out_sems)
    stage_ref[1, EARLY_UNITS[1] * C : EARLY, :] = jnp.zeros((EARLY - EARLY_UNITS[1] * C, 128), BF16)
    spare = stage_ref.at[1, EARLY_UNITS[1] * C : EARLY]
    spare_copy = pltpu.make_async_copy(
        spare, keep_ref.at[EARLY_UNITS[1] * C : EARLY], out_sems.at[8]
    )

    @pl.when(core_ref[0] == 1)
    def keep_spare():
        spare_copy.start()

    @pl.when(core_ref[0] != 1)
    def give_spare():
        pltpu.make_async_copy(
            spare, give_ref.at[EARLY_UNITS[1] * C : EARLY], out_sems.at[8]
        ).start()

    masks = tile_masks()
    order = order_matrix()
    rows = mm(order, rows_ref[...].reshape(N, 1024))
    x1 = rows[:, 0:C]
    side_ref[...] = rows[:, C:].astype(BF16)
    normed, inverse = norm(x1)
    n2 = normed.astype(BF16)
    fetched[0].wait()
    qkv_ref[...] = mm(n2, wqkv_ref[...]).astype(BF16)

    lane = lax.broadcasted_iota(jnp.int32, (1, 256), 1)
    lane_head = jnp.where(lane < 3 * POINTS, (lane % POINTS) // P_SIZE, lane - 3 * POINTS)
    raw = jnp.zeros((1, 256), F32)
    for h in range(H):
        raw = jnp.where((lane < 3 * POINTS) & (lane_head == h), weight_ref[h], raw)
    soft = jnp.maximum(raw, 0.0) + jnp.log(1.0 + jnp.exp(-jnp.abs(raw)))
    strength = jnp.where(lane < 3 * POINTS, soft * STRENGTH, 0.0)
    head_masks = [jnp.where(lane_head == h, 1.0, 0.0).astype(BF16) for h in range(H)]

    for copy in fetched[1:4]:
        copy.wait()
    turned = mm(side_ref[:, C : C + 128], turn_ref[...])
    turns = [turned[:, b * 256 : (b + 1) * 256] for b in range(3)]
    local = mt(n2, wrep_ref[...])
    placed = []
    for c in range(2):
        total = turned[:, 768:1024]
        for b in range(3):
            total = total + turns[b] * local[:, (3 * c + b) * 256 : (3 * c + b + 1) * 256]
        placed.append(total)
    gq = placed[0]
    gk_bf = placed[1].astype(BF16)
    gk = gk_bf.astype(F32)
    heads = heads_ref[...]
    own = sum(mt(part, heads) for part in split_three(gq * gq * (0.5 * strength)))
    other = sum(mt(heads, part) for part in split_three(gk * gk * (0.5 * strength)))
    q_high, q_low = split_two(gq * strength)
    ones = (lane >= 3 * POINTS) & (lane < 3 * POINTS + 16)
    keys_one = jnp.where(ones, 1.0, gk).astype(BF16)
    queries_one = jnp.where(ones, 1.0, gq).astype(BF16)
    two_keys = jnp.concatenate([gk_bf, gk_bf], axis=1)
    count = side_ref[:, C + 128 : C + 256].astype(F32)
    near = count > 0.0

    for g in range(3):
        q = qkv_ref[:, g * 128 : (g + 1) * 128]
        k = qkv_ref[:, C + g * 128 : C + (g + 1) * 128]
        v = qkv_ref[:, 2 * C + g * 128 : 2 * C + (g + 1) * 128]
        for m in range(4):
            h = 4 * g + m
            at = slice(h * 128, (h + 1) * 128)
            direct = mt(q * masks[m], k) * (SCALE * math.sqrt(0.5))
            cross = mt(
                jnp.concatenate([q_high * head_masks[h], q_low * head_masks[h]], axis=1), two_keys
            )
            spot = cross - own[:, h : h + 1] - other[h : h + 1, :]
            point_ref[:, at] = spot
            logits = jnp.where(near, direct + spot, -1e30)
            raised = jnp.exp(logits - jnp.max(logits, axis=-1, keepdims=True)) * count
            shares = raised / jnp.sum(raised, axis=-1, keepdims=True)
            shares_ref[:, at] = shares
            prow_ref[:, at] = shares.astype(BF16)
            pcol_ref[at, :] = shares.astype(BF16)
            keys_ref[at, :] = keys_one * head_masks[h]
            queries_ref[at, :] = queries_one * head_masks[h]
        mixed = mm(prow_ref[:, g * 512 : (g + 1) * 512], masked_stack(v, masks))
        mix_ref[:, g * 128 : (g + 1) * 128] = mixed.astype(BF16)

    for copy in fetched[4:7]:
        copy.wait()
    cot = side_ref[:, 0:C]
    x2 = (x1 + mm(mix_ref[...], wout_ref[...])).astype(BF16).astype(F32)
    normed2, inverse2 = norm(x2)
    n3 = normed2.astype(BF16)
    u = mm(n3, wup_ref[...])
    root = math.sqrt(2.0 / math.pi)
    bent = jnp.tanh(root * (u + 0.044715 * u * u * u))
    hidden = (0.5 * u * (1.0 + bent)).astype(BF16)
    slope = 0.5 * (1.0 + bent) + 0.5 * u * (1.0 - bent * bent) * root * (
        1.0 + 3.0 * 0.044715 * u * u
    )
    updated = (x2 + mm(hidden, wdown_ref[...])).astype(BF16)
    put("down", tm(hidden, cot))
    dhidden = mt(cot, wdown_ref[...]).astype(BF16).astype(F32)
    du = (dhidden * slope).astype(BF16)
    put("up", tm(n3, du))
    dn3 = mt(du, wup_ref[...]).astype(BF16).astype(F32)
    dx2 = (cot.astype(F32) + norm_pull(dn3, normed2, inverse2).astype(BF16).astype(F32)).astype(
        BF16
    )
    dmix = mt(dx2, wout_ref[...]).astype(BF16)
    put("ipa_out", tm(mix_ref[...], dx2))

    gains = []
    for g in range(3):
        q = qkv_ref[:, g * 128 : (g + 1) * 128]
        k = qkv_ref[:, C + g * 128 : C + (g + 1) * 128]
        v = qkv_ref[:, 2 * C + g * 128 : 2 * C + (g + 1) * 128]
        dm = dmix[:, g * 128 : (g + 1) * 128]
        for m in range(4):
            h = 4 * g + m
            at = slice(h * 128, (h + 1) * 128)
            shares = shares_ref[:, at]
            dshares = mt(dm * masks[m], v)
            dlogit = shares * (dshares - jnp.sum(shares * dshares, axis=-1, keepdims=True))
            gains.append(jnp.sum(dlogit * point_ref[:, at], axis=0, keepdims=True))
            drow_ref[:, at] = dlogit.astype(BF16)
            dcol_ref[at, :] = dlogit.astype(BF16)
        group = slice(g * 512, (g + 1) * 512)
        dq = mm(drow_ref[:, group], masked_stack(k, masks)) * (SCALE * math.sqrt(0.5))
        dk = tm(dcol_ref[group, :], masked_stack(q, masks)) * (SCALE * math.sqrt(0.5))
        dv = tm(pcol_ref[group, :], masked_stack(dm, masks))
        dqkv_ref[:, g * 128 : (g + 1) * 128] = dq.astype(BF16)
        dqkv_ref[:, C + g * 128 : C + (g + 1) * 128] = dk.astype(BF16)
        dqkv_ref[:, 2 * C + g * 128 : 2 * C + (g + 1) * 128] = dv.astype(BF16)

    lane128 = lax.broadcasted_iota(jnp.int32, (1, 128), 1)
    gain = jnp.zeros((1, 128), F32)
    raw_row = jnp.zeros((1, 128), F32)
    for h in range(H):
        here = lane128 == h
        gain = jnp.where(here, jnp.sum(gains[h], axis=1, keepdims=True), gain)
        raw_row = jnp.where(here, weight_ref[h], raw_row)
    soft_row = jnp.maximum(raw_row, 0.0) + jnp.log(1.0 + jnp.exp(-jnp.abs(raw_row)))
    gain = gain / ((1.0 + jnp.exp(-raw_row)) * soft_row)

    for copy in fetched[7:10]:
        copy.wait()
    from_keys = mm(drow_ref[...], keys_ref[...])
    from_queries = tm(dcol_ref[...], queries_ref[...])
    spread = spread_ref[...]
    own_sum = sum(mm(part, spread) for part in split_two(from_keys[:, 128:256]))
    other_sum = sum(mm(part, spread) for part in split_two(from_queries[:, 128:256]))
    dgq = strength * (from_keys - gq * own_sum)
    dgk = (strength * (from_queries - gk * other_sum)).astype(BF16).astype(F32)
    for b in range(3):
        dlocal_ref[:, b * 256 : (b + 1) * 256] = (turns[b] * dgq).astype(BF16)
        dlocal_ref[:, (3 + b) * 256 : (4 + b) * 256] = (turns[b] * dgk).astype(BF16)
    dpoints = mm(dlocal_ref[...], gather_ref[...]).astype(BF16)
    dqkv = dqkv_ref[...]
    put("ipa_qkv", tm(n2, dqkv))
    gpts = tm(dpoints, n2)
    spare_row = lax.broadcasted_iota(jnp.int32, (C, 128), 0) == GAIN_ROW
    first = gpts[:, 0:128] + jnp.where(spare_row, gain, 0.0)
    put("ipa_points", jnp.concatenate([first, gpts[:, 128:]], axis=1))
    dn2 = (mt(dqkv, wqkv_ref[...]) + mm(dpoints[:, 0 : 6 * POINTS], wpts_ref[...])).astype(BF16).astype(F32)
    dx1 = (dx2.astype(F32) + norm_pull(dn2, normed, inverse).astype(BF16).astype(F32)).astype(BF16)
    back = jnp.concatenate([dx1, updated, jnp.zeros((N, 256), BF16)], axis=1)
    back_ref[...] = tm(order, back).astype(BF16).reshape(N, 8, 128)
    for copy in leaving + [spare_copy]:
        copy.wait()


def like(shape, dtype):
    return jax.ShapeDtypeStruct(shape, dtype)


def call_pack_rows(tokens, cotangent, rigid):
    frames, residues, _ = tokens.shape
    return pl.pallas_call(
        pack_rows,
        out_shape=like((residues, frames, 2 * C + 128), BF16),
        compiler_params=limit(60),
        name="pack_rows",
    )(tokens, cotangent, rigid)


def call_time_forward(place, neighbors, rows, w_qkv, w_out):
    return pl.pallas_call(
        time_forward,
        in_specs=[SMEM, SMEM, VMEM, VMEM, VMEM],
        out_shape=(
            like((N, 8, 128), BF16), like((N, 3 * C), BF16), like((N, H * N), BF16),
            like((N, C), BF16),
        ),
        compiler_params=limit(60),
        name="time_forward",
    )(place, neighbors, rows, w_qkv, w_out)


def call_time_backward(core, back, rows, qkv, shares, mix, w_qkv, w_out, keep_early, got_early):
    return pl.pallas_call(
        time_backward,
        in_specs=[SMEM] + [VMEM] * 7 + [HBM] * 2,
        out_specs=(VMEM, VMEM, VMEM, HBM),
        out_shape=(
            like((N, 2 * C), BF16), like((LATE, 128), BF16), like((LATE, 128), BF16),
            like((HALF, 128), BF16),
        ),
        scratch_shapes=[
            pltpu.VMEM((N, 3 * C), BF16), pltpu.VMEM((4 * N, N), BF16), pltpu.VMEM((4 * N, N), BF16),
            pltpu.VMEM((EARLY, 128), BF16), pltpu.VMEM((EARLY, 128), BF16),
            pltpu.SemaphoreType.DMA((9,)),
        ],
        compiler_params=limit(20),
        name="time_backward",
    )(core, back, rows, qkv, shares, mix, w_qkv, w_out, keep_early, got_early)


def call_point_attention(core, weight, rows, w_qkv, w_pts, w_rep, w_out, w_up, w_down):
    heads, turn, spread, gather = selectors()
    sources = [w_qkv, turn, w_rep, heads, w_out, w_up, w_down, spread, gather, w_pts]
    return pl.pallas_call(
        point_attention,
        in_specs=[SMEM, SMEM, VMEM] + [HBM] * len(sources),
        out_specs=(VMEM, HBM, HBM),
        out_shape=(like((N, 8, 128), BF16), like((EARLY, 128), BF16), like((EARLY, 128), BF16)),
        scratch_shapes=[
            pltpu.VMEM((N, 3 * C), BF16), pltpu.VMEM((N, C), BF16),
            pltpu.VMEM((N, H * N), F32), pltpu.VMEM((N, H * N), F32),
            pltpu.VMEM((N, H * N), BF16), pltpu.VMEM((H * N, N), BF16),
            pltpu.VMEM((N, H * N), BF16), pltpu.VMEM((H * N, N), BF16),
            pltpu.VMEM((N, 3 * C), BF16), pltpu.VMEM((N, 6 * 256), BF16),
            pltpu.VMEM((H * N, 256), BF16), pltpu.VMEM((H * N, 256), BF16),
            pltpu.VMEM((N, 640), BF16), pltpu.VMEM((2, EARLY, 128), BF16),
            *[pltpu.VMEM(source.shape, BF16) for source in sources],
            pltpu.SemaphoreType.DMA((len(sources),)), pltpu.SemaphoreType.DMA((9,)),
        ],
        compiler_params=limit(60),
        name="point_attention",
    )(core, weight, rows, *sources)


def add_late(total_in_ref, keep_ref, got_ref, total_ref, late_ref, sem):
    late = keep_ref[...].astype(F32) + got_ref[...].astype(F32)
    late_ref[0:LATE, :] = late.astype(BF16)
    late_ref[LATE:, :] = jnp.zeros((HALF - EARLY - LATE, 128), BF16)
    copy = pltpu.make_async_copy(late_ref, total_ref.at[EARLY:HALF], sem)
    copy.start()
    copy.wait()


def call_add_late(total, keep, got):
    return pl.pallas_call(
        add_late,
        in_specs=[HBM, VMEM, VMEM],
        out_specs=HBM,
        out_shape=like((HALF, 128), BF16),
        scratch_shapes=[pltpu.VMEM((HALF - EARLY, 128), BF16), pltpu.SemaphoreType.DMA],
        input_output_aliases={0: 0},
        compiler_params=limit(8),
        name="add_late",
    )(total, keep, got)


def add_parts(parts_ref, copies_ref):
    count = parts_ref.shape[0]
    total = parts_ref[0].astype(F32)
    for k in range(1, count):
        total = total + parts_ref[k].astype(F32)
    total = total.astype(BF16)
    for k in range(count):
        copies_ref[k] = total


def call_add_parts(parts):
    return pl.pallas_call(
        add_parts, out_shape=like(parts.shape, BF16), compiler_params=limit(12), name="add_parts"
    )(parts)


def unpack(core_ref, mine_ref, other_ref, ended_ref, *refs):
    out_refs, gain_ref, output_ref, token_ref = refs[:7], refs[7], refs[8], refs[9]
    half_ref, stages, in_sems, out_sems = refs[10], refs[11:18], refs[18], refs[19]
    core = core_ref[0]
    mine = pltpu.make_async_copy(mine_ref, half_ref.at[core], in_sems.at[0])
    other = pltpu.make_async_copy(other_ref, half_ref.at[1 - core], in_sems.at[1])
    mine.start()
    other.start()
    residues, frames, _ = ended_ref.shape
    ended = mm(order_matrix(), ended_ref[...].reshape(N, 2 * C)).astype(BF16)
    token_ref[...] = ended[:, 0:C].reshape(frames, residues, C)
    output_ref[...] = ended[:, C:].reshape(frames, residues, C)
    mine.wait()
    other.wait()
    leaving = []
    for k, (name, (rows, columns)) in enumerate(PIECES.items()):
        tiles = columns // 128
        for unit, (half, at) in enumerate(UNITS[name]):
            down, across = (unit // tiles) * C, (unit % tiles) * 128
            value = half_ref[half, at : at + C, :].astype(F32)
            if name == "ipa_points":
                stages[k][:, across : across + 128] = value[0:GAIN_ROW]
                if across == 0:
                    gain = value[GAIN_ROW : GAIN_ROW + 1, :]
            else:
                stages[k][down : down + C, across : across + 128] = value
        leaving.append(pltpu.make_async_copy(stages[k], out_refs[k], out_sems.at[k]))
        leaving[-1].start()
    lane = lax.broadcasted_iota(jnp.int32, (1, 128), 1)
    for h in range(H):
        gain_ref[h] = jnp.sum(jnp.where(lane == h, gain, 0.0))
    for copy in leaving:
        copy.wait()


def call_unpack(core, mine, other, ended):
    residues, frames, _ = ended.shape
    shapes = [
        (GAIN_ROW if name == "ipa_points" else rows, columns)
        for name, (rows, columns) in PIECES.items()
    ]
    rows = like((frames, residues, C), BF16)
    return pl.pallas_call(
        unpack,
        in_specs=[SMEM, HBM, HBM, VMEM],
        out_specs=(*[HBM] * 7, SMEM, VMEM, VMEM),
        out_shape=(*[like(shape, F32) for shape in shapes], like((H,), F32), rows, rows),
        scratch_shapes=[
            pltpu.VMEM((2, HALF, 128), BF16),
            *[pltpu.VMEM(shape, F32) for shape in shapes],
            pltpu.SemaphoreType.DMA((2,)), pltpu.SemaphoreType.DMA((7,)),
        ],
        compiler_params=limit(24),
        name="unpack",
    )(core, mine, other, ended)


def repeat_points(weight):
    parts = weight.reshape(6, POINTS, C)
    tripled = jnp.concatenate([parts, parts, parts], axis=1)
    return jnp.pad(tripled, ((0, 0), (0, 256 - 3 * POINTS), (0, 0))).reshape(6 * 256, C)


def swap_rows(rows, axes):
    return lax.all_to_all(rows, axes, split_axis=0, concat_axis=0, tiled=True)


def body(
    tokens, rigid_frames, neighbors, w_time_qkv, w_time_out, w_ipa_qkv, w_ipa_points,
    point_weight, w_ipa_out, w_up, w_down, cotangent,
):
    frames, residues = tokens.shape[:2]
    place = lax.axis_index(("line", "core")).astype(jnp.int32).reshape(1)
    core = lax.axis_index("core").astype(jnp.int32).reshape(1)
    swap = [(0, 1), (1, 0)]
    points = w_ipa_points.T
    rows = swap_rows(call_pack_rows(tokens, cotangent, rigid_frames), ("line", "core"))
    rows = rows.reshape(N, 2 * C + 128)
    sent, qkv, shares, mix = call_time_forward(place, neighbors, rows, w_time_qkv, w_time_out)
    back, keep_early, give_early = call_point_attention(
        core, point_weight, swap_rows(sent, EVERYONE), w_ipa_qkv, points, repeat_points(points),
        w_ipa_out, w_up, w_down,
    )
    got_early = lax.ppermute(give_early, "core", swap)
    ended, keep_late, give_late, total = call_time_backward(
        core, swap_rows(back, EVERYONE), rows, qkv, shares, mix, w_time_qkv, w_time_out,
        keep_early, got_early,
    )
    got_late = lax.ppermute(give_late, "core", swap)
    total = call_add_late(total, keep_late, got_late)
    parts = swap_rows(total.reshape(SHARERS, HALF // SHARERS, 128), ("line", "res"))
    mine = swap_rows(call_add_parts(parts), ("line", "res")).reshape(HALF, 128)
    other = lax.ppermute(mine, "core", swap)
    ended = swap_rows(ended.reshape(residues, frames, 2 * C), ("line", "core"))
    *grads, gain, output, token_grad = call_unpack(core, mine, other, ended)
    grads = dict(zip(PIECES, grads))
    return (
        output, token_grad, grads["time_qkv"], grads["time_out"], grads["ipa_qkv"],
        grads["ipa_points"].T, gain, grads["ipa_out"], grads["up"], grads["down"],
    )


def solution(mesh):
    devices = mesh.devices
    split = Mesh(
        devices.reshape(devices.shape[0] // 2, 2, devices.shape[1]), ("line", "core", "res")
    )
    frame = ("line", "core")
    rows = P(frame, "res", None)
    placed = (rows, P(None, frame, "res"), P("res", None)) + (P(),) * 8 + (rows,)
    return jax.shard_map(
        body,
        mesh=split,
        in_specs=placed,
        out_specs=(rows, rows) + (P(),) * 8,
        check_vma=False,
    )
```

```python
import math

import jax
import jax.numpy as jnp
import numpy as np
from jax import lax
from jax.experimental import pallas as pl
from jax.experimental.pallas import tpu as pltpu
from jax.sharding import Mesh, PartitionSpec as P

H = 12
P_SIZE = 4
NB = 32
C = 384
HID = 1536
N = 128
POINTS = H * P_SIZE
EPSILON = 1e-05
SCALE = 1.0 / math.sqrt(C // H)
STRENGTH = math.sqrt(2.0 / (9.0 * P_SIZE)) * math.sqrt(0.5)
F32 = jnp.float32
BF16 = jnp.bfloat16
EVERYONE = ("line", "core", "res")
SHARERS = 32
GAIN_ROW = 6 * POINTS

PIECES = {
    "up": (C, HID),
    "ipa_out": (C, C),
    "ipa_points": (C, C),
    "ipa_qkv": (C, 3 * C),
    "down": (HID, C),
    "time_qkv": (C, 3 * C),
    "time_out": (C, C),
}
EARLY_UNITS = [20, 19]
LATE_UNITS = [6, 6]
EARLY = max(EARLY_UNITS) * C
LATE = max(LATE_UNITS) * C
QUARTER = -(-(EARLY + LATE) // (2 * SHARERS * 16)) * SHARERS * 16
CHUNK = QUARTER // SHARERS


def pair_groups():
    bits = (2, 1)
    place = lambda line, core, res: (line * 2 + core) * 8 + res
    spots = [(line, core, res) for line in range(8) for core in range(2) for res in range(8)]
    pairs = [(place(*spot), place(spot[0], spot[1], spot[2] ^ bits[spot[1]])) for spot in spots]
    groups = [
        [place(line, core, res) for line in range(8) for res in range(8) if bool(res & bits[core]) == odd]
        for core in range(2)
        for odd in (False, True)
    ]
    return pairs, groups


PAIRS, GROUPS = pair_groups()


def place_units():
    units, taken = {}, {True: [0, 0], False: [0, 0]}
    for name, (rows, columns) in PIECES.items():
        late = name.startswith("time")
        room = LATE_UNITS if late else EARLY_UNITS
        units[name] = []
        for _ in range(rows * columns // (C * 128)):
            half = 0 if taken[late][0] < room[0] else 1
            units[name].append((half, (EARLY if late else 0) + taken[late][half] * C))
            taken[late][half] += 1
    return units


UNITS = place_units()


def halves(core, keep_ref, give_ref):
    def put(name, value):
        tiles = value.shape[1] // 128
        base = EARLY if name.startswith("time") else 0
        pieces = [[], []]
        for unit, (half, at) in enumerate(UNITS[name]):
            down, across = (unit // tiles) * C, (unit % tiles) * 128
            part = value[down : down + C, across : across + 128].astype(BF16)
            pieces[half].append((at - base, part))

        for half in range(2):
            for ref, mine in ((keep_ref, True), (give_ref, False)):
                @pl.when((core == half) == mine)
                def store(ref=ref, parts=pieces[half]):
                    for at, part in parts:
                        ref[at : at + C, :] = part

    return put


def staged(core, stage_ref, keep_ref, give_ref, sems):
    waits = []

    def put(name, value):
        tiles = value.shape[1] // 128
        spans = {}
        for unit, (half, at) in enumerate(UNITS[name]):
            down, across = (unit // tiles) * C, (unit % tiles) * 128
            stage_ref[half, at : at + C, :] = value[down : down + C, across : across + 128].astype(
                BF16
            )
            low, _ = spans.get(half, (at, at))
            spans[half] = (low, at + C)
        for half, (low, high) in spans.items():
            sem = sems.at[len(waits)]
            source = stage_ref.at[half, low:high]

            @pl.when(core == half)
            def keep(source=source, low=low, high=high, sem=sem):
                pltpu.make_async_copy(source, keep_ref.at[low:high], sem).start()

            @pl.when(core != half)
            def give(source=source, low=low, high=high, sem=sem):
                pltpu.make_async_copy(source, give_ref.at[low:high], sem).start()

            waits.append(pltpu.make_async_copy(source, keep_ref.at[low:high], sem))

    return put, waits


MEGA = 1024 * 1024


def limit(megabytes):
    return pltpu.CompilerParams(vmem_limit_bytes=megabytes * MEGA)


SMEM = pl.BlockSpec(memory_space=pltpu.SMEM)
VMEM = pl.BlockSpec(memory_space=pltpu.VMEM)
HBM = pl.BlockSpec(memory_space=pltpu.HBM)


def mm(left, right):
    return lax.dot_general(left, right, (((1,), (0,)), ((), ())), preferred_element_type=F32)


def mt(left, right):
    return lax.dot_general(left, right, (((1,), (1,)), ((), ())), preferred_element_type=F32)


def tm(left, right):
    return lax.dot_general(left, right, (((0,), (0,)), ((), ())), preferred_element_type=F32)


def norm(values):
    centered = values - jnp.mean(values, axis=-1, keepdims=True)
    inverse = lax.rsqrt(jnp.mean(centered * centered, axis=-1, keepdims=True) + EPSILON)
    return centered * inverse, inverse


def norm_pull(cotangent, normed, inverse):
    return inverse * (
        cotangent
        - jnp.mean(cotangent, axis=-1, keepdims=True)
        - normed * jnp.mean(cotangent * normed, axis=-1, keepdims=True)
    )


def split_two(values):
    high = values.astype(BF16)
    return high, (values - high.astype(F32)).astype(BF16)


def split_three(values):
    high, rest = values.astype(BF16), None
    rest = values - high.astype(F32)
    middle = rest.astype(BF16)
    return high, middle, (rest - middle.astype(F32)).astype(BF16)


def order_matrix():
    row = lax.broadcasted_iota(jnp.int32, (N, N), 0)
    col = lax.broadcasted_iota(jnp.int32, (N, N), 1)
    return jnp.where((col // 8 == row % 16) & (col % 8 == row // 16), 1.0, 0.0).astype(BF16)


def tile_masks():
    lane = lax.broadcasted_iota(jnp.int32, (1, 128), 1)
    return [jnp.where(lane // 32 == m, 1.0, 0.0).astype(BF16) for m in range(4)]


def masked_stack(tile, masks):
    return jnp.concatenate([tile * mask for mask in masks], axis=0)


def pack_rows(tokens_ref, cotangent_ref, rigid_ref, packed_ref):
    frames, residues, _ = tokens_ref.shape
    order = order_matrix()
    for at, ref in ((0, tokens_ref), (C, cotangent_ref)):
        turned = tm(order, ref[...].reshape(N, C))
        packed_ref[:, :, at : at + C] = turned.reshape(residues, frames, C).astype(BF16)
    row = lax.broadcasted_iota(jnp.int32, (N, residues), 0)
    col = lax.broadcasted_iota(jnp.int32, (N, residues), 1)
    rigid = jnp.zeros((N, 12), F32)
    for f in range(frames):
        pick = jnp.where(row == col * frames + f, 1.0, 0.0).astype(BF16)
        rigid = rigid + mt(pick, rigid_ref[:, f, :])
    packed_ref[:, :, 2 * C :] = jnp.zeros((residues, frames, 128), BF16)
    packed_ref[:, :, 2 * C : 2 * C + 12] = rigid.reshape(residues, frames, 12).astype(BF16)


def time_forward(
    place_ref, neighbors_ref, rows_ref, wqkv_ref, wout_ref, sent_ref, qkv_ref, shares_ref, mix_ref
):
    x = rows_ref[:, 0:C].astype(F32)
    normed, _ = norm(x)
    qkv_ref[...] = mm(normed.astype(BF16), wqkv_ref[...]).astype(BF16)
    masks = tile_masks()
    for g in range(3):
        q = qkv_ref[:, g * 128 : (g + 1) * 128]
        k = qkv_ref[:, C + g * 128 : C + (g + 1) * 128]
        v = qkv_ref[:, 2 * C + g * 128 : 2 * C + (g + 1) * 128]
        for m in range(4):
            h = 4 * g + m
            scores = mt(q * masks[m], k) * SCALE
            raised = jnp.exp(scores - jnp.max(scores, axis=-1, keepdims=True))
            shares = raised / jnp.sum(raised, axis=-1, keepdims=True)
            shares_ref[:, h * 128 : (h + 1) * 128] = shares.astype(BF16)
        mixed = mm(shares_ref[:, g * 512 : (g + 1) * 512], masked_stack(v, masks))
        mix_ref[:, g * 128 : (g + 1) * 128] = mixed.astype(BF16)
    x1 = (x + mm(mix_ref[...], wout_ref[...])).astype(BF16)
    lane = lax.broadcasted_iota(jnp.int32, (N, 128), 1)
    count = jnp.zeros((N, 128), F32)
    for n in range(NB):
        count = count + jnp.where(lane == neighbors_ref[place_ref[0], n], 1.0, 0.0)
    sent = jnp.concatenate([x1, rows_ref[:, C:], count.astype(BF16)], axis=1)
    sent_ref[...] = sent.reshape(N, 8, 128)


def time_backward(
    core_ref, back_ref, rows_ref, qkv_ref, shares_ref, mix_ref, wqkv_ref, wout_ref,
    sent_ref, keep_ref, give_ref, dqkv_ref, dcol_ref, pcol_ref,
):
    put = halves(core_ref[0], keep_ref, give_ref)
    back = back_ref[...].reshape(N, 1024)
    dx1 = back[:, 0:C]
    normed, inverse = norm(rows_ref[:, 0:C].astype(F32))
    dmix = mt(dx1, wout_ref[...]).astype(BF16)
    put("time_out", tm(mix_ref[...], dx1))
    masks = tile_masks()
    for g in range(3):
        q = qkv_ref[:, g * 128 : (g + 1) * 128]
        k = qkv_ref[:, C + g * 128 : C + (g + 1) * 128]
        v = qkv_ref[:, 2 * C + g * 128 : 2 * C + (g + 1) * 128]
        dm = dmix[:, g * 128 : (g + 1) * 128]
        rows = []
        for m in range(4):
            h = 4 * g + m
            kept = shares_ref[:, h * 128 : (h + 1) * 128]
            pcol_ref[m * 128 : (m + 1) * 128, :] = kept
            shares = kept.astype(F32)
            dshares = mt(dm * masks[m], v)
            inner = jnp.sum(shares * dshares, axis=-1, keepdims=True)
            dlogit = (shares * (dshares - inner) * SCALE).astype(BF16)
            dcol_ref[m * 128 : (m + 1) * 128, :] = dlogit
            rows.append(dlogit)
        dq = mm(jnp.concatenate(rows, axis=1), masked_stack(k, masks))
        dk = tm(dcol_ref[...], masked_stack(q, masks))
        dv = tm(pcol_ref[...], masked_stack(dm, masks))
        dqkv_ref[:, g * 128 : (g + 1) * 128] = dq.astype(BF16)
        dqkv_ref[:, C + g * 128 : C + (g + 1) * 128] = dk.astype(BF16)
        dqkv_ref[:, 2 * C + g * 128 : 2 * C + (g + 1) * 128] = dv.astype(BF16)
    put("time_qkv", tm(normed.astype(BF16), dqkv_ref[...]))
    dnormed = mt(dqkv_ref[...], wqkv_ref[...]).astype(BF16).astype(F32)
    pulled = norm_pull(dnormed, normed, inverse).astype(BF16).astype(F32)
    sent_ref[:, 0:C] = (dx1.astype(F32) + pulled).astype(BF16)
    sent_ref[:, C : 2 * C] = back[:, C : 2 * C]


def selectors():
    lane = np.arange(256)
    inside = lane < 3 * POINTS
    head = np.where(inside, (lane % POINTS) // P_SIZE, -1)
    heads = (head[None, :] == np.arange(16)[:, None]).astype(np.float32)
    turn = np.zeros((128, 4 * 256), np.float32)
    for a in range(3):
        at = a * POINTS + np.arange(POINTS)
        for b in range(3):
            turn[3 * a + b, b * 256 + at] = 1.0
        turn[9 + a, 3 * 256 + at] = 1.0
    spread = np.zeros((128, 256), np.float32)
    spread[16:32] = heads
    gather = np.zeros((6 * 256, C), np.float32)
    for c in range(2):
        for b in range(3):
            for a in range(3):
                for p in range(POINTS):
                    gather[(3 * c + b) * 256 + a * POINTS + p, (3 * c + b) * POINTS + p] = 1.0
    return [jnp.asarray(item, BF16) for item in (heads, turn, spread, gather)]


def point_attention(
    core_ref, weight_ref, rows_ref, *refs
):
    sources, refs = refs[:10], refs[10:]
    back_ref, keep_ref, give_ref = refs[:3]
    (
        qkv_ref, mix_ref, shares_ref, point_ref, prow_ref, pcol_ref, drow_ref, dcol_ref,
        dqkv_ref, dlocal_ref, keys_ref, queries_ref, side_ref, stage_ref,
    ) = refs[3:17]
    held, sems, out_sems = refs[17:27], refs[27], refs[28]
    fetched = [
        pltpu.make_async_copy(source, target, sems.at[k])
        for k, (source, target) in enumerate(zip(sources, held))
    ]
    for copy in fetched:
        copy.start()
    (
        wqkv_ref, turn_ref, wrep_ref, heads_ref, wout_ref, wup_ref, wdown_ref, spread_ref,
        gather_ref, wpts_ref,
    ) = held
    put, leaving = staged(core_ref[0], stage_ref, keep_ref, give_ref, out_sems)
    stage_ref[1, EARLY_UNITS[1] * C : EARLY, :] = jnp.zeros((EARLY - EARLY_UNITS[1] * C, 128), BF16)
    spare = stage_ref.at[1, EARLY_UNITS[1] * C : EARLY]
    spare_copy = pltpu.make_async_copy(
        spare, keep_ref.at[EARLY_UNITS[1] * C : EARLY], out_sems.at[8]
    )

    @pl.when(core_ref[0] == 1)
    def keep_spare():
        spare_copy.start()

    @pl.when(core_ref[0] != 1)
    def give_spare():
        pltpu.make_async_copy(
            spare, give_ref.at[EARLY_UNITS[1] * C : EARLY], out_sems.at[8]
        ).start()

    masks = tile_masks()
    order = order_matrix()
    rows = mm(order, rows_ref[...].reshape(N, 1024))
    x1 = rows[:, 0:C]
    side_ref[...] = rows[:, C:].astype(BF16)
    normed, inverse = norm(x1)
    n2 = normed.astype(BF16)
    fetched[0].wait()
    qkv_ref[...] = mm(n2, wqkv_ref[...]).astype(BF16)

    lane = lax.broadcasted_iota(jnp.int32, (1, 256), 1)
    lane_head = jnp.where(lane < 3 * POINTS, (lane % POINTS) // P_SIZE, lane - 3 * POINTS)
    raw = jnp.zeros((1, 256), F32)
    for h in range(H):
        raw = jnp.where((lane < 3 * POINTS) & (lane_head == h), weight_ref[h], raw)
    soft = jnp.maximum(raw, 0.0) + jnp.log(1.0 + jnp.exp(-jnp.abs(raw)))
    strength = jnp.where(lane < 3 * POINTS, soft * STRENGTH, 0.0)
    head_masks = [jnp.where(lane_head == h, 1.0, 0.0).astype(BF16) for h in range(H)]

    for copy in fetched[1:4]:
        copy.wait()
    turned = mm(side_ref[:, C : C + 128], turn_ref[...])
    turns = [turned[:, b * 256 : (b + 1) * 256] for b in range(3)]
    local = mt(n2, wrep_ref[...])
    placed = []
    for c in range(2):
        total = turned[:, 768:1024]
        for b in range(3):
            total = total + turns[b] * local[:, (3 * c + b) * 256 : (3 * c + b + 1) * 256]
        placed.append(total)
    gq = placed[0]
    gk_bf = placed[1].astype(BF16)
    gk = gk_bf.astype(F32)
    heads = heads_ref[...]
    own = sum(mt(part, heads) for part in split_three(gq * gq * (0.5 * strength)))
    other = sum(mt(heads, part) for part in split_three(gk * gk * (0.5 * strength)))
    q_high, q_low = split_two(gq * strength)
    ones = (lane >= 3 * POINTS) & (lane < 3 * POINTS + 16)
    keys_one = jnp.where(ones, 1.0, gk).astype(BF16)
    queries_one = jnp.where(ones, 1.0, gq).astype(BF16)
    two_keys = jnp.concatenate([gk_bf, gk_bf], axis=1)
    count = side_ref[:, C + 128 : C + 256].astype(F32)
    near = count > 0.0

    for g in range(3):
        q = qkv_ref[:, g * 128 : (g + 1) * 128]
        k = qkv_ref[:, C + g * 128 : C + (g + 1) * 128]
        v = qkv_ref[:, 2 * C + g * 128 : 2 * C + (g + 1) * 128]
        for m in range(4):
            h = 4 * g + m
            at = slice(h * 128, (h + 1) * 128)
            direct = mt(q * masks[m], k) * (SCALE * math.sqrt(0.5))
            cross = mt(
                jnp.concatenate([q_high * head_masks[h], q_low * head_masks[h]], axis=1), two_keys
            )
            spot = cross - own[:, h : h + 1] - other[h : h + 1, :]
            point_ref[:, at] = spot
            logits = jnp.where(near, direct + spot, -1e30)
            raised = jnp.exp(logits - jnp.max(logits, axis=-1, keepdims=True)) * count
            shares = raised / jnp.sum(raised, axis=-1, keepdims=True)
            shares_ref[:, at] = shares
            prow_ref[:, at] = shares.astype(BF16)
            pcol_ref[at, :] = shares.astype(BF16)
            keys_ref[at, :] = keys_one * head_masks[h]
            queries_ref[at, :] = queries_one * head_masks[h]
        mixed = mm(prow_ref[:, g * 512 : (g + 1) * 512], masked_stack(v, masks))
        mix_ref[:, g * 128 : (g + 1) * 128] = mixed.astype(BF16)

    for copy in fetched[4:7]:
        copy.wait()
    cot = side_ref[:, 0:C]
    x2 = (x1 + mm(mix_ref[...], wout_ref[...])).astype(BF16).astype(F32)
    normed2, inverse2 = norm(x2)
    n3 = normed2.astype(BF16)
    u = mm(n3, wup_ref[...])
    root = math.sqrt(2.0 / math.pi)
    bent = jnp.tanh(root * (u + 0.044715 * u * u * u))
    hidden = (0.5 * u * (1.0 + bent)).astype(BF16)
    slope = 0.5 * (1.0 + bent) + 0.5 * u * (1.0 - bent * bent) * root * (
        1.0 + 3.0 * 0.044715 * u * u
    )
    updated = (x2 + mm(hidden, wdown_ref[...])).astype(BF16)
    put("down", tm(hidden, cot))
    dhidden = mt(cot, wdown_ref[...]).astype(BF16).astype(F32)
    du = (dhidden * slope).astype(BF16)
    put("up", tm(n3, du))
    dn3 = mt(du, wup_ref[...]).astype(BF16).astype(F32)
    dx2 = (cot.astype(F32) + norm_pull(dn3, normed2, inverse2).astype(BF16).astype(F32)).astype(
        BF16
    )
    dmix = mt(dx2, wout_ref[...]).astype(BF16)
    put("ipa_out", tm(mix_ref[...], dx2))

    gains = []
    for g in range(3):
        q = qkv_ref[:, g * 128 : (g + 1) * 128]
        k = qkv_ref[:, C + g * 128 : C + (g + 1) * 128]
        v = qkv_ref[:, 2 * C + g * 128 : 2 * C + (g + 1) * 128]
        dm = dmix[:, g * 128 : (g + 1) * 128]
        for m in range(4):
            h = 4 * g + m
            at = slice(h * 128, (h + 1) * 128)
            shares = shares_ref[:, at]
            dshares = mt(dm * masks[m], v)
            dlogit = shares * (dshares - jnp.sum(shares * dshares, axis=-1, keepdims=True))
            gains.append(jnp.sum(dlogit * point_ref[:, at], axis=0, keepdims=True))
            drow_ref[:, at] = dlogit.astype(BF16)
            dcol_ref[at, :] = dlogit.astype(BF16)
        group = slice(g * 512, (g + 1) * 512)
        dq = mm(drow_ref[:, group], masked_stack(k, masks)) * (SCALE * math.sqrt(0.5))
        dk = tm(dcol_ref[group, :], masked_stack(q, masks)) * (SCALE * math.sqrt(0.5))
        dv = tm(pcol_ref[group, :], masked_stack(dm, masks))
        dqkv_ref[:, g * 128 : (g + 1) * 128] = dq.astype(BF16)
        dqkv_ref[:, C + g * 128 : C + (g + 1) * 128] = dk.astype(BF16)
        dqkv_ref[:, 2 * C + g * 128 : 2 * C + (g + 1) * 128] = dv.astype(BF16)

    lane128 = lax.broadcasted_iota(jnp.int32, (1, 128), 1)
    gain = jnp.zeros((1, 128), F32)
    raw_row = jnp.zeros((1, 128), F32)
    for h in range(H):
        here = lane128 == h
        gain = jnp.where(here, jnp.sum(gains[h], axis=1, keepdims=True), gain)
        raw_row = jnp.where(here, weight_ref[h], raw_row)
    soft_row = jnp.maximum(raw_row, 0.0) + jnp.log(1.0 + jnp.exp(-jnp.abs(raw_row)))
    gain = gain / ((1.0 + jnp.exp(-raw_row)) * soft_row)

    for copy in fetched[7:10]:
        copy.wait()
    from_keys = mm(drow_ref[...], keys_ref[...])
    from_queries = tm(dcol_ref[...], queries_ref[...])
    spread = spread_ref[...]
    own_sum = sum(mm(part, spread) for part in split_two(from_keys[:, 128:256]))
    other_sum = sum(mm(part, spread) for part in split_two(from_queries[:, 128:256]))
    dgq = strength * (from_keys - gq * own_sum)
    dgk = (strength * (from_queries - gk * other_sum)).astype(BF16).astype(F32)
    for b in range(3):
        dlocal_ref[:, b * 256 : (b + 1) * 256] = (turns[b] * dgq).astype(BF16)
        dlocal_ref[:, (3 + b) * 256 : (4 + b) * 256] = (turns[b] * dgk).astype(BF16)
    dpoints = mm(dlocal_ref[...], gather_ref[...]).astype(BF16)
    dqkv = dqkv_ref[...]
    put("ipa_qkv", tm(n2, dqkv))
    gpts = tm(dpoints, n2)
    spare_row = lax.broadcasted_iota(jnp.int32, (C, 128), 0) == GAIN_ROW
    first = gpts[:, 0:128] + jnp.where(spare_row, gain, 0.0)
    put("ipa_points", jnp.concatenate([first, gpts[:, 128:]], axis=1))
    dn2 = (mt(dqkv, wqkv_ref[...]) + mm(dpoints[:, 0 : 6 * POINTS], wpts_ref[...])).astype(BF16).astype(F32)
    dx1 = (dx2.astype(F32) + norm_pull(dn2, normed, inverse).astype(BF16).astype(F32)).astype(BF16)
    back = jnp.concatenate([dx1, updated, jnp.zeros((N, 256), BF16)], axis=1)
    back_ref[...] = tm(order, back).astype(BF16).reshape(N, 8, 128)
    for copy in leaving + [spare_copy]:
        copy.wait()


def like(shape, dtype):
    return jax.ShapeDtypeStruct(shape, dtype)


def call_pack_rows(tokens, cotangent, rigid):
    frames, residues, _ = tokens.shape
    return pl.pallas_call(
        pack_rows,
        out_shape=like((residues, frames, 2 * C + 128), BF16),
        compiler_params=limit(60),
        name="pack_rows",
    )(tokens, cotangent, rigid)


def call_time_forward(place, neighbors, rows, w_qkv, w_out):
    return pl.pallas_call(
        time_forward,
        in_specs=[SMEM, SMEM, VMEM, VMEM, VMEM],
        out_shape=(
            like((N, 8, 128), BF16), like((N, 3 * C), BF16), like((N, H * N), BF16),
            like((N, C), BF16),
        ),
        compiler_params=limit(60),
        name="time_forward",
    )(place, neighbors, rows, w_qkv, w_out)


def call_time_backward(core, back, rows, qkv, shares, mix, w_qkv, w_out):
    return pl.pallas_call(
        time_backward,
        in_specs=[SMEM] + [VMEM] * 7,
        out_shape=(like((N, 2 * C), BF16), like((LATE, 128), BF16), like((LATE, 128), BF16)),
        scratch_shapes=[
            pltpu.VMEM((N, 3 * C), BF16), pltpu.VMEM((4 * N, N), BF16), pltpu.VMEM((4 * N, N), BF16),
        ],
        compiler_params=limit(20),
        name="time_backward",
    )(core, back, rows, qkv, shares, mix, w_qkv, w_out)


def call_point_attention(core, weight, rows, w_qkv, w_pts, w_rep, w_out, w_up, w_down):
    heads, turn, spread, gather = selectors()
    sources = [w_qkv, turn, w_rep, heads, w_out, w_up, w_down, spread, gather, w_pts]
    return pl.pallas_call(
        point_attention,
        in_specs=[SMEM, SMEM, VMEM] + [HBM] * len(sources),
        out_specs=(VMEM, HBM, HBM),
        out_shape=(like((N, 8, 128), BF16), like((EARLY, 128), BF16), like((EARLY, 128), BF16)),
        scratch_shapes=[
            pltpu.VMEM((N, 3 * C), BF16), pltpu.VMEM((N, C), BF16),
            pltpu.VMEM((N, H * N), F32), pltpu.VMEM((N, H * N), F32),
            pltpu.VMEM((N, H * N), BF16), pltpu.VMEM((H * N, N), BF16),
            pltpu.VMEM((N, H * N), BF16), pltpu.VMEM((H * N, N), BF16),
            pltpu.VMEM((N, 3 * C), BF16), pltpu.VMEM((N, 6 * 256), BF16),
            pltpu.VMEM((H * N, 256), BF16), pltpu.VMEM((H * N, 256), BF16),
            pltpu.VMEM((N, 640), BF16), pltpu.VMEM((2, EARLY, 128), BF16),
            *[pltpu.VMEM(source.shape, BF16) for source in sources],
            pltpu.SemaphoreType.DMA((len(sources),)), pltpu.SemaphoreType.DMA((9,)),
        ],
        compiler_params=limit(60),
        name="point_attention",
    )(core, weight, rows, *sources)


def add_early(side_ref, keep_ref, got_ref, mine_ref, give_ref, one_ref, two_ref, sems):
    part = EARLY // 2
    steps = []
    for step, target in enumerate((give_ref, mine_ref)):
        start = pl.multiple_of((side_ref[0] if step else 1 - side_ref[0]) * part, part)
        span = slice(step * part, (step + 1) * part)
        steps.append(
            (
                pltpu.make_async_copy(keep_ref.at[pl.ds(start, part)], one_ref.at[span], sems.at[3 * step]),
                pltpu.make_async_copy(got_ref.at[pl.ds(start, part)], two_ref.at[span], sems.at[3 * step + 1]),
                pltpu.make_async_copy(one_ref.at[span], target, sems.at[3 * step + 2]),
            )
        )
    for first, second, _ in steps:
        first.start()
        second.start()
    for step, (first, second, out) in enumerate(steps):
        first.wait()
        second.wait()
        span = slice(step * part, (step + 1) * part)
        summed = one_ref[span, :].astype(F32) + two_ref[span, :].astype(F32)
        one_ref[span, :] = summed.astype(BF16)
        out.start()
    for _, _, out in steps:
        out.wait()


def call_add_early(side, keep, got):
    part = like((EARLY // 2, 128), BF16)
    return pl.pallas_call(
        add_early,
        in_specs=[SMEM, HBM, HBM],
        out_specs=(HBM, HBM),
        out_shape=(part, part),
        scratch_shapes=[
            pltpu.VMEM((EARLY, 128), BF16), pltpu.VMEM((EARLY, 128), BF16),
            pltpu.SemaphoreType.DMA((6,)),
        ],
        compiler_params=limit(60),
        cost_estimate=pl.CostEstimate(flops=EARLY * 128, bytes_accessed=EARLY * 128 * 6, transcendentals=0),
        name="add_early",
    )(side, keep, got)


def add_late(side_ref, keep_ref, got_ref, mine_ref, give_ref):
    part = LATE // 2
    for ref, index in ((mine_ref, side_ref[0]), (give_ref, 1 - side_ref[0])):
        span = pl.ds(pl.multiple_of(index * part, part), part)
        summed = keep_ref[span, :].astype(F32) + got_ref[span, :].astype(F32)
        ref[...] = summed.astype(BF16)


def call_add_late(side, keep, got):
    part = like((LATE // 2, 128), BF16)
    return pl.pallas_call(
        add_late,
        in_specs=[SMEM, VMEM, VMEM],
        out_shape=(part, part),
        compiler_params=limit(8),
        name="add_late",
    )(side, keep, got)


def add_pairs(early_ref, got_early_ref, late_ref, got_late_ref, total_ref):
    early, late = EARLY // 2, LATE // 2
    summed = early_ref[...].astype(F32) + got_early_ref[...].astype(F32)
    total_ref[0:early, :] = summed.astype(BF16)
    summed = late_ref[...].astype(F32) + got_late_ref[...].astype(F32)
    total_ref[early : early + late, :] = summed.astype(BF16)
    total_ref[early + late :, :] = jnp.zeros((QUARTER - early - late, 128), BF16)


def call_add_pairs(*parts):
    return pl.pallas_call(
        add_pairs, out_shape=like((QUARTER, 128), BF16), compiler_params=limit(12), name="add_pairs"
    )(*parts)


def add_parts(parts_ref, copies_ref):
    count = parts_ref.shape[0]
    total = parts_ref[0].astype(F32)
    for k in range(1, count):
        total = total + parts_ref[k].astype(F32)
    total = total.astype(BF16)
    for k in range(copies_ref.shape[0]):
        copies_ref[k] = total


def call_add_parts(parts):
    return pl.pallas_call(
        add_parts, out_shape=like((2 * SHARERS, *parts.shape[1:]), BF16), compiler_params=limit(12),
        name="add_parts",
    )(parts)


def final_spot(late, at):
    unit = (at - EARLY if late else at) // C
    room = (LATE if late else EARLY) // (2 * C)
    return unit // room, (EARLY // 2 if late else 0) + (unit % room) * C


def segments(row):
    begin = row
    while begin < row + C:
        chunk, low = divmod(begin, CHUNK)
        size = min(CHUNK - low, row + C - begin)
        yield chunk, low, size, begin - row
        begin += size


def unpack_half(own, core_ref, parts_ref, out_refs, held_ref, stage_ref, gain_ref, in_sems, out_sems):
    for half in range(2):

        @pl.when((core_ref[0] == half) == own)
        def run(half=half):
            for q in range(2):
                for line in range(8):
                    for high in range(2):
                        source = (
                            parts_ref.at[line, high, q] if half == 0 else parts_ref.at[line, high, :, q]
                        )
                        target = held_ref.at[q, pl.ds((line * 2 + high) * 2, 2)]
                        pltpu.make_async_copy(source, target, in_sems.at[q]).start()
            leaving = []
            for q in range(2):
                pltpu.make_async_copy(held_ref.at[q], held_ref.at[q], in_sems.at[q]).wait()
                for k, name in enumerate(PIECES):
                    tiles = PIECES[name][1] // 128
                    for unit, (owner, at) in enumerate(UNITS[name]):
                        quarter, row = final_spot(name.startswith("time"), at)
                        if owner != half or quarter != q:
                            continue
                        slot = len(leaving)
                        for chunk, low, size, to in segments(row):
                            stage_ref[slot, to : to + size, :] = held_ref[
                                q, chunk, low : low + size, :
                            ].astype(F32)
                        down, across = (unit // tiles) * C, (unit % tiles) * 128
                        rows = GAIN_ROW if name == "ipa_points" else C
                        if name == "ipa_points" and across == 0:
                            gain_ref[...] = stage_ref[slot, GAIN_ROW : GAIN_ROW + 1, :]
                        leaving.append(
                            pltpu.make_async_copy(
                                stage_ref.at[slot, 0:rows],
                                out_refs[k].at[down : down + rows, across : across + 128],
                                out_sems.at[slot],
                            )
                        )
                        leaving[-1].start()
            for copy in leaving:
                copy.wait()


def unpack_own(core_ref, parts_ref, *refs):
    gain_ref = refs[7]
    gain_ref[...] = jnp.zeros((1, 128), F32)
    unpack_half(True, core_ref, parts_ref, refs[:7], refs[8], refs[9], gain_ref, refs[10], refs[11])


def unpack_other(core_ref, parts_ref, gain_own_ref, ended_ref, *refs):
    out_refs, gain_ref, output_ref, token_ref = refs[7:14], refs[14], refs[15], refs[16]
    held_ref, stage_ref, part_ref, in_sems, out_sems = refs[17:]
    residues, frames, _ = ended_ref.shape
    ended = mm(order_matrix(), ended_ref[...].reshape(N, 2 * C)).astype(BF16)
    token_ref[...] = ended[:, 0:C].reshape(frames, residues, C)
    output_ref[...] = ended[:, C:].reshape(frames, residues, C)
    part_ref[...] = jnp.zeros((1, 128), F32)
    unpack_half(False, core_ref, parts_ref, out_refs, held_ref, stage_ref, part_ref, in_sems, out_sems)
    gain = gain_own_ref[...] + part_ref[...]
    lane = lax.broadcasted_iota(jnp.int32, (1, 128), 1)
    for h in range(H):
        gain_ref[h] = jnp.sum(jnp.where(lane == h, gain, 0.0))


OUTS = [
    (GAIN_ROW if name == "ipa_points" else rows, columns) for name, (rows, columns) in PIECES.items()
]
UNPACK_SCRATCH = [
    pltpu.VMEM((2, SHARERS, CHUNK, 128), BF16),
    pltpu.VMEM((EARLY_UNITS[0] + LATE_UNITS[0], C, 128), F32),
]
UNPACK_SEMS = [
    pltpu.SemaphoreType.DMA((2,)), pltpu.SemaphoreType.DMA((EARLY_UNITS[0] + LATE_UNITS[0],)),
]


def call_unpack_own(core, parts):
    return pl.pallas_call(
        unpack_own,
        in_specs=[SMEM, HBM],
        out_specs=(*[HBM] * 7, VMEM),
        out_shape=(*[like(shape, F32) for shape in OUTS], like((1, 128), F32)),
        scratch_shapes=UNPACK_SCRATCH + UNPACK_SEMS,
        compiler_params=limit(20),
        cost_estimate=pl.CostEstimate(flops=0, bytes_accessed=8 * MEGA, transcendentals=0),
        name="unpack_own",
    )(core, parts)


def call_unpack_other(core, parts, gain, ended, grads):
    residues, frames, _ = ended.shape
    rows = like((frames, residues, C), BF16)
    return pl.pallas_call(
        unpack_other,
        in_specs=[SMEM, HBM, VMEM, VMEM] + [HBM] * 7,
        out_specs=(*[HBM] * 7, SMEM, VMEM, VMEM),
        out_shape=(*[like(shape, F32) for shape in OUTS], like((H,), F32), rows, rows),
        scratch_shapes=UNPACK_SCRATCH + [pltpu.VMEM((1, 128), F32)] + UNPACK_SEMS,
        input_output_aliases={4 + k: k for k in range(7)},
        compiler_params=limit(20),
        name="unpack_other",
    )(core, parts, gain, ended, *grads)


def repeat_points(weight):
    parts = weight.reshape(6, POINTS, C)
    tripled = jnp.concatenate([parts, parts, parts], axis=1)
    return jnp.pad(tripled, ((0, 0), (0, 256 - 3 * POINTS), (0, 0))).reshape(6 * 256, C)


def swap_rows(rows, axes):
    return lax.all_to_all(rows, axes, split_axis=0, concat_axis=0, tiled=True)


def body(
    tokens, rigid_frames, neighbors, w_time_qkv, w_time_out, w_ipa_qkv, w_ipa_points,
    point_weight, w_ipa_out, w_up, w_down, cotangent,
):
    frames, residues = tokens.shape[:2]
    place = lax.axis_index(("line", "core")).astype(jnp.int32).reshape(1)
    core = lax.axis_index("core").astype(jnp.int32).reshape(1)
    place_res = lax.axis_index("res").astype(jnp.int32)
    side = jnp.where(core == 0, (place_res >> 1) & 1, place_res & 1)
    swap = [(0, 1), (1, 0)]
    points = w_ipa_points.T
    rows = swap_rows(call_pack_rows(tokens, cotangent, rigid_frames), ("line", "core"))
    rows = rows.reshape(N, 2 * C + 128)
    sent, qkv, shares, mix = call_time_forward(place, neighbors, rows, w_time_qkv, w_time_out)
    back, keep_early, give_early = call_point_attention(
        core, point_weight, swap_rows(sent, EVERYONE), w_ipa_qkv, points, repeat_points(points),
        w_ipa_out, w_up, w_down,
    )
    got_early = lax.ppermute(give_early, "core", swap)
    mine_early, give_early = call_add_early(side, keep_early, got_early)
    got_early = lax.ppermute(give_early, EVERYONE, PAIRS)
    ended, keep_late, give_late = call_time_backward(
        core, swap_rows(back, EVERYONE), rows, qkv, shares, mix, w_time_qkv, w_time_out
    )
    got_late = lax.ppermute(give_late, "core", swap)
    mine_late, give_late = call_add_late(side, keep_late, got_late)
    got_late = lax.ppermute(give_late, EVERYONE, PAIRS)
    total = call_add_pairs(mine_early, got_early, mine_late, got_late)
    parts = lax.all_to_all(
        total.reshape(SHARERS, CHUNK, 128), EVERYONE, split_axis=0, concat_axis=0, tiled=True,
        axis_index_groups=GROUPS,
    )
    own = swap_rows(call_add_parts(parts), ("line", "res")).reshape(8, 2, 2, 2, CHUNK, 128)
    other = lax.ppermute(own, "core", swap)
    ended = swap_rows(ended.reshape(residues, frames, 2 * C), ("line", "core"))
    *grads, gain = call_unpack_own(core, own)
    *grads, gain, output, token_grad = call_unpack_other(core, other, gain, ended, grads)
    grads = dict(zip(PIECES, grads))
    return (
        output, token_grad, grads["time_qkv"], grads["time_out"], grads["ipa_qkv"],
        grads["ipa_points"].T, gain, grads["ipa_out"], grads["up"], grads["down"],
    )


def solution(mesh):
    devices = mesh.devices
    split = Mesh(
        devices.reshape(devices.shape[0] // 2, 2, devices.shape[1]), ("line", "core", "res")
    )
    frame = ("line", "core")
    rows = P(frame, "res", None)
    placed = (rows, P(None, frame, "res"), P("res", None)) + (P(),) * 8 + (rows,)
    return jax.shard_map(
        body,
        mesh=split,
        in_specs=placed,
        out_specs=(rows, rows) + (P(),) * 8,
        check_vma=False,
    )
```

```python
import math

import jax
import jax.numpy as jnp
import numpy as np
from jax import lax
from jax.experimental import pallas as pl
from jax.experimental.pallas import tpu as pltpu
from jax.sharding import Mesh, PartitionSpec as P

H = 12
P_SIZE = 4
NB = 32
C = 384
HID = 1536
N = 128
POINTS = H * P_SIZE
EPSILON = 1e-05
SCALE = 1.0 / math.sqrt(C // H)
STRENGTH = math.sqrt(2.0 / (9.0 * P_SIZE)) * math.sqrt(0.5)
F32 = jnp.float32
BF16 = jnp.bfloat16
EVERYONE = ("line", "core", "res")
SHARERS = 32
GAIN_ROW = 6 * POINTS

PIECES = {
    "up": (C, HID),
    "ipa_out": (C, C),
    "ipa_points": (C, C),
    "ipa_qkv": (C, 3 * C),
    "down": (HID, C),
    "time_qkv": (C, 3 * C),
    "time_out": (C, C),
}
EARLY_UNITS = [20, 19]
LATE_UNITS = [6, 6]
EARLY = max(EARLY_UNITS) * C
LATE = max(LATE_UNITS) * C
QUARTER = -(-(EARLY + LATE) // (2 * SHARERS * 16)) * SHARERS * 16
CHUNK = QUARTER // SHARERS


def ring_groups():
    bits = (2, 1)
    rings, groups = ([], []), [[], [], [], []]
    for line in range(8):
        for core in range(2):
            for res in range(8):
                place = (line * 2 + core) * 8 + res
                groups[2 * core + bool(res & bits[core])].append(place)
                for ring, step in zip(rings, (1, 3)):
                    x, y = res // 2, line % 2 * 2 + res % 2
                    if core == 0:
                        x = (x + step) % 4
                    else:
                        y = (y + step) % 4
                    there = ((line // 2 * 2 + y // 2) * 2 + core) * 8 + x * 2 + y % 2
                    ring.append((place, there))
    return rings, groups


RINGS, GROUPS = ring_groups()


def place_units():
    units, taken = {}, {True: [0, 0], False: [0, 0]}
    for name, (rows, columns) in PIECES.items():
        late = name.startswith("time")
        room = LATE_UNITS if late else EARLY_UNITS
        units[name] = []
        for _ in range(rows * columns // (C * 128)):
            half = 0 if taken[late][0] < room[0] else 1
            units[name].append((half, (EARLY if late else 0) + taken[late][half] * C))
            taken[late][half] += 1
    return units


UNITS = place_units()


def halves(core, keep_ref, give_ref):
    def put(name, value):
        tiles = value.shape[1] // 128
        base = EARLY if name.startswith("time") else 0
        pieces = [[], []]
        for unit, (half, at) in enumerate(UNITS[name]):
            down, across = (unit // tiles) * C, (unit % tiles) * 128
            part = value[down : down + C, across : across + 128].astype(BF16)
            pieces[half].append((at - base, part))

        for half in range(2):
            for ref, mine in ((keep_ref, True), (give_ref, False)):
                @pl.when((core == half) == mine)
                def store(ref=ref, parts=pieces[half]):
                    for at, part in parts:
                        ref[at : at + C, :] = part

    return put


def staged(core, stage_ref, keep_ref, give_ref, sems):
    waits = []

    def put(name, value):
        tiles = value.shape[1] // 128
        spans = {}
        for unit, (half, at) in enumerate(UNITS[name]):
            down, across = (unit // tiles) * C, (unit % tiles) * 128
            stage_ref[half, at : at + C, :] = value[down : down + C, across : across + 128].astype(
                BF16
            )
            low, _ = spans.get(half, (at, at))
            spans[half] = (low, at + C)
        for half, (low, high) in spans.items():
            sem = sems.at[len(waits)]
            source = stage_ref.at[half, low:high]

            @pl.when(core == half)
            def keep(source=source, low=low, high=high, sem=sem):
                pltpu.make_async_copy(source, keep_ref.at[low:high], sem).start()

            @pl.when(core != half)
            def give(source=source, low=low, high=high, sem=sem):
                pltpu.make_async_copy(source, give_ref.at[low:high], sem).start()

            waits.append(pltpu.make_async_copy(source, keep_ref.at[low:high], sem))

    return put, waits


MEGA = 1024 * 1024


def limit(megabytes):
    return pltpu.CompilerParams(vmem_limit_bytes=megabytes * MEGA)


SMEM = pl.BlockSpec(memory_space=pltpu.SMEM)
VMEM = pl.BlockSpec(memory_space=pltpu.VMEM)
HBM = pl.BlockSpec(memory_space=pltpu.HBM)


def mm(left, right):
    return lax.dot_general(left, right, (((1,), (0,)), ((), ())), preferred_element_type=F32)


def mt(left, right):
    return lax.dot_general(left, right, (((1,), (1,)), ((), ())), preferred_element_type=F32)


def tm(left, right):
    return lax.dot_general(left, right, (((0,), (0,)), ((), ())), preferred_element_type=F32)


def norm(values):
    centered = values - jnp.mean(values, axis=-1, keepdims=True)
    inverse = lax.rsqrt(jnp.mean(centered * centered, axis=-1, keepdims=True) + EPSILON)
    return centered * inverse, inverse


def norm_pull(cotangent, normed, inverse):
    return inverse * (
        cotangent
        - jnp.mean(cotangent, axis=-1, keepdims=True)
        - normed * jnp.mean(cotangent * normed, axis=-1, keepdims=True)
    )


def split_two(values):
    high = values.astype(BF16)
    return high, (values - high.astype(F32)).astype(BF16)


def split_three(values):
    high, rest = values.astype(BF16), None
    rest = values - high.astype(F32)
    middle = rest.astype(BF16)
    return high, middle, (rest - middle.astype(F32)).astype(BF16)


def order_matrix():
    row = lax.broadcasted_iota(jnp.int32, (N, N), 0)
    col = lax.broadcasted_iota(jnp.int32, (N, N), 1)
    return jnp.where((col // 8 == row % 16) & (col % 8 == row // 16), 1.0, 0.0).astype(BF16)


def tile_masks():
    lane = lax.broadcasted_iota(jnp.int32, (1, 128), 1)
    return [jnp.where(lane // 32 == m, 1.0, 0.0).astype(BF16) for m in range(4)]


def masked_stack(tile, masks):
    return jnp.concatenate([tile * mask for mask in masks], axis=0)


def pack_rows(tokens_ref, cotangent_ref, rigid_ref, packed_ref):
    frames, residues, _ = tokens_ref.shape
    order = order_matrix()
    for at, ref in ((0, tokens_ref), (C, cotangent_ref)):
        turned = tm(order, ref[...].reshape(N, C))
        packed_ref[:, :, at : at + C] = turned.reshape(residues, frames, C).astype(BF16)
    row = lax.broadcasted_iota(jnp.int32, (N, residues), 0)
    col = lax.broadcasted_iota(jnp.int32, (N, residues), 1)
    rigid = jnp.zeros((N, 12), F32)
    for f in range(frames):
        pick = jnp.where(row == col * frames + f, 1.0, 0.0).astype(BF16)
        rigid = rigid + mt(pick, rigid_ref[:, f, :])
    packed_ref[:, :, 2 * C :] = jnp.zeros((residues, frames, 128), BF16)
    packed_ref[:, :, 2 * C : 2 * C + 12] = rigid.reshape(residues, frames, 12).astype(BF16)


def time_forward(
    place_ref, neighbors_ref, rows_ref, wqkv_ref, wout_ref, sent_ref, qkv_ref, shares_ref, mix_ref
):
    x = rows_ref[:, 0:C].astype(F32)
    normed, _ = norm(x)
    qkv_ref[...] = mm(normed.astype(BF16), wqkv_ref[...]).astype(BF16)
    masks = tile_masks()
    for g in range(3):
        q = qkv_ref[:, g * 128 : (g + 1) * 128]
        k = qkv_ref[:, C + g * 128 : C + (g + 1) * 128]
        v = qkv_ref[:, 2 * C + g * 128 : 2 * C + (g + 1) * 128]
        for m in range(4):
            h = 4 * g + m
            scores = mt(q * masks[m], k) * SCALE
            raised = jnp.exp(scores - jnp.max(scores, axis=-1, keepdims=True))
            shares = raised / jnp.sum(raised, axis=-1, keepdims=True)
            shares_ref[:, h * 128 : (h + 1) * 128] = shares.astype(BF16)
        mixed = mm(shares_ref[:, g * 512 : (g + 1) * 512], masked_stack(v, masks))
        mix_ref[:, g * 128 : (g + 1) * 128] = mixed.astype(BF16)
    x1 = (x + mm(mix_ref[...], wout_ref[...])).astype(BF16)
    lane = lax.broadcasted_iota(jnp.int32, (N, 128), 1)
    count = jnp.zeros((N, 128), F32)
    for n in range(NB):
        count = count + jnp.where(lane == neighbors_ref[place_ref[0], n], 1.0, 0.0)
    sent = jnp.concatenate([x1, rows_ref[:, C:], count.astype(BF16)], axis=1)
    sent_ref[...] = sent.reshape(N, 8, 128)


def time_backward(
    core_ref, back_ref, rows_ref, qkv_ref, shares_ref, mix_ref, wqkv_ref, wout_ref,
    sent_ref, keep_ref, give_ref, dqkv_ref, dcol_ref, pcol_ref,
):
    put = halves(core_ref[0], keep_ref, give_ref)
    back = back_ref[...].reshape(N, 1024)
    dx1 = back[:, 0:C]
    normed, inverse = norm(rows_ref[:, 0:C].astype(F32))
    dmix = mt(dx1, wout_ref[...]).astype(BF16)
    put("time_out", tm(mix_ref[...], dx1))
    masks = tile_masks()
    for g in range(3):
        q = qkv_ref[:, g * 128 : (g + 1) * 128]
        k = qkv_ref[:, C + g * 128 : C + (g + 1) * 128]
        v = qkv_ref[:, 2 * C + g * 128 : 2 * C + (g + 1) * 128]
        dm = dmix[:, g * 128 : (g + 1) * 128]
        rows = []
        for m in range(4):
            h = 4 * g + m
            kept = shares_ref[:, h * 128 : (h + 1) * 128]
            pcol_ref[m * 128 : (m + 1) * 128, :] = kept
            shares = kept.astype(F32)
            dshares = mt(dm * masks[m], v)
            inner = jnp.sum(shares * dshares, axis=-1, keepdims=True)
            dlogit = (shares * (dshares - inner) * SCALE).astype(BF16)
            dcol_ref[m * 128 : (m + 1) * 128, :] = dlogit
            rows.append(dlogit)
        dq = mm(jnp.concatenate(rows, axis=1), masked_stack(k, masks))
        dk = tm(dcol_ref[...], masked_stack(q, masks))
        dv = tm(pcol_ref[...], masked_stack(dm, masks))
        dqkv_ref[:, g * 128 : (g + 1) * 128] = dq.astype(BF16)
        dqkv_ref[:, C + g * 128 : C + (g + 1) * 128] = dk.astype(BF16)
        dqkv_ref[:, 2 * C + g * 128 : 2 * C + (g + 1) * 128] = dv.astype(BF16)
    put("time_qkv", tm(normed.astype(BF16), dqkv_ref[...]))
    dnormed = mt(dqkv_ref[...], wqkv_ref[...]).astype(BF16).astype(F32)
    pulled = norm_pull(dnormed, normed, inverse).astype(BF16).astype(F32)
    sent_ref[:, 0:C] = (dx1.astype(F32) + pulled).astype(BF16)
    sent_ref[:, C : 2 * C] = back[:, C : 2 * C]


def selectors():
    lane = np.arange(256)
    inside = lane < 3 * POINTS
    head = np.where(inside, (lane % POINTS) // P_SIZE, -1)
    heads = (head[None, :] == np.arange(16)[:, None]).astype(np.float32)
    turn = np.zeros((128, 4 * 256), np.float32)
    for a in range(3):
        at = a * POINTS + np.arange(POINTS)
        for b in range(3):
            turn[3 * a + b, b * 256 + at] = 1.0
        turn[9 + a, 3 * 256 + at] = 1.0
    spread = np.zeros((128, 256), np.float32)
    spread[16:32] = heads
    gather = np.zeros((6 * 256, C), np.float32)
    for c in range(2):
        for b in range(3):
            for a in range(3):
                for p in range(POINTS):
                    gather[(3 * c + b) * 256 + a * POINTS + p, (3 * c + b) * POINTS + p] = 1.0
    return [jnp.asarray(item, BF16) for item in (heads, turn, spread, gather)]


def point_attention(
    core_ref, weight_ref, rows_ref, *refs
):
    sources, refs = refs[:10], refs[10:]
    back_ref, keep_ref, give_ref = refs[:3]
    (
        qkv_ref, mix_ref, shares_ref, point_ref, prow_ref, pcol_ref, drow_ref, dcol_ref,
        dqkv_ref, dlocal_ref, keys_ref, queries_ref, side_ref, stage_ref,
    ) = refs[3:17]
    held, sems, out_sems = refs[17:27], refs[27], refs[28]
    fetched = [
        pltpu.make_async_copy(source, target, sems.at[k])
        for k, (source, target) in enumerate(zip(sources, held))
    ]
    for copy in fetched:
        copy.start()
    (
        wqkv_ref, turn_ref, wrep_ref, heads_ref, wout_ref, wup_ref, wdown_ref, spread_ref,
        gather_ref, wpts_ref,
    ) = held
    put, leaving = staged(core_ref[0], stage_ref, keep_ref, give_ref, out_sems)
    stage_ref[1, EARLY_UNITS[1] * C : EARLY, :] = jnp.zeros((EARLY - EARLY_UNITS[1] * C, 128), BF16)
    spare = stage_ref.at[1, EARLY_UNITS[1] * C : EARLY]
    spare_copy = pltpu.make_async_copy(
        spare, keep_ref.at[EARLY_UNITS[1] * C : EARLY], out_sems.at[8]
    )

    @pl.when(core_ref[0] == 1)
    def keep_spare():
        spare_copy.start()

    @pl.when(core_ref[0] != 1)
    def give_spare():
        pltpu.make_async_copy(
            spare, give_ref.at[EARLY_UNITS[1] * C : EARLY], out_sems.at[8]
        ).start()

    masks = tile_masks()
    order = order_matrix()
    rows = mm(order, rows_ref[...].reshape(N, 1024))
    x1 = rows[:, 0:C]
    side_ref[...] = rows[:, C:].astype(BF16)
    normed, inverse = norm(x1)
    n2 = normed.astype(BF16)
    fetched[0].wait()
    qkv_ref[...] = mm(n2, wqkv_ref[...]).astype(BF16)

    lane = lax.broadcasted_iota(jnp.int32, (1, 256), 1)
    lane_head = jnp.where(lane < 3 * POINTS, (lane % POINTS) // P_SIZE, lane - 3 * POINTS)
    raw = jnp.zeros((1, 256), F32)
    for h in range(H):
        raw = jnp.where((lane < 3 * POINTS) & (lane_head == h), weight_ref[h], raw)
    soft = jnp.maximum(raw, 0.0) + jnp.log(1.0 + jnp.exp(-jnp.abs(raw)))
    strength = jnp.where(lane < 3 * POINTS, soft * STRENGTH, 0.0)
    head_masks = [jnp.where(lane_head == h, 1.0, 0.0).astype(BF16) for h in range(H)]

    for copy in fetched[1:4]:
        copy.wait()
    turned = mm(side_ref[:, C : C + 128], turn_ref[...])
    turns = [turned[:, b * 256 : (b + 1) * 256] for b in range(3)]
    local = mt(n2, wrep_ref[...])
    placed = []
    for c in range(2):
        total = turned[:, 768:1024]
        for b in range(3):
            total = total + turns[b] * local[:, (3 * c + b) * 256 : (3 * c + b + 1) * 256]
        placed.append(total)
    gq = placed[0]
    gk_bf = placed[1].astype(BF16)
    gk = gk_bf.astype(F32)
    heads = heads_ref[...]
    own = sum(mt(part, heads) for part in split_three(gq * gq * (0.5 * strength)))
    other = sum(mt(heads, part) for part in split_three(gk * gk * (0.5 * strength)))
    q_high, q_low = split_two(gq * strength)
    ones = (lane >= 3 * POINTS) & (lane < 3 * POINTS + 16)
    keys_one = jnp.where(ones, 1.0, gk).astype(BF16)
    queries_one = jnp.where(ones, 1.0, gq).astype(BF16)
    two_keys = jnp.concatenate([gk_bf, gk_bf], axis=1)
    count = side_ref[:, C + 128 : C + 256].astype(F32)
    near = count > 0.0

    for g in range(3):
        q = qkv_ref[:, g * 128 : (g + 1) * 128]
        k = qkv_ref[:, C + g * 128 : C + (g + 1) * 128]
        v = qkv_ref[:, 2 * C + g * 128 : 2 * C + (g + 1) * 128]
        for m in range(4):
            h = 4 * g + m
            at = slice(h * 128, (h + 1) * 128)
            direct = mt(q * masks[m], k) * (SCALE * math.sqrt(0.5))
            cross = mt(
                jnp.concatenate([q_high * head_masks[h], q_low * head_masks[h]], axis=1), two_keys
            )
            spot = cross - own[:, h : h + 1] - other[h : h + 1, :]
            point_ref[:, at] = spot
            logits = jnp.where(near, direct + spot, -1e30)
            raised = jnp.exp(logits - jnp.max(logits, axis=-1, keepdims=True)) * count
            shares = raised / jnp.sum(raised, axis=-1, keepdims=True)
            shares_ref[:, at] = shares
            prow_ref[:, at] = shares.astype(BF16)
            pcol_ref[at, :] = shares.astype(BF16)
            keys_ref[at, :] = keys_one * head_masks[h]
            queries_ref[at, :] = queries_one * head_masks[h]
        mixed = mm(prow_ref[:, g * 512 : (g + 1) * 512], masked_stack(v, masks))
        mix_ref[:, g * 128 : (g + 1) * 128] = mixed.astype(BF16)

    for copy in fetched[4:7]:
        copy.wait()
    cot = side_ref[:, 0:C]
    x2 = (x1 + mm(mix_ref[...], wout_ref[...])).astype(BF16).astype(F32)
    normed2, inverse2 = norm(x2)
    n3 = normed2.astype(BF16)
    u = mm(n3, wup_ref[...])
    root = math.sqrt(2.0 / math.pi)
    bent = jnp.tanh(root * (u + 0.044715 * u * u * u))
    hidden = (0.5 * u * (1.0 + bent)).astype(BF16)
    slope = 0.5 * (1.0 + bent) + 0.5 * u * (1.0 - bent * bent) * root * (
        1.0 + 3.0 * 0.044715 * u * u
    )
    updated = (x2 + mm(hidden, wdown_ref[...])).astype(BF16)
    put("down", tm(hidden, cot))
    dhidden = mt(cot, wdown_ref[...]).astype(BF16).astype(F32)
    du = (dhidden * slope).astype(BF16)
    put("up", tm(n3, du))
    dn3 = mt(du, wup_ref[...]).astype(BF16).astype(F32)
    dx2 = (cot.astype(F32) + norm_pull(dn3, normed2, inverse2).astype(BF16).astype(F32)).astype(
        BF16
    )
    dmix = mt(dx2, wout_ref[...]).astype(BF16)
    put("ipa_out", tm(mix_ref[...], dx2))

    gains = []
    for g in range(3):
        q = qkv_ref[:, g * 128 : (g + 1) * 128]
        k = qkv_ref[:, C + g * 128 : C + (g + 1) * 128]
        v = qkv_ref[:, 2 * C + g * 128 : 2 * C + (g + 1) * 128]
        dm = dmix[:, g * 128 : (g + 1) * 128]
        for m in range(4):
            h = 4 * g + m
            at = slice(h * 128, (h + 1) * 128)
            shares = shares_ref[:, at]
            dshares = mt(dm * masks[m], v)
            dlogit = shares * (dshares - jnp.sum(shares * dshares, axis=-1, keepdims=True))
            gains.append(jnp.sum(dlogit * point_ref[:, at], axis=0, keepdims=True))
            drow_ref[:, at] = dlogit.astype(BF16)
            dcol_ref[at, :] = dlogit.astype(BF16)
        group = slice(g * 512, (g + 1) * 512)
        dq = mm(drow_ref[:, group], masked_stack(k, masks)) * (SCALE * math.sqrt(0.5))
        dk = tm(dcol_ref[group, :], masked_stack(q, masks)) * (SCALE * math.sqrt(0.5))
        dv = tm(pcol_ref[group, :], masked_stack(dm, masks))
        dqkv_ref[:, g * 128 : (g + 1) * 128] = dq.astype(BF16)
        dqkv_ref[:, C + g * 128 : C + (g + 1) * 128] = dk.astype(BF16)
        dqkv_ref[:, 2 * C + g * 128 : 2 * C + (g + 1) * 128] = dv.astype(BF16)

    lane128 = lax.broadcasted_iota(jnp.int32, (1, 128), 1)
    gain = jnp.zeros((1, 128), F32)
    raw_row = jnp.zeros((1, 128), F32)
    for h in range(H):
        here = lane128 == h
        gain = jnp.where(here, jnp.sum(gains[h], axis=1, keepdims=True), gain)
        raw_row = jnp.where(here, weight_ref[h], raw_row)
    soft_row = jnp.maximum(raw_row, 0.0) + jnp.log(1.0 + jnp.exp(-jnp.abs(raw_row)))
    gain = gain / ((1.0 + jnp.exp(-raw_row)) * soft_row)

    for copy in fetched[7:10]:
        copy.wait()
    from_keys = mm(drow_ref[...], keys_ref[...])
    from_queries = tm(dcol_ref[...], queries_ref[...])
    spread = spread_ref[...]
    own_sum = sum(mm(part, spread) for part in split_two(from_keys[:, 128:256]))
    other_sum = sum(mm(part, spread) for part in split_two(from_queries[:, 128:256]))
    dgq = strength * (from_keys - gq * own_sum)
    dgk = (strength * (from_queries - gk * other_sum)).astype(BF16).astype(F32)
    for b in range(3):
        dlocal_ref[:, b * 256 : (b + 1) * 256] = (turns[b] * dgq).astype(BF16)
        dlocal_ref[:, (3 + b) * 256 : (4 + b) * 256] = (turns[b] * dgk).astype(BF16)
    dpoints = mm(dlocal_ref[...], gather_ref[...]).astype(BF16)
    dqkv = dqkv_ref[...]
    put("ipa_qkv", tm(n2, dqkv))
    gpts = tm(dpoints, n2)
    spare_row = lax.broadcasted_iota(jnp.int32, (C, 128), 0) == GAIN_ROW
    first = gpts[:, 0:128] + jnp.where(spare_row, gain, 0.0)
    put("ipa_points", jnp.concatenate([first, gpts[:, 128:]], axis=1))
    dn2 = (mt(dqkv, wqkv_ref[...]) + mm(dpoints[:, 0 : 6 * POINTS], wpts_ref[...])).astype(BF16).astype(F32)
    dx1 = (dx2.astype(F32) + norm_pull(dn2, normed, inverse).astype(BF16).astype(F32)).astype(BF16)
    back = jnp.concatenate([dx1, updated, jnp.zeros((N, 256), BF16)], axis=1)
    back_ref[...] = tm(order, back).astype(BF16).reshape(N, 8, 128)
    for copy in leaving + [spare_copy]:
        copy.wait()


def like(shape, dtype):
    return jax.ShapeDtypeStruct(shape, dtype)


def call_pack_rows(tokens, cotangent, rigid):
    frames, residues, _ = tokens.shape
    return pl.pallas_call(
        pack_rows,
        out_shape=like((residues, frames, 2 * C + 128), BF16),
        compiler_params=limit(60),
        name="pack_rows",
    )(tokens, cotangent, rigid)


def call_time_forward(place, neighbors, rows, w_qkv, w_out):
    return pl.pallas_call(
        time_forward,
        in_specs=[SMEM, SMEM, VMEM, VMEM, VMEM],
        out_shape=(
            like((N, 8, 128), BF16), like((N, 3 * C), BF16), like((N, H * N), BF16),
            like((N, C), BF16),
        ),
        compiler_params=limit(60),
        name="time_forward",
    )(place, neighbors, rows, w_qkv, w_out)


def call_time_backward(core, back, rows, qkv, shares, mix, w_qkv, w_out):
    return pl.pallas_call(
        time_backward,
        in_specs=[SMEM] + [VMEM] * 7,
        out_shape=(like((N, 2 * C), BF16), like((LATE, 128), BF16), like((LATE, 128), BF16)),
        scratch_shapes=[
            pltpu.VMEM((N, 3 * C), BF16), pltpu.VMEM((4 * N, N), BF16), pltpu.VMEM((4 * N, N), BF16),
        ],
        compiler_params=limit(20),
        cost_estimate=pl.CostEstimate(flops=1000, bytes_accessed=1000, transcendentals=0),
        name="time_backward",
    )(core, back, rows, qkv, shares, mix, w_qkv, w_out)


def call_point_attention(core, weight, rows, w_qkv, w_pts, w_rep, w_out, w_up, w_down):
    heads, turn, spread, gather = selectors()
    sources = [w_qkv, turn, w_rep, heads, w_out, w_up, w_down, spread, gather, w_pts]
    return pl.pallas_call(
        point_attention,
        in_specs=[SMEM, SMEM, VMEM] + [HBM] * len(sources),
        out_specs=(VMEM, HBM, HBM),
        out_shape=(like((N, 8, 128), BF16), like((EARLY, 128), BF16), like((EARLY, 128), BF16)),
        scratch_shapes=[
            pltpu.VMEM((N, 3 * C), BF16), pltpu.VMEM((N, C), BF16),
            pltpu.VMEM((N, H * N), F32), pltpu.VMEM((N, H * N), F32),
            pltpu.VMEM((N, H * N), BF16), pltpu.VMEM((H * N, N), BF16),
            pltpu.VMEM((N, H * N), BF16), pltpu.VMEM((H * N, N), BF16),
            pltpu.VMEM((N, 3 * C), BF16), pltpu.VMEM((N, 6 * 256), BF16),
            pltpu.VMEM((H * N, 256), BF16), pltpu.VMEM((H * N, 256), BF16),
            pltpu.VMEM((N, 640), BF16), pltpu.VMEM((2, EARLY, 128), BF16),
            *[pltpu.VMEM(source.shape, BF16) for source in sources],
            pltpu.SemaphoreType.DMA((len(sources),)), pltpu.SemaphoreType.DMA((9,)),
        ],
        compiler_params=limit(60),
        name="point_attention",
    )(core, weight, rows, *sources)


def add_early(side_ref, keep_ref, got_ref, give_a_ref, give_b_ref, mine_ref, one_ref, two_ref, sems):
    part = EARLY // 4
    give, mine = 2 * (1 - side_ref[0]), 2 * side_ref[0]
    targets = (
        (give, give_a_ref), (give + 1, give_b_ref),
        (mine, mine_ref.at[0:part]), (mine + 1, mine_ref.at[part : 2 * part]),
    )
    steps = []
    for step, (index, target) in enumerate(targets):
        source = pl.ds(pl.multiple_of(index * part, part), part)
        span = slice(step * part, (step + 1) * part)
        steps.append(
            (
                pltpu.make_async_copy(keep_ref.at[source], one_ref.at[span], sems.at[3 * step]),
                pltpu.make_async_copy(got_ref.at[source], two_ref.at[span], sems.at[3 * step + 1]),
                pltpu.make_async_copy(one_ref.at[span], target, sems.at[3 * step + 2]),
            )
        )
    for first, second, _ in steps:
        first.start()
        second.start()
    for step, (first, second, out) in enumerate(steps):
        first.wait()
        second.wait()
        span = slice(step * part, (step + 1) * part)
        summed = one_ref[span, :].astype(F32) + two_ref[span, :].astype(F32)
        one_ref[span, :] = summed.astype(BF16)
        out.start()
    for _, _, out in steps:
        out.wait()


def call_add_early(side, keep, got):
    part = like((EARLY // 4, 128), BF16)
    return pl.pallas_call(
        add_early,
        in_specs=[SMEM, HBM, HBM],
        out_specs=(HBM, HBM, HBM),
        out_shape=(part, part, like((EARLY // 2, 128), BF16)),
        scratch_shapes=[
            pltpu.VMEM((EARLY, 128), BF16), pltpu.VMEM((EARLY, 128), BF16),
            pltpu.SemaphoreType.DMA((12,)),
        ],
        compiler_params=limit(60),
        cost_estimate=pl.CostEstimate(flops=EARLY * 128, bytes_accessed=EARLY * 128 * 6, transcendentals=0),
        name="add_early",
    )(side, keep, got)


def add_late(side_ref, keep_ref, got_ref, give_a_ref, give_b_ref, mine_ref):
    part = LATE // 4
    give, mine = 2 * (1 - side_ref[0]), 2 * side_ref[0]
    targets = (
        (give, give_a_ref, 0), (give + 1, give_b_ref, 0), (mine, mine_ref, 0), (mine + 1, mine_ref, part)
    )
    for index, ref, at in targets:
        span = pl.ds(pl.multiple_of(index * part, part), part)
        summed = keep_ref[span, :].astype(F32) + got_ref[span, :].astype(F32)
        ref[at : at + part, :] = summed.astype(BF16)


def call_add_late(side, keep, got):
    part = like((LATE // 4, 128), BF16)
    return pl.pallas_call(
        add_late,
        in_specs=[SMEM, VMEM, VMEM],
        out_shape=(part, part, like((LATE // 2, 128), BF16)),
        compiler_params=limit(8),
        name="add_late",
    )(side, keep, got)


def add_pairs(early_ref, early_a_ref, early_b_ref, late_ref, late_a_ref, late_b_ref, total_ref):
    at = 0
    for mine, parts in ((early_ref, (early_a_ref, early_b_ref)), (late_ref, (late_a_ref, late_b_ref))):
        size = parts[0].shape[0]
        for k, part in enumerate(parts):
            summed = mine[k * size : (k + 1) * size, :].astype(F32) + part[...].astype(F32)
            total_ref[at : at + size, :] = summed.astype(BF16)
            at += size
    total_ref[at:, :] = jnp.zeros((QUARTER - at, 128), BF16)


def call_add_pairs(*parts):
    return pl.pallas_call(
        add_pairs, out_shape=like((QUARTER, 128), BF16), compiler_params=limit(12), name="add_pairs"
    )(*parts)


def add_parts(parts_ref, copies_ref):
    count = parts_ref.shape[0]
    total = parts_ref[0].astype(F32)
    for k in range(1, count):
        total = total + parts_ref[k].astype(F32)
    total = total.astype(BF16)
    for k in range(copies_ref.shape[0]):
        copies_ref[k] = total


def call_add_parts(parts):
    return pl.pallas_call(
        add_parts, out_shape=like(parts.shape, BF16), compiler_params=limit(12),
        name="add_parts",
    )(parts)


def final_spot(late, at):
    unit = (at - EARLY if late else at) // C
    room = (LATE if late else EARLY) // (2 * C)
    return unit // room, (EARLY // 2 if late else 0) + (unit % room) * C


def segments(row):
    begin = row
    while begin < row + C:
        chunk, low = divmod(begin, CHUNK)
        size = min(CHUNK - low, row + C - begin)
        yield chunk, low, size, begin - row
        begin += size


FETCHES = 4


class Quarter:
    def __init__(self, spot, parts, out_refs, gain_ref, held_ref, stage_ref, in_sems, out_sems):
        self.spot, self.out_refs, self.gain_ref = spot, out_refs, gain_ref
        self.held_ref, self.stage_ref, self.out_sems = held_ref, stage_ref, out_sems
        size = SHARERS // FETCHES
        each = FETCHES // len(parts)
        self.fetches = [
            pltpu.make_async_copy(
                parts[k // each].at[k % each * size : (k % each + 1) * size],
                held_ref.at[k * size : (k + 1) * size],
                in_sems.at[k],
            )
            for k in range(FETCHES)
        ]
        for copy in self.fetches:
            copy.start()

    def leaving(self, half, quarter):
        found = []
        for k, name in enumerate(PIECES):
            tiles = PIECES[name][1] // 128
            for unit, (owner, at) in enumerate(UNITS[name]):
                where, row = final_spot(name.startswith("time"), at)
                if (owner, where) != (half, quarter):
                    continue
                down, across = (unit // tiles) * C, (unit % tiles) * 128
                rows = GAIN_ROW if name == "ipa_points" else C
                slot = len(found)
                copy = pltpu.make_async_copy(
                    self.stage_ref.at[slot, 0:rows],
                    self.out_refs[k].at[down : down + rows, across : across + 128],
                    self.out_sems.at[slot],
                )
                found.append((row, copy, name == "ipa_points" and across == 0))
        return found

    def each(self, act):
        for half in range(2):
            for quarter in range(2):
                pl.when(self.spot == 2 * half + quarter)(lambda h=half, q=quarter: act(h, q))

    def send(self):
        def act(half, quarter):
            waited = 0
            for slot, (row, copy, gains) in enumerate(self.leaving(half, quarter)):
                for chunk, low, size, to in segments(row):
                    while waited * (SHARERS // FETCHES) <= chunk:
                        self.fetches[waited].wait()
                        waited += 1
                    self.stage_ref[slot, to : to + size, :] = self.held_ref[
                        chunk, low : low + size, :
                    ].astype(F32)
                copy.start()
                if gains:
                    self.gain_ref[...] += self.stage_ref[slot, GAIN_ROW : GAIN_ROW + 1, :]
            for copy in self.fetches[waited:]:
                copy.wait()

        self.each(act)

    def finish(self):
        def act(half, quarter):
            for _, copy, _ in self.leaving(half, quarter):
                copy.wait()

        self.each(act)


def unpack_first(spots_ref, own_ref, swapped_ref, *refs):
    out_refs, gain_ref = refs[:7], refs[7]
    gain_ref[...] = jnp.zeros((1, 128), F32)
    quarters = [
        Quarter(spots_ref[0], (own_ref,), out_refs, gain_ref, *refs[8:12]),
        Quarter(spots_ref[1], (swapped_ref,), out_refs, gain_ref, *refs[12:16]),
    ]
    for quarter in quarters:
        quarter.send()
    for quarter in quarters:
        quarter.finish()


def unpack_second(spots_ref, part_a_ref, part_b_ref, gain_in_ref, *refs):
    out_refs, gain_ref = refs[7:14], refs[14]
    gain_ref[...] = gain_in_ref[...]
    quarter = Quarter(spots_ref[2], (part_a_ref, part_b_ref), out_refs, gain_ref, *refs[15:19])
    quarter.send()
    quarter.finish()


def unpack_last(spots_ref, part_a_ref, part_b_ref, gain_in_ref, ended_ref, *refs):
    out_refs, gain_ref, output_ref, token_ref = refs[7:14], refs[14], refs[15], refs[16]
    total_ref = refs[17]
    total_ref[...] = gain_in_ref[...]
    quarter = Quarter(spots_ref[3], (part_a_ref, part_b_ref), out_refs, total_ref, *refs[18:22])
    residues, frames, _ = ended_ref.shape
    ended = mm(order_matrix(), ended_ref[...].reshape(N, 2 * C)).astype(BF16)
    token_ref[...] = ended[:, 0:C].reshape(frames, residues, C)
    output_ref[...] = ended[:, C:].reshape(frames, residues, C)
    quarter.send()
    lane = lax.broadcasted_iota(jnp.int32, (1, 128), 1)
    for h in range(H):
        gain_ref[h] = jnp.sum(jnp.where(lane == h, total_ref[...], 0.0))
    quarter.finish()


OUTS = [
    like((GAIN_ROW if name == "ipa_points" else rows, columns), F32)
    for name, (rows, columns) in PIECES.items()
]
MOST = (EARLY_UNITS[0] + LATE_UNITS[0]) // 2
QUARTER_SCRATCH = [
    pltpu.VMEM((SHARERS, CHUNK, 128), BF16),
    pltpu.VMEM((MOST, C, 128), F32),
    pltpu.SemaphoreType.DMA((FETCHES,)),
    pltpu.SemaphoreType.DMA((MOST,)),
]
COST = pl.CostEstimate(flops=0, bytes_accessed=8 * MEGA, transcendentals=0)


def call_unpack_first(spots, own, swapped):
    return pl.pallas_call(
        unpack_first,
        in_specs=[SMEM, HBM, HBM],
        out_specs=(*[HBM] * 7, VMEM),
        out_shape=(*OUTS, like((1, 128), F32)),
        scratch_shapes=QUARTER_SCRATCH * 2,
        compiler_params=limit(20),
        cost_estimate=COST,
        name="unpack_first",
    )(spots, own, swapped)


def call_unpack_second(spots, parts, gain, grads):
    return pl.pallas_call(
        unpack_second,
        in_specs=[SMEM, HBM, HBM, VMEM] + [HBM] * 7,
        out_specs=(*[HBM] * 7, VMEM),
        out_shape=(*OUTS, like((1, 128), F32)),
        scratch_shapes=QUARTER_SCRATCH,
        input_output_aliases={4 + k: k for k in range(7)},
        compiler_params=limit(20),
        cost_estimate=COST,
        name="unpack_second",
    )(spots, *parts, gain, *grads)


def call_unpack_last(spots, parts, gain, ended, grads):
    residues, frames, _ = ended.shape
    rows = like((frames, residues, C), BF16)
    return pl.pallas_call(
        unpack_last,
        in_specs=[SMEM, HBM, HBM, VMEM, VMEM] + [HBM] * 7,
        out_specs=(*[HBM] * 7, SMEM, VMEM, VMEM),
        out_shape=(*OUTS, like((H,), F32), rows, rows),
        scratch_shapes=[pltpu.VMEM((1, 128), F32)] + QUARTER_SCRATCH,
        input_output_aliases={5 + k: k for k in range(7)},
        compiler_params=limit(20),
        name="unpack_last",
    )(spots, *parts, gain, ended, *grads)


def repeat_points(weight):
    parts = weight.reshape(6, POINTS, C)
    tripled = jnp.concatenate([parts, parts, parts], axis=1)
    return jnp.pad(tripled, ((0, 0), (0, 256 - 3 * POINTS), (0, 0))).reshape(6 * 256, C)


def swap_rows(rows, axes):
    return lax.all_to_all(rows, axes, split_axis=0, concat_axis=0, tiled=True)


def both_ways(parts):
    return [lax.ppermute(part, EVERYONE, ring) for part, ring in zip(parts, RINGS)]


def share(parts):
    return lax.all_to_all(
        parts, EVERYONE, split_axis=0, concat_axis=0, tiled=True, axis_index_groups=GROUPS
    )


def body(
    tokens, rigid_frames, neighbors, w_time_qkv, w_time_out, w_ipa_qkv, w_ipa_points,
    point_weight, w_ipa_out, w_up, w_down, cotangent,
):
    frames, residues = tokens.shape[:2]
    place = lax.axis_index(("line", "core")).astype(jnp.int32).reshape(1)
    core = lax.axis_index("core").astype(jnp.int32).reshape(1)
    place_res = lax.axis_index("res").astype(jnp.int32)
    sides = jnp.stack([(place_res >> 1) & 1, place_res & 1])
    side = jnp.where(core == 0, sides[0], sides[1])
    far = jnp.where(core == 0, sides[1], sides[0])
    spots = jnp.concatenate(
        [2 * core + side, 2 - 2 * core + far, 2 * core + 1 - side, 2 - 2 * core + 1 - far]
    )
    swap = [(0, 1), (1, 0)]
    points = w_ipa_points.T
    rows = swap_rows(call_pack_rows(tokens, cotangent, rigid_frames), ("line", "core"))
    rows = rows.reshape(N, 2 * C + 128)
    sent, qkv, shares, mix = call_time_forward(place, neighbors, rows, w_time_qkv, w_time_out)
    back, keep_early, give_early = call_point_attention(
        core, point_weight, swap_rows(sent, EVERYONE), w_ipa_qkv, points, repeat_points(points),
        w_ipa_out, w_up, w_down,
    )
    got_early = lax.ppermute(give_early, "core", swap)
    *give_early, mine_early = call_add_early(side, keep_early, got_early)
    got_early = both_ways(give_early)
    back, _ = lax.optimization_barrier((swap_rows(back, EVERYONE), give_early))
    ended, keep_late, give_late = call_time_backward(
        core, back, rows, qkv, shares, mix, w_time_qkv, w_time_out
    )
    got_late = lax.ppermute(give_late, "core", swap)
    *give_late, mine_late = call_add_late(side, keep_late, got_late)
    got_late = both_ways(give_late)
    total = call_add_pairs(mine_early, *got_early, mine_late, *got_late)
    parts = share(total.reshape(SHARERS, CHUNK, 128))
    own = share(call_add_parts(parts))
    paired = both_ways((own[: SHARERS // 2], own[SHARERS // 2 :]))
    swapped = lax.ppermute(own, "core", swap)
    ended = swap_rows(ended.reshape(residues, frames, 2 * C), ("line", "core"))
    *grads, gain = call_unpack_first(spots, own, swapped)
    paired, ended, gain = lax.optimization_barrier((paired, ended, gain))
    last = [lax.ppermute(part, "core", swap) for part in paired]
    *grads, gain = call_unpack_second(spots, paired, gain, grads)
    *grads, gain, output, token_grad = call_unpack_last(spots, last, gain, ended, grads)
    grads = dict(zip(PIECES, grads))
    return (
        output, token_grad, grads["time_qkv"], grads["time_out"], grads["ipa_qkv"],
        grads["ipa_points"].T, gain, grads["ipa_out"], grads["up"], grads["down"],
    )


def solution(mesh):
    devices = mesh.devices
    split = Mesh(
        devices.reshape(devices.shape[0] // 2, 2, devices.shape[1]), ("line", "core", "res")
    )
    frame = ("line", "core")
    rows = P(frame, "res", None)
    placed = (rows, P(None, frame, "res"), P("res", None)) + (P(),) * 8 + (rows,)
    return jax.shard_map(
        body,
        mesh=split,
        in_specs=placed,
        out_specs=(rows, rows) + (P(),) * 8,
        check_vma=False,
    )
```

```python
import math

import jax
import jax.numpy as jnp
import numpy as np
from jax import lax
from jax.experimental import pallas as pl
from jax.experimental.pallas import tpu as pltpu
from jax.sharding import Mesh, PartitionSpec as P

H = 12
P_SIZE = 4
NB = 32
C = 384
HID = 1536
N = 128
POINTS = H * P_SIZE
EPSILON = 1e-05
SCALE = 1.0 / math.sqrt(C // H)
STRENGTH = math.sqrt(2.0 / (9.0 * P_SIZE)) * math.sqrt(0.5)
F32 = jnp.float32
BF16 = jnp.bfloat16
EVERYONE = ("line", "core", "res")
SHARERS = 32
GAIN_ROW = 6 * POINTS

PIECES = {
    "up": (C, HID),
    "ipa_out": (C, C),
    "ipa_points": (C, C),
    "ipa_qkv": (C, 3 * C),
    "down": (HID, C),
    "time_qkv": (C, 3 * C),
    "time_out": (C, C),
}
EARLY_UNITS = [20, 19]
LATE_UNITS = [6, 6]
EARLY = max(EARLY_UNITS) * C
LATE = max(LATE_UNITS) * C
QUARTER = -(-(EARLY + LATE) // (2 * SHARERS * 16)) * SHARERS * 16
CHUNK = QUARTER // SHARERS


def ring_groups():
    bits = (2, 1)
    rings, groups = ([], []), [[], [], [], []]
    for line in range(8):
        for core in range(2):
            for res in range(8):
                place = (line * 2 + core) * 8 + res
                groups[2 * core + bool(res & bits[core])].append(place)
                for ring, step in zip(rings, (1, 3)):
                    x, y = res // 2, line % 2 * 2 + res % 2
                    if core == 0:
                        x = (x + step) % 4
                    else:
                        y = (y + step) % 4
                    there = ((line // 2 * 2 + y // 2) * 2 + core) * 8 + x * 2 + y % 2
                    ring.append((place, there))
    return rings, groups


RINGS, GROUPS = ring_groups()


def place_units():
    units, taken = {}, {True: [0, 0], False: [0, 0]}
    for name, (rows, columns) in PIECES.items():
        late = name.startswith("time")
        room = LATE_UNITS if late else EARLY_UNITS
        units[name] = []
        for _ in range(rows * columns // (C * 128)):
            half = 0 if taken[late][0] < room[0] else 1
            units[name].append((half, (EARLY if late else 0) + taken[late][half] * C))
            taken[late][half] += 1
    return units


UNITS = place_units()


def halves(core, keep_ref, give_ref):
    def put(name, value):
        tiles = value.shape[1] // 128
        base = EARLY if name.startswith("time") else 0
        pieces = [[], []]
        for unit, (half, at) in enumerate(UNITS[name]):
            down, across = (unit // tiles) * C, (unit % tiles) * 128
            part = value[down : down + C, across : across + 128].astype(BF16)
            pieces[half].append((at - base, part))

        for half in range(2):
            for ref, mine in ((keep_ref, True), (give_ref, False)):
                @pl.when((core == half) == mine)
                def store(ref=ref, parts=pieces[half]):
                    for at, part in parts:
                        ref[at : at + C, :] = part

    return put


def staged(core, stage_ref, keep_ref, give_ref, sems):
    waits = []

    def put(name, value):
        tiles = value.shape[1] // 128
        spans = {}
        for unit, (half, at) in enumerate(UNITS[name]):
            down, across = (unit // tiles) * C, (unit % tiles) * 128
            stage_ref[half, at : at + C, :] = value[down : down + C, across : across + 128].astype(
                BF16
            )
            low, _ = spans.get(half, (at, at))
            spans[half] = (low, at + C)
        for half, (low, high) in spans.items():
            sem = sems.at[len(waits)]
            source = stage_ref.at[half, low:high]

            @pl.when(core == half)
            def keep(source=source, low=low, high=high, sem=sem):
                pltpu.make_async_copy(source, keep_ref.at[low:high], sem).start()

            @pl.when(core != half)
            def give(source=source, low=low, high=high, sem=sem):
                pltpu.make_async_copy(source, give_ref.at[low:high], sem).start()

            waits.append(pltpu.make_async_copy(source, keep_ref.at[low:high], sem))

    return put, waits


MEGA = 1024 * 1024


def pinned(*arrays):
    return [pltpu.with_memory_space_constraint(array, pltpu.HBM) for array in arrays]


def limit(megabytes):
    return pltpu.CompilerParams(vmem_limit_bytes=megabytes * MEGA)


SMEM = pl.BlockSpec(memory_space=pltpu.SMEM)
VMEM = pl.BlockSpec(memory_space=pltpu.VMEM)
HBM = pl.BlockSpec(memory_space=pltpu.HBM)


def mm(left, right):
    return lax.dot_general(left, right, (((1,), (0,)), ((), ())), preferred_element_type=F32)


def mt(left, right):
    return lax.dot_general(left, right, (((1,), (1,)), ((), ())), preferred_element_type=F32)


def tm(left, right):
    return lax.dot_general(left, right, (((0,), (0,)), ((), ())), preferred_element_type=F32)


def norm(values):
    centered = values - jnp.mean(values, axis=-1, keepdims=True)
    inverse = lax.rsqrt(jnp.mean(centered * centered, axis=-1, keepdims=True) + EPSILON)
    return centered * inverse, inverse


def norm_pull(cotangent, normed, inverse):
    return inverse * (
        cotangent
        - jnp.mean(cotangent, axis=-1, keepdims=True)
        - normed * jnp.mean(cotangent * normed, axis=-1, keepdims=True)
    )


def split_two(values):
    high = values.astype(BF16)
    return high, (values - high.astype(F32)).astype(BF16)


def split_three(values):
    high, rest = values.astype(BF16), None
    rest = values - high.astype(F32)
    middle = rest.astype(BF16)
    return high, middle, (rest - middle.astype(F32)).astype(BF16)


def order_matrix():
    row = lax.broadcasted_iota(jnp.int32, (N, N), 0)
    col = lax.broadcasted_iota(jnp.int32, (N, N), 1)
    return jnp.where((col // 8 == row % 16) & (col % 8 == row // 16), 1.0, 0.0).astype(BF16)


def tile_masks():
    lane = lax.broadcasted_iota(jnp.int32, (1, 128), 1)
    return [jnp.where(lane // 32 == m, 1.0, 0.0).astype(BF16) for m in range(4)]


def masked_stack(tile, masks):
    return jnp.concatenate([tile * mask for mask in masks], axis=0)


def pack_rows(tokens_ref, cotangent_ref, rigid_ref, packed_ref):
    frames, residues, _ = tokens_ref.shape
    order = order_matrix()
    for at, ref in ((0, tokens_ref), (C, cotangent_ref)):
        turned = tm(order, ref[...].reshape(N, C))
        packed_ref[:, :, at : at + C] = turned.reshape(residues, frames, C).astype(BF16)
    row = lax.broadcasted_iota(jnp.int32, (N, residues), 0)
    col = lax.broadcasted_iota(jnp.int32, (N, residues), 1)
    rigid = jnp.zeros((N, 12), F32)
    for f in range(frames):
        pick = jnp.where(row == col * frames + f, 1.0, 0.0).astype(BF16)
        rigid = rigid + mt(pick, rigid_ref[:, f, :])
    packed_ref[:, :, 2 * C :] = jnp.zeros((residues, frames, 128), BF16)
    packed_ref[:, :, 2 * C : 2 * C + 12] = rigid.reshape(residues, frames, 12).astype(BF16)


def time_forward(
    place_ref, neighbors_ref, rows_ref, wqkv_hbm, wout_hbm, sent_ref, qkv_ref, shares_ref, mix_ref,
    tokens_ref, wqkv_ref, wout_ref, sems,
):
    fetched = [
        pltpu.make_async_copy(wqkv_hbm, wqkv_ref, sems.at[0]),
        pltpu.make_async_copy(wout_hbm, wout_ref, sems.at[1]),
    ]
    for copy in fetched:
        copy.start()
    tokens_ref[...] = rows_ref[:, 0:C]
    x = rows_ref[:, 0:C].astype(F32)
    normed, _ = norm(x)
    fetched[0].wait()
    qkv_ref[...] = mm(normed.astype(BF16), wqkv_ref[...]).astype(BF16)
    masks = tile_masks()
    for g in range(3):
        q = qkv_ref[:, g * 128 : (g + 1) * 128]
        k = qkv_ref[:, C + g * 128 : C + (g + 1) * 128]
        v = qkv_ref[:, 2 * C + g * 128 : 2 * C + (g + 1) * 128]
        for m in range(4):
            h = 4 * g + m
            scores = mt(q * masks[m], k) * SCALE
            raised = jnp.exp(scores - jnp.max(scores, axis=-1, keepdims=True))
            shares = raised / jnp.sum(raised, axis=-1, keepdims=True)
            shares_ref[:, h * 128 : (h + 1) * 128] = shares.astype(BF16)
        mixed = mm(shares_ref[:, g * 512 : (g + 1) * 512], masked_stack(v, masks))
        mix_ref[:, g * 128 : (g + 1) * 128] = mixed.astype(BF16)
    fetched[1].wait()
    x1 = (x + mm(mix_ref[...], wout_ref[...])).astype(BF16)
    lane = lax.broadcasted_iota(jnp.int32, (N, 128), 1)
    count = jnp.zeros((N, 128), F32)
    for n in range(NB):
        count = count + jnp.where(lane == neighbors_ref[place_ref[0], n], 1.0, 0.0)
    sent = jnp.concatenate([x1, rows_ref[:, C:], count.astype(BF16)], axis=1)
    sent_ref[...] = sent.reshape(N, 8, 128)


def time_backward(
    core_ref, back_ref, rows_ref, qkv_ref, shares_ref, mix_ref, wqkv_ref, wout_ref,
    sent_ref, keep_ref, give_ref, dqkv_ref, dcol_ref, pcol_ref,
):
    put = halves(core_ref[0], keep_ref, give_ref)
    back = back_ref[...].reshape(N, 1024)
    dx1 = back[:, 0:C]
    normed, inverse = norm(rows_ref[...].astype(F32))
    dmix = mt(dx1, wout_ref[...]).astype(BF16)
    put("time_out", tm(mix_ref[...], dx1))
    masks = tile_masks()
    for g in range(3):
        q = qkv_ref[:, g * 128 : (g + 1) * 128]
        k = qkv_ref[:, C + g * 128 : C + (g + 1) * 128]
        v = qkv_ref[:, 2 * C + g * 128 : 2 * C + (g + 1) * 128]
        dm = dmix[:, g * 128 : (g + 1) * 128]
        rows = []
        for m in range(4):
            h = 4 * g + m
            kept = shares_ref[:, h * 128 : (h + 1) * 128]
            pcol_ref[m * 128 : (m + 1) * 128, :] = kept
            shares = kept.astype(F32)
            dshares = mt(dm * masks[m], v)
            inner = jnp.sum(shares * dshares, axis=-1, keepdims=True)
            dlogit = (shares * (dshares - inner) * SCALE).astype(BF16)
            dcol_ref[m * 128 : (m + 1) * 128, :] = dlogit
            rows.append(dlogit)
        dq = mm(jnp.concatenate(rows, axis=1), masked_stack(k, masks))
        dk = tm(dcol_ref[...], masked_stack(q, masks))
        dv = tm(pcol_ref[...], masked_stack(dm, masks))
        dqkv_ref[:, g * 128 : (g + 1) * 128] = dq.astype(BF16)
        dqkv_ref[:, C + g * 128 : C + (g + 1) * 128] = dk.astype(BF16)
        dqkv_ref[:, 2 * C + g * 128 : 2 * C + (g + 1) * 128] = dv.astype(BF16)
    put("time_qkv", tm(normed.astype(BF16), dqkv_ref[...]))
    dnormed = mt(dqkv_ref[...], wqkv_ref[...]).astype(BF16).astype(F32)
    pulled = norm_pull(dnormed, normed, inverse).astype(BF16).astype(F32)
    sent_ref[:, 0:C] = (dx1.astype(F32) + pulled).astype(BF16)
    sent_ref[:, C : 2 * C] = back[:, C : 2 * C]


def selectors():
    lane = np.arange(256)
    inside = lane < 3 * POINTS
    head = np.where(inside, (lane % POINTS) // P_SIZE, -1)
    heads = (head[None, :] == np.arange(16)[:, None]).astype(np.float32)
    turn = np.zeros((128, 4 * 256), np.float32)
    for a in range(3):
        at = a * POINTS + np.arange(POINTS)
        for b in range(3):
            turn[3 * a + b, b * 256 + at] = 1.0
        turn[9 + a, 3 * 256 + at] = 1.0
    spread = np.zeros((128, 256), np.float32)
    spread[16:32] = heads
    gather = np.zeros((6 * 256, C), np.float32)
    for c in range(2):
        for b in range(3):
            for a in range(3):
                for p in range(POINTS):
                    gather[(3 * c + b) * 256 + a * POINTS + p, (3 * c + b) * POINTS + p] = 1.0
    return [jnp.asarray(item, BF16) for item in (heads, turn, spread, gather)]


def point_attention(
    core_ref, weight_ref, rows_ref, *refs
):
    sources, refs = refs[:10], refs[10:]
    back_ref, keep_ref, give_ref = refs[:3]
    (
        qkv_ref, mix_ref, shares_ref, point_ref, prow_ref, pcol_ref, drow_ref, dcol_ref,
        dqkv_ref, dlocal_ref, keys_ref, queries_ref, side_ref, stage_ref,
    ) = refs[3:17]
    held, sems, out_sems = refs[17:27], refs[27], refs[28]
    fetched = [
        pltpu.make_async_copy(source, target, sems.at[k])
        for k, (source, target) in enumerate(zip(sources, held))
    ]
    for copy in fetched:
        copy.start()
    (
        wqkv_ref, turn_ref, wrep_ref, heads_ref, wout_ref, wup_ref, wdown_ref, spread_ref,
        gather_ref, wpts_ref,
    ) = held
    put, leaving = staged(core_ref[0], stage_ref, keep_ref, give_ref, out_sems)
    stage_ref[1, EARLY_UNITS[1] * C : EARLY, :] = jnp.zeros((EARLY - EARLY_UNITS[1] * C, 128), BF16)
    spare = stage_ref.at[1, EARLY_UNITS[1] * C : EARLY]
    spare_copy = pltpu.make_async_copy(
        spare, keep_ref.at[EARLY_UNITS[1] * C : EARLY], out_sems.at[8]
    )

    @pl.when(core_ref[0] == 1)
    def keep_spare():
        spare_copy.start()

    @pl.when(core_ref[0] != 1)
    def give_spare():
        pltpu.make_async_copy(
            spare, give_ref.at[EARLY_UNITS[1] * C : EARLY], out_sems.at[8]
        ).start()

    masks = tile_masks()
    order = order_matrix()
    rows = mm(order, rows_ref[...].reshape(N, 1024))
    x1 = rows[:, 0:C]
    side_ref[...] = rows[:, C:].astype(BF16)
    normed, inverse = norm(x1)
    n2 = normed.astype(BF16)
    fetched[0].wait()
    qkv_ref[...] = mm(n2, wqkv_ref[...]).astype(BF16)

    lane = lax.broadcasted_iota(jnp.int32, (1, 256), 1)
    lane_head = jnp.where(lane < 3 * POINTS, (lane % POINTS) // P_SIZE, lane - 3 * POINTS)
    raw = jnp.zeros((1, 256), F32)
    for h in range(H):
        raw = jnp.where((lane < 3 * POINTS) & (lane_head == h), weight_ref[h], raw)
    soft = jnp.maximum(raw, 0.0) + jnp.log(1.0 + jnp.exp(-jnp.abs(raw)))
    strength = jnp.where(lane < 3 * POINTS, soft * STRENGTH, 0.0)
    head_masks = [jnp.where(lane_head == h, 1.0, 0.0).astype(BF16) for h in range(H)]

    for copy in fetched[1:4]:
        copy.wait()
    turned = mm(side_ref[:, C : C + 128], turn_ref[...])
    turns = [turned[:, b * 256 : (b + 1) * 256] for b in range(3)]
    local = mt(n2, wrep_ref[...])
    placed = []
    for c in range(2):
        total = turned[:, 768:1024]
        for b in range(3):
            total = total + turns[b] * local[:, (3 * c + b) * 256 : (3 * c + b + 1) * 256]
        placed.append(total)
    gq = placed[0]
    gk_bf = placed[1].astype(BF16)
    gk = gk_bf.astype(F32)
    heads = heads_ref[...]
    own = sum(mt(part, heads) for part in split_three(gq * gq * (0.5 * strength)))
    other = sum(mt(heads, part) for part in split_three(gk * gk * (0.5 * strength)))
    q_high, q_low = split_two(gq * strength)
    ones = (lane >= 3 * POINTS) & (lane < 3 * POINTS + 16)
    keys_one = jnp.where(ones, 1.0, gk).astype(BF16)
    queries_one = jnp.where(ones, 1.0, gq).astype(BF16)
    two_keys = jnp.concatenate([gk_bf, gk_bf], axis=1)
    count = side_ref[:, C + 128 : C + 256].astype(F32)
    near = count > 0.0

    for g in range(3):
        q = qkv_ref[:, g * 128 : (g + 1) * 128]
        k = qkv_ref[:, C + g * 128 : C + (g + 1) * 128]
        v = qkv_ref[:, 2 * C + g * 128 : 2 * C + (g + 1) * 128]
        for m in range(4):
            h = 4 * g + m
            at = slice(h * 128, (h + 1) * 128)
            direct = mt(q * masks[m], k) * (SCALE * math.sqrt(0.5))
            cross = mt(
                jnp.concatenate([q_high * head_masks[h], q_low * head_masks[h]], axis=1), two_keys
            )
            spot = cross - own[:, h : h + 1] - other[h : h + 1, :]
            point_ref[:, at] = spot
            logits = jnp.where(near, direct + spot, -1e30)
            raised = jnp.exp(logits - jnp.max(logits, axis=-1, keepdims=True)) * count
            shares = raised / jnp.sum(raised, axis=-1, keepdims=True)
            shares_ref[:, at] = shares
            prow_ref[:, at] = shares.astype(BF16)
            pcol_ref[at, :] = shares.astype(BF16)
            keys_ref[at, :] = keys_one * head_masks[h]
            queries_ref[at, :] = queries_one * head_masks[h]
        mixed = mm(prow_ref[:, g * 512 : (g + 1) * 512], masked_stack(v, masks))
        mix_ref[:, g * 128 : (g + 1) * 128] = mixed.astype(BF16)

    for copy in fetched[4:7]:
        copy.wait()
    cot = side_ref[:, 0:C]
    x2 = (x1 + mm(mix_ref[...], wout_ref[...])).astype(BF16).astype(F32)
    normed2, inverse2 = norm(x2)
    n3 = normed2.astype(BF16)
    u = mm(n3, wup_ref[...])
    root = math.sqrt(2.0 / math.pi)
    bent = jnp.tanh(root * (u + 0.044715 * u * u * u))
    hidden = (0.5 * u * (1.0 + bent)).astype(BF16)
    slope = 0.5 * (1.0 + bent) + 0.5 * u * (1.0 - bent * bent) * root * (
        1.0 + 3.0 * 0.044715 * u * u
    )
    updated = (x2 + mm(hidden, wdown_ref[...])).astype(BF16)
    put("down", tm(hidden, cot))
    dhidden = mt(cot, wdown_ref[...]).astype(BF16).astype(F32)
    du = (dhidden * slope).astype(BF16)
    put("up", tm(n3, du))
    dn3 = mt(du, wup_ref[...]).astype(BF16).astype(F32)
    dx2 = (cot.astype(F32) + norm_pull(dn3, normed2, inverse2).astype(BF16).astype(F32)).astype(
        BF16
    )
    dmix = mt(dx2, wout_ref[...]).astype(BF16)
    put("ipa_out", tm(mix_ref[...], dx2))

    gains = []
    for g in range(3):
        q = qkv_ref[:, g * 128 : (g + 1) * 128]
        k = qkv_ref[:, C + g * 128 : C + (g + 1) * 128]
        v = qkv_ref[:, 2 * C + g * 128 : 2 * C + (g + 1) * 128]
        dm = dmix[:, g * 128 : (g + 1) * 128]
        for m in range(4):
            h = 4 * g + m
            at = slice(h * 128, (h + 1) * 128)
            shares = shares_ref[:, at]
            dshares = mt(dm * masks[m], v)
            dlogit = shares * (dshares - jnp.sum(shares * dshares, axis=-1, keepdims=True))
            gains.append(jnp.sum(dlogit * point_ref[:, at], axis=0, keepdims=True))
            drow_ref[:, at] = dlogit.astype(BF16)
            dcol_ref[at, :] = dlogit.astype(BF16)
        group = slice(g * 512, (g + 1) * 512)
        dq = mm(drow_ref[:, group], masked_stack(k, masks)) * (SCALE * math.sqrt(0.5))
        dk = tm(dcol_ref[group, :], masked_stack(q, masks)) * (SCALE * math.sqrt(0.5))
        dv = tm(pcol_ref[group, :], masked_stack(dm, masks))
        dqkv_ref[:, g * 128 : (g + 1) * 128] = dq.astype(BF16)
        dqkv_ref[:, C + g * 128 : C + (g + 1) * 128] = dk.astype(BF16)
        dqkv_ref[:, 2 * C + g * 128 : 2 * C + (g + 1) * 128] = dv.astype(BF16)

    lane128 = lax.broadcasted_iota(jnp.int32, (1, 128), 1)
    gain = jnp.zeros((1, 128), F32)
    raw_row = jnp.zeros((1, 128), F32)
    for h in range(H):
        here = lane128 == h
        gain = jnp.where(here, jnp.sum(gains[h], axis=1, keepdims=True), gain)
        raw_row = jnp.where(here, weight_ref[h], raw_row)
    soft_row = jnp.maximum(raw_row, 0.0) + jnp.log(1.0 + jnp.exp(-jnp.abs(raw_row)))
    gain = gain / ((1.0 + jnp.exp(-raw_row)) * soft_row)

    for copy in fetched[7:10]:
        copy.wait()
    from_keys = mm(drow_ref[...], keys_ref[...])
    from_queries = tm(dcol_ref[...], queries_ref[...])
    spread = spread_ref[...]
    own_sum = sum(mm(part, spread) for part in split_two(from_keys[:, 128:256]))
    other_sum = sum(mm(part, spread) for part in split_two(from_queries[:, 128:256]))
    dgq = strength * (from_keys - gq * own_sum)
    dgk = (strength * (from_queries - gk * other_sum)).astype(BF16).astype(F32)
    for b in range(3):
        dlocal_ref[:, b * 256 : (b + 1) * 256] = (turns[b] * dgq).astype(BF16)
        dlocal_ref[:, (3 + b) * 256 : (4 + b) * 256] = (turns[b] * dgk).astype(BF16)
    dpoints = mm(dlocal_ref[...], gather_ref[...]).astype(BF16)
    dqkv = dqkv_ref[...]
    put("ipa_qkv", tm(n2, dqkv))
    gpts = tm(dpoints, n2)
    spare_row = lax.broadcasted_iota(jnp.int32, (C, 128), 0) == GAIN_ROW
    first = gpts[:, 0:128] + jnp.where(spare_row, gain, 0.0)
    put("ipa_points", jnp.concatenate([first, gpts[:, 128:]], axis=1))
    dn2 = (mt(dqkv, wqkv_ref[...]) + mm(dpoints[:, 0 : 6 * POINTS], wpts_ref[...])).astype(BF16).astype(F32)
    dx1 = (dx2.astype(F32) + norm_pull(dn2, normed, inverse).astype(BF16).astype(F32)).astype(BF16)
    back = jnp.concatenate([dx1, updated, jnp.zeros((N, 256), BF16)], axis=1)
    back_ref[...] = tm(order, back).astype(BF16).reshape(N, 8, 128)
    for copy in leaving + [spare_copy]:
        copy.wait()


def like(shape, dtype):
    return jax.ShapeDtypeStruct(shape, dtype)


def call_pack_rows(tokens, cotangent, rigid):
    frames, residues, _ = tokens.shape
    return pl.pallas_call(
        pack_rows,
        out_shape=like((residues, frames, 2 * C + 128), BF16),
        compiler_params=limit(8),
        name="pack_rows",
    )(*pinned(tokens, cotangent, rigid))


def call_time_forward(place, neighbors, rows, w_qkv, w_out):
    return pl.pallas_call(
        time_forward,
        in_specs=[SMEM, SMEM, VMEM, HBM, HBM],
        scratch_shapes=[
            pltpu.VMEM((C, 3 * C), BF16), pltpu.VMEM((C, C), BF16), pltpu.SemaphoreType.DMA((2,)),
        ],
        out_shape=(
            like((N, 8, 128), BF16), pltpu.HBM((N, 3 * C), BF16), pltpu.HBM((N, H * N), BF16),
            pltpu.HBM((N, C), BF16), pltpu.HBM((N, C), BF16),
        ),
        compiler_params=limit(12),
        name="time_forward",
    )(place, *pinned(neighbors), rows, *pinned(w_qkv, w_out))


def call_time_backward(core, back, rows, qkv, shares, mix, w_qkv, w_out):
    return pl.pallas_call(
        time_backward,
        in_specs=[SMEM] + [VMEM] * 7,
        out_shape=(like((N, 2 * C), BF16), like((LATE, 128), BF16), like((LATE, 128), BF16)),
        scratch_shapes=[
            pltpu.VMEM((N, 3 * C), BF16), pltpu.VMEM((4 * N, N), BF16), pltpu.VMEM((4 * N, N), BF16),
        ],
        compiler_params=limit(20),
        cost_estimate=pl.CostEstimate(flops=1000, bytes_accessed=1000, transcendentals=0),
        name="time_backward",
    )(core, back, *pinned(rows, qkv, shares, mix, w_qkv, w_out))


def call_point_attention(core, weight, rows, w_qkv, w_pts, w_rep, w_out, w_up, w_down):
    heads, turn, spread, gather = selectors()
    sources = [w_qkv, turn, w_rep, heads, w_out, w_up, w_down, spread, gather, w_pts]
    return pl.pallas_call(
        point_attention,
        in_specs=[SMEM, SMEM, VMEM] + [HBM] * len(sources),
        out_specs=(VMEM, HBM, HBM),
        out_shape=(like((N, 8, 128), BF16), pltpu.HBM((EARLY, 128), BF16), pltpu.HBM((EARLY, 128), BF16)),
        scratch_shapes=[
            pltpu.VMEM((N, 3 * C), BF16), pltpu.VMEM((N, C), BF16),
            pltpu.VMEM((N, H * N), F32), pltpu.VMEM((N, H * N), F32),
            pltpu.VMEM((N, H * N), BF16), pltpu.VMEM((H * N, N), BF16),
            pltpu.VMEM((N, H * N), BF16), pltpu.VMEM((H * N, N), BF16),
            pltpu.VMEM((N, 3 * C), BF16), pltpu.VMEM((N, 6 * 256), BF16),
            pltpu.VMEM((H * N, 256), BF16), pltpu.VMEM((H * N, 256), BF16),
            pltpu.VMEM((N, 640), BF16), pltpu.VMEM((2, EARLY, 128), BF16),
            *[pltpu.VMEM(source.shape, BF16) for source in sources],
            pltpu.SemaphoreType.DMA((len(sources),)), pltpu.SemaphoreType.DMA((9,)),
        ],
        compiler_params=limit(40),
        name="point_attention",
    )(core, weight, rows, *pinned(*sources))


def add_early(side_ref, keep_ref, got_ref, give_ref, mine_ref, one_ref, two_ref, sems):
    part = EARLY // 4
    give, mine = 2 * (1 - side_ref[0]), 2 * side_ref[0]
    targets = (
        (give, give_ref.at[0:part]), (give + 1, give_ref.at[part : 2 * part]),
        (mine, mine_ref.at[0:part]), (mine + 1, mine_ref.at[part : 2 * part]),
    )
    steps = []
    for step, (index, target) in enumerate(targets):
        source = pl.ds(pl.multiple_of(index * part, part), part)
        span = slice(step * part, (step + 1) * part)
        steps.append(
            (
                pltpu.make_async_copy(keep_ref.at[source], one_ref.at[span], sems.at[3 * step]),
                pltpu.make_async_copy(got_ref.at[source], two_ref.at[span], sems.at[3 * step + 1]),
                pltpu.make_async_copy(one_ref.at[span], target, sems.at[3 * step + 2]),
            )
        )
    for first, second, _ in steps:
        first.start()
        second.start()
    for step, (first, second, out) in enumerate(steps):
        first.wait()
        second.wait()
        span = slice(step * part, (step + 1) * part)
        summed = one_ref[span, :].astype(F32) + two_ref[span, :].astype(F32)
        one_ref[span, :] = summed.astype(BF16)
        out.start()
    for _, _, out in steps:
        out.wait()


def call_add_early(side, keep, got):
    part = like((EARLY // 2, 128), BF16)
    return pl.pallas_call(
        add_early,
        in_specs=[SMEM, HBM, HBM],
        out_specs=(HBM, HBM),
        out_shape=(pltpu.HBM(part.shape, BF16),) * 2,
        scratch_shapes=[
            pltpu.VMEM((EARLY, 128), BF16), pltpu.VMEM((EARLY, 128), BF16),
            pltpu.SemaphoreType.DMA((12,)),
        ],
        compiler_params=limit(8),
        cost_estimate=pl.CostEstimate(flops=EARLY * 128, bytes_accessed=EARLY * 128 * 6, transcendentals=0),
        name="add_early",
    )(side, *pinned(keep), got)


def add_late(side_ref, keep_ref, got_ref, give_a_ref, give_b_ref, mine_ref):
    part = LATE // 4
    give, mine = 2 * (1 - side_ref[0]), 2 * side_ref[0]
    targets = (
        (give, give_a_ref, 0), (give + 1, give_b_ref, 0), (mine, mine_ref, 0), (mine + 1, mine_ref, part)
    )
    for index, ref, at in targets:
        span = pl.ds(pl.multiple_of(index * part, part), part)
        summed = keep_ref[span, :].astype(F32) + got_ref[span, :].astype(F32)
        ref[at : at + part, :] = summed.astype(BF16)


def call_add_late(side, keep, got):
    part = like((LATE // 4, 128), BF16)
    return pl.pallas_call(
        add_late,
        in_specs=[SMEM, VMEM, VMEM],
        out_shape=(part, part, like((LATE // 2, 128), BF16)),
        compiler_params=limit(8),
        name="add_late",
    )(side, keep, got)


def add_pairs(early_ref, got_early_ref, late_ref, late_a_ref, late_b_ref, total_ref):
    at = 0
    for mine, parts in ((early_ref, (got_early_ref,)), (late_ref, (late_a_ref, late_b_ref))):
        size = parts[0].shape[0]
        for k, part in enumerate(parts):
            summed = mine[k * size : (k + 1) * size, :].astype(F32) + part[...].astype(F32)
            total_ref[at : at + size, :] = summed.astype(BF16)
            at += size
    total_ref[at:, :] = jnp.zeros((QUARTER - at, 128), BF16)


def call_add_pairs(*parts):
    return pl.pallas_call(
        add_pairs, out_shape=like((QUARTER, 128), BF16), compiler_params=limit(12), name="add_pairs"
    )(*parts)


def add_parts(parts_ref, copies_ref):
    count = parts_ref.shape[0]
    total = parts_ref[0].astype(F32)
    for k in range(1, count):
        total = total + parts_ref[k].astype(F32)
    total = total.astype(BF16)
    for k in range(copies_ref.shape[0]):
        copies_ref[k] = total


def call_add_parts(parts):
    return pl.pallas_call(
        add_parts, out_shape=like(parts.shape, BF16), compiler_params=limit(12),
        name="add_parts",
    )(parts)


def final_spot(late, at):
    unit = (at - EARLY if late else at) // C
    room = (LATE if late else EARLY) // (2 * C)
    return unit // room, (EARLY // 2 if late else 0) + (unit % room) * C


def segments(row):
    begin = row
    while begin < row + C:
        chunk, low = divmod(begin, CHUNK)
        size = min(CHUNK - low, row + C - begin)
        yield chunk, low, size, begin - row
        begin += size


FETCHES = 4


class Quarter:
    def __init__(self, spot, parts, out_refs, gain_ref, held_ref, stage_ref, in_sems, out_sems):
        self.spot, self.out_refs, self.gain_ref = spot, out_refs, gain_ref
        self.held_ref, self.stage_ref, self.out_sems = held_ref, stage_ref, out_sems
        size = SHARERS // FETCHES
        each = FETCHES // len(parts)
        self.fetches = [
            pltpu.make_async_copy(
                parts[k // each].at[k % each * size : (k % each + 1) * size],
                held_ref.at[k * size : (k + 1) * size],
                in_sems.at[k],
            )
            for k in range(FETCHES)
        ]
        for copy in self.fetches:
            copy.start()

    def leaving(self, half, quarter):
        found = []
        for k, name in enumerate(PIECES):
            tiles = PIECES[name][1] // 128
            for unit, (owner, at) in enumerate(UNITS[name]):
                where, row = final_spot(name.startswith("time"), at)
                if (owner, where) != (half, quarter):
                    continue
                down, across = (unit // tiles) * C, (unit % tiles) * 128
                rows = GAIN_ROW if name == "ipa_points" else C
                slot = len(found)
                copy = pltpu.make_async_copy(
                    self.stage_ref.at[slot, 0:rows],
                    self.out_refs[k].at[down : down + rows, across : across + 128],
                    self.out_sems.at[slot],
                )
                found.append((row, copy, name == "ipa_points" and across == 0))
        return found

    def each(self, act):
        for half in range(2):
            for quarter in range(2):
                pl.when(self.spot == 2 * half + quarter)(lambda h=half, q=quarter: act(h, q))

    def send(self):
        def act(half, quarter):
            waited = 0
            for slot, (row, copy, gains) in enumerate(self.leaving(half, quarter)):
                for chunk, low, size, to in segments(row):
                    while waited * (SHARERS // FETCHES) <= chunk:
                        self.fetches[waited].wait()
                        waited += 1
                    self.stage_ref[slot, to : to + size, :] = self.held_ref[
                        chunk, low : low + size, :
                    ].astype(F32)
                copy.start()
                if gains:
                    self.gain_ref[...] += self.stage_ref[slot, GAIN_ROW : GAIN_ROW + 1, :]
            for copy in self.fetches[waited:]:
                copy.wait()

        self.each(act)

    def finish(self):
        def act(half, quarter):
            for _, copy, _ in self.leaving(half, quarter):
                copy.wait()

        self.each(act)


def unpack_first(spots_ref, own_ref, swapped_ref, *refs):
    out_refs, gain_ref = refs[:7], refs[7]
    gain_ref[...] = jnp.zeros((1, 128), F32)
    quarters = [
        Quarter(spots_ref[0], (own_ref,), out_refs, gain_ref, *refs[8:12]),
        Quarter(spots_ref[1], (swapped_ref,), out_refs, gain_ref, *refs[12:16]),
    ]
    for quarter in quarters:
        quarter.send()
    for quarter in quarters:
        quarter.finish()


def unpack_second(spots_ref, part_a_ref, part_b_ref, gain_in_ref, *refs):
    out_refs, gain_ref = refs[7:14], refs[14]
    gain_ref[...] = gain_in_ref[...]
    quarter = Quarter(spots_ref[2], (part_a_ref, part_b_ref), out_refs, gain_ref, *refs[15:19])
    quarter.send()
    quarter.finish()


def unpack_last(spots_ref, part_a_ref, part_b_ref, gain_in_ref, ended_ref, *refs):
    out_refs, gain_ref, output_ref, token_ref = refs[7:14], refs[14], refs[15], refs[16]
    total_ref = refs[17]
    total_ref[...] = gain_in_ref[...]
    quarter = Quarter(spots_ref[3], (part_a_ref, part_b_ref), out_refs, total_ref, *refs[18:22])
    residues, frames, _ = ended_ref.shape
    ended = mm(order_matrix(), ended_ref[...].reshape(N, 2 * C)).astype(BF16)
    token_ref[...] = ended[:, 0:C].reshape(frames, residues, C)
    output_ref[...] = ended[:, C:].reshape(frames, residues, C)
    quarter.send()
    lane = lax.broadcasted_iota(jnp.int32, (1, 128), 1)
    for h in range(H):
        gain_ref[h] = jnp.sum(jnp.where(lane == h, total_ref[...], 0.0))
    quarter.finish()


OUTS = [
    like((GAIN_ROW if name == "ipa_points" else rows, columns), F32)
    for name, (rows, columns) in PIECES.items()
]
MOST = (EARLY_UNITS[0] + LATE_UNITS[0]) // 2
QUARTER_SCRATCH = [
    pltpu.VMEM((SHARERS, CHUNK, 128), BF16),
    pltpu.VMEM((MOST, C, 128), F32),
    pltpu.SemaphoreType.DMA((FETCHES,)),
    pltpu.SemaphoreType.DMA((MOST,)),
]
COST = pl.CostEstimate(flops=0, bytes_accessed=8 * MEGA, transcendentals=0)


def call_unpack_first(spots, own, swapped):
    return pl.pallas_call(
        unpack_first,
        in_specs=[SMEM, HBM, HBM],
        out_specs=(*[HBM] * 7, VMEM),
        out_shape=(*OUTS, like((1, 128), F32)),
        scratch_shapes=QUARTER_SCRATCH * 2,
        compiler_params=limit(20),
        cost_estimate=COST,
        name="unpack_first",
    )(spots, own, swapped)


def call_unpack_second(spots, parts, gain, grads):
    return pl.pallas_call(
        unpack_second,
        in_specs=[SMEM, HBM, HBM, VMEM] + [HBM] * 7,
        out_specs=(*[HBM] * 7, VMEM),
        out_shape=(*OUTS, like((1, 128), F32)),
        scratch_shapes=QUARTER_SCRATCH,
        input_output_aliases={4 + k: k for k in range(7)},
        compiler_params=limit(20),
        cost_estimate=COST,
        name="unpack_second",
    )(spots, *parts, gain, *grads)


def call_unpack_last(spots, parts, gain, ended, grads):
    residues, frames, _ = ended.shape
    rows = like((frames, residues, C), BF16)
    return pl.pallas_call(
        unpack_last,
        in_specs=[SMEM, HBM, HBM, VMEM, VMEM] + [HBM] * 7,
        out_specs=(*[HBM] * 7, SMEM, VMEM, VMEM),
        out_shape=(*OUTS, like((H,), F32), rows, rows),
        scratch_shapes=[pltpu.VMEM((1, 128), F32)] + QUARTER_SCRATCH,
        input_output_aliases={5 + k: k for k in range(7)},
        compiler_params=limit(20),
        name="unpack_last",
    )(spots, *parts, gain, ended, *grads)


def repeat_points(weight):
    parts = weight.reshape(6, POINTS, C)
    tripled = jnp.concatenate([parts, parts, parts], axis=1)
    return jnp.pad(tripled, ((0, 0), (0, 256 - 3 * POINTS), (0, 0))).reshape(6 * 256, C)


def swap_rows(rows, axes):
    return lax.all_to_all(rows, axes, split_axis=0, concat_axis=0, tiled=True)


def both_ways(parts):
    return [lax.ppermute(part, EVERYONE, ring) for part, ring in zip(parts, RINGS)]


def share(parts):
    return lax.all_to_all(
        parts, EVERYONE, split_axis=0, concat_axis=0, tiled=True, axis_index_groups=GROUPS
    )


def body(
    tokens, rigid_frames, neighbors, w_time_qkv, w_time_out, w_ipa_qkv, w_ipa_points,
    point_weight, w_ipa_out, w_up, w_down, cotangent,
):
    frames, residues = tokens.shape[:2]
    place = lax.axis_index(("line", "core")).astype(jnp.int32).reshape(1)
    core = lax.axis_index("core").astype(jnp.int32).reshape(1)
    place_res = lax.axis_index("res").astype(jnp.int32)
    sides = jnp.stack([(place_res >> 1) & 1, place_res & 1])
    side = jnp.where(core == 0, sides[0], sides[1])
    far = jnp.where(core == 0, sides[1], sides[0])
    spots = jnp.concatenate(
        [2 * core + side, 2 - 2 * core + far, 2 * core + 1 - side, 2 - 2 * core + 1 - far]
    )
    swap = [(0, 1), (1, 0)]
    points = w_ipa_points.T
    rows = swap_rows(call_pack_rows(tokens, cotangent, rigid_frames), ("line", "core"))
    rows = rows.reshape(N, 2 * C + 128)
    sent, qkv, shares, mix, rows = call_time_forward(place, neighbors, rows, w_time_qkv, w_time_out)
    back, keep_early, give_early = call_point_attention(
        core, point_weight, swap_rows(sent, EVERYONE), w_ipa_qkv, points, repeat_points(points),
        w_ipa_out, w_up, w_down,
    )
    got_early = lax.ppermute(give_early, "core", swap)
    give_early, mine_early = call_add_early(side, keep_early, got_early)
    got_early = lax.ppermute(give_early, EVERYONE, RINGS[0])
    back = swap_rows(back, EVERYONE)
    ended, keep_late, give_late = call_time_backward(
        core, back, rows, qkv, shares, mix, w_time_qkv, w_time_out
    )
    got_late = lax.ppermute(give_late, "core", swap)
    *give_late, mine_late = call_add_late(side, keep_late, got_late)
    got_late = both_ways(give_late)
    total = call_add_pairs(mine_early, got_early, mine_late, *got_late)
    parts = share(total.reshape(SHARERS, CHUNK, 128))
    own = share(call_add_parts(parts))
    paired = both_ways((own[: SHARERS // 2], own[SHARERS // 2 :]))
    swapped = lax.ppermute(own, "core", swap)
    ended = swap_rows(ended.reshape(residues, frames, 2 * C), ("line", "core"))
    *grads, gain = call_unpack_first(spots, own, swapped)
    paired, ended, gain = lax.optimization_barrier((paired, ended, gain))
    last = [lax.ppermute(part, "core", swap) for part in paired]
    *grads, gain = call_unpack_second(spots, paired, gain, grads)
    *grads, gain, output, token_grad = call_unpack_last(spots, last, gain, ended, grads)
    grads = dict(zip(PIECES, grads))
    return (
        output, token_grad, grads["time_qkv"], grads["time_out"], grads["ipa_qkv"],
        grads["ipa_points"].T, gain, grads["ipa_out"], grads["up"], grads["down"],
    )


def solution(mesh):
    devices = mesh.devices
    split = Mesh(
        devices.reshape(devices.shape[0] // 2, 2, devices.shape[1]), ("line", "core", "res")
    )
    frame = ("line", "core")
    rows = P(frame, "res", None)
    placed = (rows, P(None, frame, "res"), P("res", None)) + (P(),) * 8 + (rows,)
    return jax.shard_map(
        body,
        mesh=split,
        in_specs=placed,
        out_specs=(rows, rows) + (P(),) * 8,
        check_vma=False,
    )
```

```python
import math

import jax
import jax.numpy as jnp
import numpy as np
from jax import lax
from jax.experimental import pallas as pl
from jax.experimental.pallas import tpu as pltpu
from jax.sharding import Mesh, PartitionSpec as P

H = 12
P_SIZE = 4
NB = 32
C = 384
HID = 1536
N = 128
POINTS = H * P_SIZE
EPSILON = 1e-05
SCALE = 1.0 / math.sqrt(C // H)
STRENGTH = math.sqrt(2.0 / (9.0 * P_SIZE)) * math.sqrt(0.5)
F32 = jnp.float32
BF16 = jnp.bfloat16
EVERYONE = ("line", "core", "res")
SHARERS = 32
GAIN_ROW = 6 * POINTS

PIECES = {
    "up": (C, HID),
    "ipa_out": (C, C),
    "ipa_points": (C, C),
    "ipa_qkv": (C, 3 * C),
    "down": (HID, C),
    "time_qkv": (C, 3 * C),
    "time_out": (C, C),
}
EARLY_UNITS = [20, 19]
LATE_UNITS = [6, 6]
EARLY = max(EARLY_UNITS) * C
LATE = max(LATE_UNITS) * C
QUARTER = -(-(EARLY + LATE) // (2 * SHARERS * 16)) * SHARERS * 16
CHUNK = QUARTER // SHARERS


def ring_groups():
    bits = (2, 1)
    rings, groups = ([], []), [[], [], [], []]
    for line in range(8):
        for core in range(2):
            for res in range(8):
                place = (line * 2 + core) * 8 + res
                groups[2 * core + bool(res & bits[core])].append(place)
                for ring, step in zip(rings, (1, 3)):
                    x, y = res // 2, line % 2 * 2 + res % 2
                    if core == 0:
                        x = (x + step) % 4
                    else:
                        y = (y + step) % 4
                    there = ((line // 2 * 2 + y // 2) * 2 + core) * 8 + x * 2 + y % 2
                    ring.append((place, there))
    return rings, groups


RINGS, GROUPS = ring_groups()


def place_units():
    units, taken = {}, {True: [0, 0], False: [0, 0]}
    for name, (rows, columns) in PIECES.items():
        late = name.startswith("time")
        room = LATE_UNITS if late else EARLY_UNITS
        units[name] = []
        for _ in range(rows * columns // (C * 128)):
            half = 0 if taken[late][0] < room[0] else 1
            units[name].append((half, (EARLY if late else 0) + taken[late][half] * C))
            taken[late][half] += 1
    return units


UNITS = place_units()


def halves(core, keep_ref, give_ref):
    def put(name, value):
        tiles = value.shape[1] // 128
        base = EARLY if name.startswith("time") else 0
        pieces = [[], []]
        for unit, (half, at) in enumerate(UNITS[name]):
            down, across = (unit // tiles) * C, (unit % tiles) * 128
            part = value[down : down + C, across : across + 128].astype(BF16)
            pieces[half].append((at - base, part))

        for half in range(2):
            for ref, mine in ((keep_ref, True), (give_ref, False)):
                @pl.when((core == half) == mine)
                def store(ref=ref, parts=pieces[half]):
                    for at, part in parts:
                        ref[at : at + C, :] = part

    return put


def staged(core, stage_ref, keep_ref, give_ref, sems):
    waits = []

    def put(name, value):
        tiles = value.shape[1] // 128
        spans = {}
        for unit, (half, at) in enumerate(UNITS[name]):
            down, across = (unit // tiles) * C, (unit % tiles) * 128
            stage_ref[half, at : at + C, :] = value[down : down + C, across : across + 128].astype(
                BF16
            )
            low, _ = spans.get(half, (at, at))
            spans[half] = (low, at + C)
        for half, (low, high) in spans.items():
            sem = sems.at[len(waits)]
            source = stage_ref.at[half, low:high]

            @pl.when(core == half)
            def keep(source=source, low=low, high=high, sem=sem):
                pltpu.make_async_copy(source, keep_ref.at[low:high], sem).start()

            @pl.when(core != half)
            def give(source=source, low=low, high=high, sem=sem):
                pltpu.make_async_copy(source, give_ref.at[low:high], sem).start()

            waits.append(pltpu.make_async_copy(source, keep_ref.at[low:high], sem))

    return put, waits


MEGA = 1024 * 1024


def pinned(*arrays):
    return [pltpu.with_memory_space_constraint(array, pltpu.HBM) for array in arrays]


def limit(megabytes):
    return pltpu.CompilerParams(vmem_limit_bytes=megabytes * MEGA)


SMEM = pl.BlockSpec(memory_space=pltpu.SMEM)
VMEM = pl.BlockSpec(memory_space=pltpu.VMEM)
HBM = pl.BlockSpec(memory_space=pltpu.HBM)


def mm(left, right):
    return lax.dot_general(left, right, (((1,), (0,)), ((), ())), preferred_element_type=F32)


def mt(left, right):
    return lax.dot_general(left, right, (((1,), (1,)), ((), ())), preferred_element_type=F32)


def tm(left, right):
    return lax.dot_general(left, right, (((0,), (0,)), ((), ())), preferred_element_type=F32)


def norm(values):
    centered = values - jnp.mean(values, axis=-1, keepdims=True)
    inverse = lax.rsqrt(jnp.mean(centered * centered, axis=-1, keepdims=True) + EPSILON)
    return centered * inverse, inverse


def norm_pull(cotangent, normed, inverse):
    return inverse * (
        cotangent
        - jnp.mean(cotangent, axis=-1, keepdims=True)
        - normed * jnp.mean(cotangent * normed, axis=-1, keepdims=True)
    )


def split_two(values):
    high = values.astype(BF16)
    return high, (values - high.astype(F32)).astype(BF16)


def split_three(values):
    high, rest = values.astype(BF16), None
    rest = values - high.astype(F32)
    middle = rest.astype(BF16)
    return high, middle, (rest - middle.astype(F32)).astype(BF16)


def order_matrix():
    row = lax.broadcasted_iota(jnp.int32, (N, N), 0)
    col = lax.broadcasted_iota(jnp.int32, (N, N), 1)
    return jnp.where((col // 8 == row % 16) & (col % 8 == row // 16), 1.0, 0.0).astype(BF16)


def tile_masks():
    lane = lax.broadcasted_iota(jnp.int32, (1, 128), 1)
    return [jnp.where(lane // 32 == m, 1.0, 0.0).astype(BF16) for m in range(4)]


def masked_stack(tile, masks):
    return jnp.concatenate([tile * mask for mask in masks], axis=0)


def pack_rows(tokens_ref, cotangent_ref, rigid_ref, packed_ref):
    frames, residues, _ = tokens_ref.shape
    order = order_matrix()
    for at, ref in ((0, tokens_ref), (C, cotangent_ref)):
        turned = tm(order, ref[...].reshape(N, C))
        packed_ref[:, :, at : at + C] = turned.reshape(residues, frames, C).astype(BF16)
    row = lax.broadcasted_iota(jnp.int32, (N, residues), 0)
    col = lax.broadcasted_iota(jnp.int32, (N, residues), 1)
    rigid = jnp.zeros((N, 12), F32)
    for f in range(frames):
        pick = jnp.where(row == col * frames + f, 1.0, 0.0).astype(BF16)
        rigid = rigid + mt(pick, rigid_ref[:, f, :])
    packed_ref[:, :, 2 * C :] = jnp.zeros((residues, frames, 128), BF16)
    packed_ref[:, :, 2 * C : 2 * C + 12] = rigid.reshape(residues, frames, 12).astype(BF16)


def time_forward(
    place_ref, neighbors_ref, rows_ref, wqkv_hbm, wout_hbm, sent_ref, qkv_hbm, shares_hbm, mix_hbm,
    tokens_hbm, wqkv_ref, wout_ref, sems, qkv_ref, shares_ref, mix_ref, tokens_ref, out_sems,
):
    saved = [
        pltpu.make_async_copy(source, target, out_sems.at[k])
        for k, (source, target) in enumerate(
            (
                (tokens_ref, tokens_hbm), (qkv_ref, qkv_hbm), (shares_ref, shares_hbm),
                (mix_ref, mix_hbm),
            )
        )
    ]
    fetched = [
        pltpu.make_async_copy(wqkv_hbm, wqkv_ref, sems.at[0]),
        pltpu.make_async_copy(wout_hbm, wout_ref, sems.at[1]),
    ]
    for copy in fetched:
        copy.start()
    tokens_ref[...] = rows_ref[:, 0:C]
    saved[0].start()
    x = rows_ref[:, 0:C].astype(F32)
    normed, _ = norm(x)
    fetched[0].wait()
    qkv_ref[...] = mm(normed.astype(BF16), wqkv_ref[...]).astype(BF16)
    saved[1].start()
    masks = tile_masks()
    for g in range(3):
        q = qkv_ref[:, g * 128 : (g + 1) * 128]
        k = qkv_ref[:, C + g * 128 : C + (g + 1) * 128]
        v = qkv_ref[:, 2 * C + g * 128 : 2 * C + (g + 1) * 128]
        for m in range(4):
            h = 4 * g + m
            scores = mt(q * masks[m], k) * SCALE
            raised = jnp.exp(scores - jnp.max(scores, axis=-1, keepdims=True))
            shares = raised / jnp.sum(raised, axis=-1, keepdims=True)
            shares_ref[:, h * 128 : (h + 1) * 128] = shares.astype(BF16)
        mixed = mm(shares_ref[:, g * 512 : (g + 1) * 512], masked_stack(v, masks))
        mix_ref[:, g * 128 : (g + 1) * 128] = mixed.astype(BF16)
    saved[2].start()
    saved[3].start()
    fetched[1].wait()
    x1 = (x + mm(mix_ref[...], wout_ref[...])).astype(BF16)
    lane = lax.broadcasted_iota(jnp.int32, (N, 128), 1)
    count = jnp.zeros((N, 128), F32)
    for n in range(NB):
        count = count + jnp.where(lane == neighbors_ref[place_ref[0], n], 1.0, 0.0)
    sent = jnp.concatenate([x1, rows_ref[:, C:], count.astype(BF16)], axis=1)
    sent_ref[...] = sent.reshape(N, 8, 128)
    for copy in saved:
        copy.wait()


def time_backward(
    core_ref, back_ref, *refs
):
    sources, (sent_ref, keep_ref, give_ref, dqkv_ref, dcol_ref, pcol_ref) = refs[:6], refs[6:12]
    held, sems = refs[12:18], refs[18]
    fetched = [
        pltpu.make_async_copy(source, target, sems.at[k])
        for k, (source, target) in enumerate(zip(sources, held))
    ]
    for copy in fetched:
        copy.start()
    wout_ref, mix_ref, rows_ref, qkv_ref, shares_ref, wqkv_ref = held
    put = halves(core_ref[0], keep_ref, give_ref)
    back = back_ref[...].reshape(N, 1024)
    dx1 = back[:, 0:C]
    for copy in fetched[0:3]:
        copy.wait()
    normed, inverse = norm(rows_ref[...].astype(F32))
    dmix = mt(dx1, wout_ref[...]).astype(BF16)
    put("time_out", tm(mix_ref[...], dx1))
    masks = tile_masks()
    for copy in fetched[3:6]:
        copy.wait()
    for g in range(3):
        q = qkv_ref[:, g * 128 : (g + 1) * 128]
        k = qkv_ref[:, C + g * 128 : C + (g + 1) * 128]
        v = qkv_ref[:, 2 * C + g * 128 : 2 * C + (g + 1) * 128]
        dm = dmix[:, g * 128 : (g + 1) * 128]
        rows = []
        for m in range(4):
            h = 4 * g + m
            kept = shares_ref[:, h * 128 : (h + 1) * 128]
            pcol_ref[m * 128 : (m + 1) * 128, :] = kept
            shares = kept.astype(F32)
            dshares = mt(dm * masks[m], v)
            inner = jnp.sum(shares * dshares, axis=-1, keepdims=True)
            dlogit = (shares * (dshares - inner) * SCALE).astype(BF16)
            dcol_ref[m * 128 : (m + 1) * 128, :] = dlogit
            rows.append(dlogit)
        dq = mm(jnp.concatenate(rows, axis=1), masked_stack(k, masks))
        dk = tm(dcol_ref[...], masked_stack(q, masks))
        dv = tm(pcol_ref[...], masked_stack(dm, masks))
        dqkv_ref[:, g * 128 : (g + 1) * 128] = dq.astype(BF16)
        dqkv_ref[:, C + g * 128 : C + (g + 1) * 128] = dk.astype(BF16)
        dqkv_ref[:, 2 * C + g * 128 : 2 * C + (g + 1) * 128] = dv.astype(BF16)
    put("time_qkv", tm(normed.astype(BF16), dqkv_ref[...]))
    dnormed = mt(dqkv_ref[...], wqkv_ref[...]).astype(BF16).astype(F32)
    pulled = norm_pull(dnormed, normed, inverse).astype(BF16).astype(F32)
    sent_ref[:, 0:C] = (dx1.astype(F32) + pulled).astype(BF16)
    sent_ref[:, C : 2 * C] = back[:, C : 2 * C]


def selectors():
    lane = np.arange(256)
    inside = lane < 3 * POINTS
    head = np.where(inside, (lane % POINTS) // P_SIZE, -1)
    heads = (head[None, :] == np.arange(16)[:, None]).astype(np.float32)
    turn = np.zeros((128, 4 * 256), np.float32)
    for a in range(3):
        at = a * POINTS + np.arange(POINTS)
        for b in range(3):
            turn[3 * a + b, b * 256 + at] = 1.0
        turn[9 + a, 3 * 256 + at] = 1.0
    spread = np.zeros((128, 256), np.float32)
    spread[16:32] = heads
    gather = np.zeros((6 * 256, C), np.float32)
    for c in range(2):
        for b in range(3):
            for a in range(3):
                for p in range(POINTS):
                    gather[(3 * c + b) * 256 + a * POINTS + p, (3 * c + b) * POINTS + p] = 1.0
    return [jnp.asarray(item, BF16) for item in (heads, turn, spread, gather)]


def point_attention(
    core_ref, weight_ref, rows_ref, *refs
):
    sources, refs = refs[:10], refs[10:]
    back_ref, keep_ref, give_ref = refs[:3]
    (
        qkv_ref, mix_ref, shares_ref, point_ref, prow_ref, pcol_ref, drow_ref, dcol_ref,
        dqkv_ref, dlocal_ref, keys_ref, queries_ref, side_ref, stage_ref,
    ) = refs[3:17]
    held, sems, out_sems = refs[17:27], refs[27], refs[28]
    fetched = [
        pltpu.make_async_copy(source, target, sems.at[k])
        for k, (source, target) in enumerate(zip(sources, held))
    ]
    for copy in fetched:
        copy.start()
    (
        wqkv_ref, turn_ref, wrep_ref, heads_ref, wout_ref, wup_ref, wdown_ref, spread_ref,
        gather_ref, wpts_ref,
    ) = held
    put, leaving = staged(core_ref[0], stage_ref, keep_ref, give_ref, out_sems)
    stage_ref[1, EARLY_UNITS[1] * C : EARLY, :] = jnp.zeros((EARLY - EARLY_UNITS[1] * C, 128), BF16)
    spare = stage_ref.at[1, EARLY_UNITS[1] * C : EARLY]
    spare_copy = pltpu.make_async_copy(
        spare, keep_ref.at[EARLY_UNITS[1] * C : EARLY], out_sems.at[8]
    )

    @pl.when(core_ref[0] == 1)
    def keep_spare():
        spare_copy.start()

    @pl.when(core_ref[0] != 1)
    def give_spare():
        pltpu.make_async_copy(
            spare, give_ref.at[EARLY_UNITS[1] * C : EARLY], out_sems.at[8]
        ).start()

    masks = tile_masks()
    order = order_matrix()
    rows = mm(order, rows_ref[...].reshape(N, 1024))
    x1 = rows[:, 0:C]
    side_ref[...] = rows[:, C:].astype(BF16)
    normed, inverse = norm(x1)
    n2 = normed.astype(BF16)
    fetched[0].wait()
    qkv_ref[...] = mm(n2, wqkv_ref[...]).astype(BF16)

    lane = lax.broadcasted_iota(jnp.int32, (1, 256), 1)
    lane_head = jnp.where(lane < 3 * POINTS, (lane % POINTS) // P_SIZE, lane - 3 * POINTS)
    raw = jnp.zeros((1, 256), F32)
    for h in range(H):
        raw = jnp.where((lane < 3 * POINTS) & (lane_head == h), weight_ref[h], raw)
    soft = jnp.maximum(raw, 0.0) + jnp.log(1.0 + jnp.exp(-jnp.abs(raw)))
    strength = jnp.where(lane < 3 * POINTS, soft * STRENGTH, 0.0)
    head_masks = [jnp.where(lane_head == h, 1.0, 0.0).astype(BF16) for h in range(H)]

    for copy in fetched[1:4]:
        copy.wait()
    turned = mm(side_ref[:, C : C + 128], turn_ref[...])
    turns = [turned[:, b * 256 : (b + 1) * 256] for b in range(3)]
    local = mt(n2, wrep_ref[...])
    placed = []
    for c in range(2):
        total = turned[:, 768:1024]
        for b in range(3):
            total = total + turns[b] * local[:, (3 * c + b) * 256 : (3 * c + b + 1) * 256]
        placed.append(total)
    gq = placed[0]
    gk_bf = placed[1].astype(BF16)
    gk = gk_bf.astype(F32)
    heads = heads_ref[...]
    own = sum(mt(part, heads) for part in split_three(gq * gq * (0.5 * strength)))
    other = sum(mt(heads, part) for part in split_three(gk * gk * (0.5 * strength)))
    q_high, q_low = split_two(gq * strength)
    ones = (lane >= 3 * POINTS) & (lane < 3 * POINTS + 16)
    keys_one = jnp.where(ones, 1.0, gk).astype(BF16)
    queries_one = jnp.where(ones, 1.0, gq).astype(BF16)
    two_keys = jnp.concatenate([gk_bf, gk_bf], axis=1)
    count = side_ref[:, C + 128 : C + 256].astype(F32)
    near = count > 0.0

    for g in range(3):
        q = qkv_ref[:, g * 128 : (g + 1) * 128]
        k = qkv_ref[:, C + g * 128 : C + (g + 1) * 128]
        v = qkv_ref[:, 2 * C + g * 128 : 2 * C + (g + 1) * 128]
        for m in range(4):
            h = 4 * g + m
            at = slice(h * 128, (h + 1) * 128)
            direct = mt(q * masks[m], k) * (SCALE * math.sqrt(0.5))
            cross = mt(
                jnp.concatenate([q_high * head_masks[h], q_low * head_masks[h]], axis=1), two_keys
            )
            spot = cross - own[:, h : h + 1] - other[h : h + 1, :]
            point_ref[:, at] = spot
            logits = jnp.where(near, direct + spot, -1e30)
            raised = jnp.exp(logits - jnp.max(logits, axis=-1, keepdims=True)) * count
            shares = raised / jnp.sum(raised, axis=-1, keepdims=True)
            shares_ref[:, at] = shares
            prow_ref[:, at] = shares.astype(BF16)
            pcol_ref[at, :] = shares.astype(BF16)
            keys_ref[at, :] = keys_one * head_masks[h]
            queries_ref[at, :] = queries_one * head_masks[h]
        mixed = mm(prow_ref[:, g * 512 : (g + 1) * 512], masked_stack(v, masks))
        mix_ref[:, g * 128 : (g + 1) * 128] = mixed.astype(BF16)

    for copy in fetched[4:7]:
        copy.wait()
    cot = side_ref[:, 0:C]
    x2 = (x1 + mm(mix_ref[...], wout_ref[...])).astype(BF16).astype(F32)
    normed2, inverse2 = norm(x2)
    n3 = normed2.astype(BF16)
    u = mm(n3, wup_ref[...])
    root = math.sqrt(2.0 / math.pi)
    bent = jnp.tanh(root * (u + 0.044715 * u * u * u))
    hidden = (0.5 * u * (1.0 + bent)).astype(BF16)
    slope = 0.5 * (1.0 + bent) + 0.5 * u * (1.0 - bent * bent) * root * (
        1.0 + 3.0 * 0.044715 * u * u
    )
    updated = (x2 + mm(hidden, wdown_ref[...])).astype(BF16)
    put("down", tm(hidden, cot))
    dhidden = mt(cot, wdown_ref[...]).astype(BF16).astype(F32)
    du = (dhidden * slope).astype(BF16)
    put("up", tm(n3, du))
    dn3 = mt(du, wup_ref[...]).astype(BF16).astype(F32)
    dx2 = (cot.astype(F32) + norm_pull(dn3, normed2, inverse2).astype(BF16).astype(F32)).astype(
        BF16
    )
    dmix = mt(dx2, wout_ref[...]).astype(BF16)
    put("ipa_out", tm(mix_ref[...], dx2))

    gains = []
    for g in range(3):
        q = qkv_ref[:, g * 128 : (g + 1) * 128]
        k = qkv_ref[:, C + g * 128 : C + (g + 1) * 128]
        v = qkv_ref[:, 2 * C + g * 128 : 2 * C + (g + 1) * 128]
        dm = dmix[:, g * 128 : (g + 1) * 128]
        for m in range(4):
            h = 4 * g + m
            at = slice(h * 128, (h + 1) * 128)
            shares = shares_ref[:, at]
            dshares = mt(dm * masks[m], v)
            dlogit = shares * (dshares - jnp.sum(shares * dshares, axis=-1, keepdims=True))
            gains.append(jnp.sum(dlogit * point_ref[:, at], axis=0, keepdims=True))
            drow_ref[:, at] = dlogit.astype(BF16)
            dcol_ref[at, :] = dlogit.astype(BF16)
        group = slice(g * 512, (g + 1) * 512)
        dq = mm(drow_ref[:, group], masked_stack(k, masks)) * (SCALE * math.sqrt(0.5))
        dk = tm(dcol_ref[group, :], masked_stack(q, masks)) * (SCALE * math.sqrt(0.5))
        dv = tm(pcol_ref[group, :], masked_stack(dm, masks))
        dqkv_ref[:, g * 128 : (g + 1) * 128] = dq.astype(BF16)
        dqkv_ref[:, C + g * 128 : C + (g + 1) * 128] = dk.astype(BF16)
        dqkv_ref[:, 2 * C + g * 128 : 2 * C + (g + 1) * 128] = dv.astype(BF16)

    lane128 = lax.broadcasted_iota(jnp.int32, (1, 128), 1)
    gain = jnp.zeros((1, 128), F32)
    raw_row = jnp.zeros((1, 128), F32)
    for h in range(H):
        here = lane128 == h
        gain = jnp.where(here, jnp.sum(gains[h], axis=1, keepdims=True), gain)
        raw_row = jnp.where(here, weight_ref[h], raw_row)
    soft_row = jnp.maximum(raw_row, 0.0) + jnp.log(1.0 + jnp.exp(-jnp.abs(raw_row)))
    gain = gain / ((1.0 + jnp.exp(-raw_row)) * soft_row)

    for copy in fetched[7:10]:
        copy.wait()
    from_keys = mm(drow_ref[...], keys_ref[...])
    from_queries = tm(dcol_ref[...], queries_ref[...])
    spread = spread_ref[...]
    own_sum = sum(mm(part, spread) for part in split_two(from_keys[:, 128:256]))
    other_sum = sum(mm(part, spread) for part in split_two(from_queries[:, 128:256]))
    dgq = strength * (from_keys - gq * own_sum)
    dgk = (strength * (from_queries - gk * other_sum)).astype(BF16).astype(F32)
    for b in range(3):
        dlocal_ref[:, b * 256 : (b + 1) * 256] = (turns[b] * dgq).astype(BF16)
        dlocal_ref[:, (3 + b) * 256 : (4 + b) * 256] = (turns[b] * dgk).astype(BF16)
    dpoints = mm(dlocal_ref[...], gather_ref[...]).astype(BF16)
    dqkv = dqkv_ref[...]
    put("ipa_qkv", tm(n2, dqkv))
    gpts = tm(dpoints, n2)
    spare_row = lax.broadcasted_iota(jnp.int32, (C, 128), 0) == GAIN_ROW
    first = gpts[:, 0:128] + jnp.where(spare_row, gain, 0.0)
    put("ipa_points", jnp.concatenate([first, gpts[:, 128:]], axis=1))
    dn2 = (mt(dqkv, wqkv_ref[...]) + mm(dpoints[:, 0 : 6 * POINTS], wpts_ref[...])).astype(BF16).astype(F32)
    dx1 = (dx2.astype(F32) + norm_pull(dn2, normed, inverse).astype(BF16).astype(F32)).astype(BF16)
    back = jnp.concatenate([dx1, updated, jnp.zeros((N, 256), BF16)], axis=1)
    back_ref[...] = tm(order, back).astype(BF16).reshape(N, 8, 128)
    for copy in leaving + [spare_copy]:
        copy.wait()


def like(shape, dtype):
    return jax.ShapeDtypeStruct(shape, dtype)


def call_pack_rows(tokens, cotangent, rigid):
    frames, residues, _ = tokens.shape
    return pl.pallas_call(
        pack_rows,
        out_shape=like((residues, frames, 2 * C + 128), BF16),
        compiler_params=limit(8),
        name="pack_rows",
    )(*pinned(tokens, cotangent, rigid))


def call_time_forward(place, neighbors, rows, w_qkv, w_out):
    return pl.pallas_call(
        time_forward,
        in_specs=[SMEM, SMEM, VMEM, HBM, HBM],
        out_specs=(VMEM, HBM, HBM, HBM, HBM),
        scratch_shapes=[
            pltpu.VMEM((C, 3 * C), BF16), pltpu.VMEM((C, C), BF16), pltpu.SemaphoreType.DMA((2,)),
            pltpu.VMEM((N, 3 * C), BF16), pltpu.VMEM((N, H * N), BF16), pltpu.VMEM((N, C), BF16),
            pltpu.VMEM((N, C), BF16), pltpu.SemaphoreType.DMA((4,)),
        ],
        out_shape=(
            like((N, 8, 128), BF16), pltpu.HBM((N, 3 * C), BF16), pltpu.HBM((N, H * N), BF16),
            pltpu.HBM((N, C), BF16), pltpu.HBM((N, C), BF16),
        ),
        compiler_params=limit(12),
        name="time_forward",
    )(place, *pinned(neighbors), rows, *pinned(w_qkv, w_out))


def call_time_backward(core, back, rows, qkv, shares, mix, w_qkv, w_out):
    sources = [w_out, mix, rows, qkv, shares, w_qkv]
    return pl.pallas_call(
        time_backward,
        in_specs=[SMEM, VMEM] + [HBM] * 6,
        out_shape=(like((N, 2 * C), BF16), like((LATE, 128), BF16), like((LATE, 128), BF16)),
        scratch_shapes=[
            pltpu.VMEM((N, 3 * C), BF16), pltpu.VMEM((4 * N, N), BF16), pltpu.VMEM((4 * N, N), BF16),
            *[pltpu.VMEM(source.shape, BF16) for source in sources],
            pltpu.SemaphoreType.DMA((len(sources),)),
        ],
        compiler_params=limit(20),
        cost_estimate=pl.CostEstimate(flops=1000, bytes_accessed=1000, transcendentals=0),
        name="time_backward",
    )(core, back, *pinned(*sources))


def call_point_attention(core, weight, rows, w_qkv, w_pts, w_rep, w_out, w_up, w_down):
    heads, turn, spread, gather = selectors()
    sources = [w_qkv, turn, w_rep, heads, w_out, w_up, w_down, spread, gather, w_pts]
    return pl.pallas_call(
        point_attention,
        in_specs=[SMEM, SMEM, VMEM] + [HBM] * len(sources),
        out_specs=(VMEM, HBM, HBM),
        out_shape=(like((N, 8, 128), BF16), pltpu.HBM((EARLY, 128), BF16), pltpu.HBM((EARLY, 128), BF16)),
        scratch_shapes=[
            pltpu.VMEM((N, 3 * C), BF16), pltpu.VMEM((N, C), BF16),
            pltpu.VMEM((N, H * N), F32), pltpu.VMEM((N, H * N), F32),
            pltpu.VMEM((N, H * N), BF16), pltpu.VMEM((H * N, N), BF16),
            pltpu.VMEM((N, H * N), BF16), pltpu.VMEM((H * N, N), BF16),
            pltpu.VMEM((N, 3 * C), BF16), pltpu.VMEM((N, 6 * 256), BF16),
            pltpu.VMEM((H * N, 256), BF16), pltpu.VMEM((H * N, 256), BF16),
            pltpu.VMEM((N, 640), BF16), pltpu.VMEM((2, EARLY, 128), BF16),
            *[pltpu.VMEM(source.shape, BF16) for source in sources],
            pltpu.SemaphoreType.DMA((len(sources),)), pltpu.SemaphoreType.DMA((9,)),
        ],
        compiler_params=limit(40),
        name="point_attention",
    )(core, weight, rows, *pinned(*sources))


def add_early(side_ref, keep_ref, got_ref, give_ref, mine_ref, one_ref, two_ref, sems):
    part = EARLY // 4
    give, mine = 2 * (1 - side_ref[0]), 2 * side_ref[0]
    targets = (
        (give, give_ref.at[0:part]), (give + 1, give_ref.at[part : 2 * part]),
        (mine, mine_ref.at[0:part]), (mine + 1, mine_ref.at[part : 2 * part]),
    )
    steps = []
    for step, (index, target) in enumerate(targets):
        source = pl.ds(pl.multiple_of(index * part, part), part)
        span = slice(step * part, (step + 1) * part)
        steps.append(
            (
                pltpu.make_async_copy(keep_ref.at[source], one_ref.at[span], sems.at[3 * step]),
                pltpu.make_async_copy(got_ref.at[source], two_ref.at[span], sems.at[3 * step + 1]),
                pltpu.make_async_copy(one_ref.at[span], target, sems.at[3 * step + 2]),
            )
        )
    for first, second, _ in steps:
        first.start()
        second.start()
    for step, (first, second, out) in enumerate(steps):
        first.wait()
        second.wait()
        span = slice(step * part, (step + 1) * part)
        summed = one_ref[span, :].astype(F32) + two_ref[span, :].astype(F32)
        one_ref[span, :] = summed.astype(BF16)
        out.start()
    for _, _, out in steps:
        out.wait()


def call_add_early(side, keep, got):
    part = like((EARLY // 2, 128), BF16)
    return pl.pallas_call(
        add_early,
        in_specs=[SMEM, HBM, HBM],
        out_specs=(HBM, HBM),
        out_shape=(pltpu.HBM(part.shape, BF16),) * 2,
        scratch_shapes=[
            pltpu.VMEM((EARLY, 128), BF16), pltpu.VMEM((EARLY, 128), BF16),
            pltpu.SemaphoreType.DMA((12,)),
        ],
        compiler_params=limit(8),
        cost_estimate=pl.CostEstimate(flops=EARLY * 128, bytes_accessed=EARLY * 128 * 6, transcendentals=0),
        name="add_early",
    )(side, *pinned(keep), got)


def add_late(side_ref, keep_ref, got_ref, give_a_ref, give_b_ref, mine_ref):
    part = LATE // 4
    give, mine = 2 * (1 - side_ref[0]), 2 * side_ref[0]
    targets = (
        (give, give_a_ref, 0), (give + 1, give_b_ref, 0), (mine, mine_ref, 0), (mine + 1, mine_ref, part)
    )
    for index, ref, at in targets:
        span = pl.ds(pl.multiple_of(index * part, part), part)
        summed = keep_ref[span, :].astype(F32) + got_ref[span, :].astype(F32)
        ref[at : at + part, :] = summed.astype(BF16)


def call_add_late(side, keep, got):
    part = like((LATE // 4, 128), BF16)
    return pl.pallas_call(
        add_late,
        in_specs=[SMEM, VMEM, VMEM],
        out_shape=(part, part, like((LATE // 2, 128), BF16)),
        compiler_params=limit(8),
        name="add_late",
    )(side, keep, got)


def add_pairs(early_ref, got_early_ref, late_ref, late_a_ref, late_b_ref, total_ref):
    at = 0
    for mine, parts in ((early_ref, (got_early_ref,)), (late_ref, (late_a_ref, late_b_ref))):
        size = parts[0].shape[0]
        for k, part in enumerate(parts):
            summed = mine[k * size : (k + 1) * size, :].astype(F32) + part[...].astype(F32)
            total_ref[at : at + size, :] = summed.astype(BF16)
            at += size
    total_ref[at:, :] = jnp.zeros((QUARTER - at, 128), BF16)


def call_add_pairs(*parts):
    return pl.pallas_call(
        add_pairs, out_shape=like((QUARTER, 128), BF16), compiler_params=limit(12), name="add_pairs"
    )(*parts)


def add_parts(parts_ref, copies_ref):
    count = parts_ref.shape[0]
    total = parts_ref[0].astype(F32)
    for k in range(1, count):
        total = total + parts_ref[k].astype(F32)
    total = total.astype(BF16)
    for k in range(copies_ref.shape[0]):
        copies_ref[k] = total


def call_add_parts(parts):
    return pl.pallas_call(
        add_parts, out_shape=like(parts.shape, BF16), compiler_params=limit(12),
        name="add_parts",
    )(parts)


def final_spot(late, at):
    unit = (at - EARLY if late else at) // C
    room = (LATE if late else EARLY) // (2 * C)
    return unit // room, (EARLY // 2 if late else 0) + (unit % room) * C


def segments(row):
    begin = row
    while begin < row + C:
        chunk, low = divmod(begin, CHUNK)
        size = min(CHUNK - low, row + C - begin)
        yield chunk, low, size, begin - row
        begin += size


FETCHES = 4


class Quarter:
    def __init__(self, spot, parts, out_refs, gain_ref, held_ref, stage_ref, in_sems, out_sems):
        self.spot, self.out_refs, self.gain_ref = spot, out_refs, gain_ref
        self.held_ref, self.stage_ref, self.out_sems = held_ref, stage_ref, out_sems
        size = SHARERS // FETCHES
        each = FETCHES // len(parts)
        self.fetches = [
            pltpu.make_async_copy(
                parts[k // each].at[k % each * size : (k % each + 1) * size],
                held_ref.at[k * size : (k + 1) * size],
                in_sems.at[k],
            )
            for k in range(FETCHES)
        ]
        for copy in self.fetches:
            copy.start()

    def leaving(self, half, quarter):
        found = []
        for k, name in enumerate(PIECES):
            tiles = PIECES[name][1] // 128
            for unit, (owner, at) in enumerate(UNITS[name]):
                where, row = final_spot(name.startswith("time"), at)
                if (owner, where) != (half, quarter):
                    continue
                down, across = (unit // tiles) * C, (unit % tiles) * 128
                rows = GAIN_ROW if name == "ipa_points" else C
                slot = len(found)
                copy = pltpu.make_async_copy(
                    self.stage_ref.at[slot, 0:rows],
                    self.out_refs[k].at[down : down + rows, across : across + 128],
                    self.out_sems.at[slot],
                )
                found.append((row, copy, name == "ipa_points" and across == 0))
        return found

    def each(self, act):
        for half in range(2):
            for quarter in range(2):
                pl.when(self.spot == 2 * half + quarter)(lambda h=half, q=quarter: act(h, q))

    def send(self):
        def act(half, quarter):
            waited = 0
            for slot, (row, copy, gains) in enumerate(self.leaving(half, quarter)):
                for chunk, low, size, to in segments(row):
                    while waited * (SHARERS // FETCHES) <= chunk:
                        self.fetches[waited].wait()
                        waited += 1
                    self.stage_ref[slot, to : to + size, :] = self.held_ref[
                        chunk, low : low + size, :
                    ].astype(F32)
                copy.start()
                if gains:
                    self.gain_ref[...] += self.stage_ref[slot, GAIN_ROW : GAIN_ROW + 1, :]
            for copy in self.fetches[waited:]:
                copy.wait()

        self.each(act)

    def finish(self):
        def act(half, quarter):
            for _, copy, _ in self.leaving(half, quarter):
                copy.wait()

        self.each(act)


def unpack_first(spots_ref, own_ref, swapped_ref, *refs):
    out_refs, gain_ref = refs[:7], refs[7]
    gain_ref[...] = jnp.zeros((1, 128), F32)
    quarters = [
        Quarter(spots_ref[0], (own_ref,), out_refs, gain_ref, *refs[8:12]),
        Quarter(spots_ref[1], (swapped_ref,), out_refs, gain_ref, *refs[12:16]),
    ]
    for quarter in quarters:
        quarter.send()
    for quarter in quarters:
        quarter.finish()


def unpack_second(spots_ref, part_a_ref, part_b_ref, gain_in_ref, *refs):
    out_refs, gain_ref = refs[7:14], refs[14]
    gain_ref[...] = gain_in_ref[...]
    quarter = Quarter(spots_ref[2], (part_a_ref, part_b_ref), out_refs, gain_ref, *refs[15:19])
    quarter.send()
    quarter.finish()


def unpack_last(spots_ref, part_a_ref, part_b_ref, gain_in_ref, ended_ref, *refs):
    out_refs, gain_ref, output_ref, token_ref = refs[7:14], refs[14], refs[15], refs[16]
    total_ref = refs[17]
    total_ref[...] = gain_in_ref[...]
    quarter = Quarter(spots_ref[3], (part_a_ref, part_b_ref), out_refs, total_ref, *refs[18:22])
    residues, frames, _ = ended_ref.shape
    ended = mm(order_matrix(), ended_ref[...].reshape(N, 2 * C)).astype(BF16)
    token_ref[...] = ended[:, 0:C].reshape(frames, residues, C)
    output_ref[...] = ended[:, C:].reshape(frames, residues, C)
    quarter.send()
    lane = lax.broadcasted_iota(jnp.int32, (1, 128), 1)
    for h in range(H):
        gain_ref[h] = jnp.sum(jnp.where(lane == h, total_ref[...], 0.0))
    quarter.finish()


OUTS = [
    like((GAIN_ROW if name == "ipa_points" else rows, columns), F32)
    for name, (rows, columns) in PIECES.items()
]
MOST = (EARLY_UNITS[0] + LATE_UNITS[0]) // 2
QUARTER_SCRATCH = [
    pltpu.VMEM((SHARERS, CHUNK, 128), BF16),
    pltpu.VMEM((MOST, C, 128), F32),
    pltpu.SemaphoreType.DMA((FETCHES,)),
    pltpu.SemaphoreType.DMA((MOST,)),
]
COST = pl.CostEstimate(flops=0, bytes_accessed=8 * MEGA, transcendentals=0)


def call_unpack_first(spots, own, swapped):
    return pl.pallas_call(
        unpack_first,
        in_specs=[SMEM, HBM, HBM],
        out_specs=(*[HBM] * 7, VMEM),
        out_shape=(*OUTS, like((1, 128), F32)),
        scratch_shapes=QUARTER_SCRATCH * 2,
        compiler_params=limit(20),
        cost_estimate=COST,
        name="unpack_first",
    )(spots, own, swapped)


def call_unpack_second(spots, parts, gain, grads):
    return pl.pallas_call(
        unpack_second,
        in_specs=[SMEM, HBM, HBM, VMEM] + [HBM] * 7,
        out_specs=(*[HBM] * 7, VMEM),
        out_shape=(*OUTS, like((1, 128), F32)),
        scratch_shapes=QUARTER_SCRATCH,
        input_output_aliases={4 + k: k for k in range(7)},
        compiler_params=limit(20),
        cost_estimate=COST,
        name="unpack_second",
    )(spots, *parts, gain, *grads)


def call_unpack_last(spots, parts, gain, ended, grads):
    residues, frames, _ = ended.shape
    rows = like((frames, residues, C), BF16)
    return pl.pallas_call(
        unpack_last,
        in_specs=[SMEM, HBM, HBM, VMEM, VMEM] + [HBM] * 7,
        out_specs=(*[HBM] * 7, SMEM, VMEM, VMEM),
        out_shape=(*OUTS, like((H,), F32), rows, rows),
        scratch_shapes=[pltpu.VMEM((1, 128), F32)] + QUARTER_SCRATCH,
        input_output_aliases={5 + k: k for k in range(7)},
        compiler_params=limit(20),
        name="unpack_last",
    )(spots, *parts, gain, ended, *grads)


def repeat_points(weight):
    parts = weight.reshape(6, POINTS, C)
    tripled = jnp.concatenate([parts, parts, parts], axis=1)
    return jnp.pad(tripled, ((0, 0), (0, 256 - 3 * POINTS), (0, 0))).reshape(6 * 256, C)


def swap_rows(rows, axes):
    return lax.all_to_all(rows, axes, split_axis=0, concat_axis=0, tiled=True)


def both_ways(parts):
    return [lax.ppermute(part, EVERYONE, ring) for part, ring in zip(parts, RINGS)]


def share(parts):
    return lax.all_to_all(
        parts, EVERYONE, split_axis=0, concat_axis=0, tiled=True, axis_index_groups=GROUPS
    )


def body(
    tokens, rigid_frames, neighbors, w_time_qkv, w_time_out, w_ipa_qkv, w_ipa_points,
    point_weight, w_ipa_out, w_up, w_down, cotangent,
):
    frames, residues = tokens.shape[:2]
    place = lax.axis_index(("line", "core")).astype(jnp.int32).reshape(1)
    core = lax.axis_index("core").astype(jnp.int32).reshape(1)
    place_res = lax.axis_index("res").astype(jnp.int32)
    sides = jnp.stack([(place_res >> 1) & 1, place_res & 1])
    side = jnp.where(core == 0, sides[0], sides[1])
    far = jnp.where(core == 0, sides[1], sides[0])
    spots = jnp.concatenate(
        [2 * core + side, 2 - 2 * core + far, 2 * core + 1 - side, 2 - 2 * core + 1 - far]
    )
    swap = [(0, 1), (1, 0)]
    points = w_ipa_points.T
    rows = swap_rows(call_pack_rows(tokens, cotangent, rigid_frames), ("line", "core"))
    rows = rows.reshape(N, 2 * C + 128)
    sent, qkv, shares, mix, rows = call_time_forward(place, neighbors, rows, w_time_qkv, w_time_out)
    back, keep_early, give_early = call_point_attention(
        core, point_weight, swap_rows(sent, EVERYONE), w_ipa_qkv, points, repeat_points(points),
        w_ipa_out, w_up, w_down,
    )
    got_early = lax.ppermute(give_early, "core", swap)
    give_early, mine_early = call_add_early(side, keep_early, got_early)
    got_early = lax.ppermute(give_early, EVERYONE, RINGS[0])
    back = swap_rows(back, EVERYONE)
    ended, keep_late, give_late = call_time_backward(
        core, back, rows, qkv, shares, mix, w_time_qkv, w_time_out
    )
    got_late = lax.ppermute(give_late, "core", swap)
    *give_late, mine_late = call_add_late(side, keep_late, got_late)
    got_late = both_ways(give_late)
    total = call_add_pairs(mine_early, got_early, mine_late, *got_late)
    parts = share(total.reshape(SHARERS, CHUNK, 128))
    own = share(call_add_parts(parts))
    paired = both_ways((own[: SHARERS // 2], own[SHARERS // 2 :]))
    swapped = lax.ppermute(own, "core", swap)
    ended = swap_rows(ended.reshape(residues, frames, 2 * C), ("line", "core"))
    *grads, gain = call_unpack_first(spots, own, swapped)
    paired, ended, gain = lax.optimization_barrier((paired, ended, gain))
    last = [lax.ppermute(part, "core", swap) for part in paired]
    *grads, gain = call_unpack_second(spots, paired, gain, grads)
    *grads, gain, output, token_grad = call_unpack_last(spots, last, gain, ended, grads)
    grads = dict(zip(PIECES, grads))
    return (
        output, token_grad, grads["time_qkv"], grads["time_out"], grads["ipa_qkv"],
        grads["ipa_points"].T, gain, grads["ipa_out"], grads["up"], grads["down"],
    )


def solution(mesh):
    devices = mesh.devices
    split = Mesh(
        devices.reshape(devices.shape[0] // 2, 2, devices.shape[1]), ("line", "core", "res")
    )
    frame = ("line", "core")
    rows = P(frame, "res", None)
    placed = (rows, P(None, frame, "res"), P("res", None)) + (P(),) * 8 + (rows,)
    return jax.shard_map(
        body,
        mesh=split,
        in_specs=placed,
        out_specs=(rows, rows) + (P(),) * 8,
        check_vma=False,
    )
```
